256 devices in a mesh: slab: 32 (over y_hi, z, core), pencil: 8 (over y_lo, x).
Axes of the slice: x: 4, y: 4 (y_hi: 2, y_lo: 2; y = y_hi * 2 + y_lo), z: 8, core: 2. Of those that a mesh axis runs over, the one named last changes fastest.
Arguments:
- sources: float32 [4, 262144], P(None, ('slab', 'pencil')), may hold values from -6 to 6
- proj_weight: float32 [262144, 128], P(('slab', 'pencil')), may hold values from -1.5 to 1.5
- tri_slot: int32 [262144], P(('slab', 'pencil')), may hold values from 0 to 127, as said below
- cell_block: int32 [32768], P(('slab', 'pencil')), may hold values from 0 to 131071, as said below
- green: float32 [256, 256, 256], P('slab', 'pencil'), may hold values from -6 to 6
- near_index: int32 [16, 262144], P(None, ('slab', 'pencil')), may hold values from 0 to 1023
- near_coef: float32 [2, 16, 262144], P(None, None, ('slab', 'pencil')), may hold values from -2 to 2
Outputs:
- adjoint_potential: float32 [4, 262144], P(None, ('slab', 'pencil'))
The draws below stay inside these ranges and needn't reach their ends.
Inputs may be any that keep to these rules, and one draw needn't show every extreme that they name: `tri_slot`: in each group of 1024 consecutive triangles, the slots named for pencil column q are exactly q * 16 to q * 16 + n - 1 for some n of 1 to 16; in every group the last column has n = 16. `cell_block`: cell slot c of group g = c // 128 names a block inside slab g // P and pencil column (c // 16) % P of the grid, where P is the size of the pencil axis and slab i holds grid rows i * 256 // Q onward (Q the size of the slab axis), column j grid columns j * 256 // P onward; in each column, slot 0 names the lowest block of that region and slot 1 the highest.
All inputs are finite; a program needn't handle non-finite values.
Results may differ from the reference program's by a relative error of at most 0.000054.
Values sent between devices are 32-bit elements; how exact they have to be, the bound alone decides.
No kernel may reach another device: no remote copies, remote signals or barrier semaphores. Data moves between devices by JAX's collectives and lax.ppermute only.
A program may use at most 128 MiB of HBM per device.

```python
import jax
import jax.numpy as jnp
from jax import lax

G = 256
WAVES = 2
S = 128
CAP = 16
NEAR = 16
TRI_DEV = 1024
CELL_SLOTS = 128
CELLS = 32768
TRIS = 262144
N_SLAB = 32
N_PENCIL = 8


def column_counts(key):
    groups = N_SLAB * N_PENCIL
    counts = jax.random.randint(key, (groups, N_PENCIL), 1, CAP + 1)
    fullest = jax.random.randint(jax.random.fold_in(key, 1), (groups, 1), 0, N_PENCIL)
    column = jnp.arange(N_PENCIL, dtype=jnp.int32)[None, :]
    full = (column == fullest) | (column == N_PENCIL - 1)
    return jnp.where(full, CAP, counts).astype(jnp.int32)


def draw_tri_slot(key, part):
    counts = column_counts(jax.random.fold_in(key, 5))
    key = jax.random.fold_in(key, 7)
    live_count = jnp.sum(counts, axis=1)
    random_pick = jax.random.randint(key, (counts.shape[0], TRI_DEV), 0, live_count[:, None])
    position = jnp.arange(TRI_DEV, dtype=jnp.int32)[None, :]
    picked = jnp.where(position < live_count[:, None], position, random_pick)
    column_end = jnp.cumsum(counts, axis=1)
    column = jnp.sum((picked[:, :, None] >= column_end[:, None, :]).astype(jnp.int32), axis=2)
    column_start = column_end - counts
    offset = picked - jnp.take_along_axis(column_start, column, axis=1)
    return (column * CAP + offset).reshape(-1).astype(jnp.int32)


def draw_cell_block(key, part):
    key = jax.random.fold_in(key, 3)
    groups = N_SLAB * N_PENCIL
    x_blocks = G // N_SLAB // 4
    y_blocks = G // N_PENCIL // 4
    z_blocks = G // 8
    draw_shape = (groups, N_PENCIL, CAP)
    subkeys = jax.random.split(key, 3)
    slot_index = jnp.arange(CAP, dtype=jnp.int32)[None, None, :]

    def corner(values, top):
        return jnp.where(slot_index == 0, 0, jnp.where(slot_index == 1, top - 1, values))
    x_part = corner(jax.random.randint(subkeys[0], draw_shape, 0, x_blocks), x_blocks)
    y_part = corner(jax.random.randint(subkeys[1], draw_shape, 0, y_blocks), y_blocks)
    z_part = corner(jax.random.randint(subkeys[2], draw_shape, 0, z_blocks), z_blocks)
    group_index = jnp.arange(groups, dtype=jnp.int32)[:, None, None]
    column = jnp.arange(N_PENCIL, dtype=jnp.int32)[None, :, None]
    grid_x = group_index // N_PENCIL * x_blocks + x_part
    grid_y = column * y_blocks + y_part
    return ((grid_x * (G // 4) + grid_y) * z_blocks + z_part).reshape(-1).astype(jnp.int32)


def place_ends(drawn, own_key, low, largest):
    dims = drawn.shape
    place = [jax.random.randint(jax.random.fold_in(own_key, axis), (), 0, dims[axis]) for axis in range(len(dims))]
    drawn = drawn.at[tuple(place)].set(low)
    longest = dims.index(max(dims))
    place[longest] = (place[longest] + 1) % dims[longest]
    return drawn.at[tuple(place)].set(largest)


def steps_of(key, shape, cuts, smallest, top_value):
    def one(dim, shards_of):
        heights = jax.random.uniform(jax.random.fold_in(jax.random.fold_in(key, 6), dim), (shards_of,), jnp.float32, smallest / len(cuts), top_value / len(cuts))
        return jnp.repeat(jnp.exp(heights), shape[dim] // shards_of).reshape((-1,) + (1,) * (len(shape) - dim - 1))

    level = one(*cuts[0])
    for cut in cuts[1:]:
        level = level * one(*cut)
    return level


def scatter_about(rng, extent, scale, reach, pieces=(), kind=jnp.bfloat16):
    drawn = jax.random.normal(rng, extent, jnp.float32) * scale
    if len(pieces) > 0:
        drawn = steps_of(rng, extent, pieces, -0.22, 0.18) * drawn
    return jnp.clip(drawn, min=-reach, max=reach).astype(kind)


def setup_inputs(seed: int = 0) -> dict:
    streams_of = jax.random.split(jax.random.key(seed), 8)
    return {
        "sources": scatter_about(streams_of[0], (2 * WAVES, TRIS), 1.0, 6.0, ((1, 256),), jnp.float32),
        "proj_weight": scatter_about(streams_of[1], (TRIS, S), 16 ** -0.5, 1.5, ((0, 256),), jnp.float32),
        "tri_slot": draw_tri_slot(jax.random.fold_in(streams_of[7], 71), 0),
        "cell_block": draw_cell_block(jax.random.fold_in(streams_of[7], 71), 0),
        "green": scatter_about(streams_of[4], (G, G, G), 1.0, 6.0, ((0, 32), (1, 8)), jnp.float32),
        "near_index": place_ends(jax.random.randint(streams_of[5], (NEAR, TRIS), 0, TRI_DEV), jax.random.fold_in(streams_of[5], 1), 0, TRI_DEV - 1).astype(jnp.int32),
        "near_coef": scatter_about(streams_of[6], (2, NEAR, TRIS), 0.15, 2.0, ((2, 256),), jnp.float32),
    }


def reference(sources, proj_weight, tri_slot, cell_block, green, near_index, near_coef):
    groups = N_SLAB * N_PENCIL
    channels = 2 * WAVES
    source_groups = sources.reshape(channels, groups, TRI_DEV).transpose(1, 0, 2)
    weight_groups = proj_weight.reshape(groups, TRI_DEV, S)
    slot_groups = tri_slot.reshape(groups, TRI_DEV)

    def anterpolate(operands):
        source_group, weight, slot_group = operands
        values = (source_group.T[:, :, None] * weight[:, None, :]).reshape(TRI_DEV, channels * S)
        return jax.ops.segment_sum(values, slot_group, num_segments=CELL_SLOTS)

    charges = lax.map(anterpolate, (source_groups, weight_groups, slot_groups)).reshape(CELLS, channels * S)
    blocks = jnp.zeros((G * G * G // 128, channels * S), charges.dtype).at[cell_block].add(charges)
    grid_field = blocks.reshape(G // 4, G // 4, G // 8, channels, 4, 4, 8).transpose(3, 0, 4, 1, 5, 2, 6).reshape(channels, G, G, G)
    spectrum = jnp.fft.fftn(grid_field[:WAVES] + 1j * grid_field[WAVES:], axes=(1, 2, 3)) * green
    potential = jnp.fft.ifftn(spectrum, axes=(1, 2, 3))
    potential_grid = jnp.concatenate([potential.real, potential.imag]).astype(grid_field.dtype)
    potential_blocks = potential_grid.reshape(channels, G // 4, 4, G // 4, 4, G // 8, 8).transpose(1, 3, 5, 0, 2, 4, 6).reshape(-1, channels * S)
    cell_potential = potential_blocks[cell_block].reshape(groups, CELL_SLOTS, channels * S)

    def interpolate(operands):
        potential_rows, weight, slot_group = operands
        picked_rows = potential_rows[slot_group].reshape(TRI_DEV, channels, S)
        return jnp.sum(picked_rows * weight[:, None, :], axis=2).T

    far_field = lax.map(interpolate, (cell_potential, weight_groups, slot_groups))
    far_field = far_field.transpose(1, 0, 2).reshape(channels, TRIS)
    offset = (jnp.arange(TRIS, dtype=jnp.int32) // TRI_DEV) * TRI_DEV
    neighbour = sources[:, near_index + offset[None, :]]
    source_real = neighbour[:WAVES]
    source_imag = neighbour[WAVES:]
    coef_real = near_coef[0][None]
    coef_imag = near_coef[1][None]
    near_real = jnp.sum(coef_real * source_real - coef_imag * source_imag, axis=1)
    near_imag = jnp.sum(coef_real * source_imag + coef_imag * source_real, axis=1)
    return far_field + jnp.concatenate([near_real, near_imag])
```

```python
import functools
import math

import jax
import jax.numpy as jnp
import numpy as np
from jax import lax
from jax.experimental import pallas as pl
from jax.experimental.pallas import tpu as pltpu
from jax.sharding import PartitionSpec as P

f32 = jnp.float32
bf16 = jnp.bfloat16
BOTH = ("slab", "pencil")
LANES = 128


def params(mib):
    return pltpu.CompilerParams(vmem_limit_bytes=mib << 20)


def call(body, out_shape, scratch=(), mib=48, cost=(0, 0)):
    return pl.pallas_call(
        body,
        out_shape=out_shape,
        scratch_shapes=list(scratch),
        compiler_params=params(mib),
        cost_estimate=pl.CostEstimate(flops=cost[0], bytes_accessed=cost[1], transcendentals=0),
    )


def halves(x):
    high = x.astype(bf16)
    return high, (x - high.astype(f32)).astype(bf16)


def dot(a, b, dims=((1,), (0,))):
    return lax.dot_general(a, b, (dims, ((), ())), preferred_element_type=f32)


def dot3(a, b):
    return dot(a[0], b[0]) + (dot(a[0], b[1]) + dot(a[1], b[0]))


def tables(n, y_order, kx_order):
    def angle(rows, columns):
        return (np.outer(rows, columns) % n) * (2.0 * math.pi / n)

    k = np.arange(n)
    z = angle(k, k)
    z_forward = np.concatenate([np.cos(z), np.sin(z)], axis=1)
    z_inverse = np.concatenate([np.cos(z), -np.sin(z)], axis=1) / n
    x = angle(kx_order, k)
    x_forward = np.concatenate([np.cos(x), np.sin(x)], axis=1)
    x_inverse = np.concatenate([np.cos(x).T, -np.sin(x).T], axis=1) / n
    a = angle(y_order.reshape(-1), k)
    cosine, sine = np.cos(a).reshape(4, 64, n), np.sin(a).reshape(4, 64, n)
    y_forward = np.stack(
        [
            np.concatenate([cosine, -sine], axis=2),
            np.concatenate([sine, cosine], axis=2),
        ],
        axis=1,
    ).reshape(2 * n, 2 * n)
    y_inverse = y_forward.T / n
    return [
        jnp.asarray(t.astype(np.float32))
        for t in (z_forward, x_forward, y_forward, y_inverse, x_inverse, z_inverse)
    ]


def lane_iota(rows):
    return lax.broadcasted_iota(jnp.int32, (rows, LANES), 1)


def swap_bit(a, b, distance, bit):
    return (
        jnp.where(bit, pltpu.roll(b, distance, 1), a),
        jnp.where(bit, b, pltpu.roll(a, LANES - distance, 1)),
    )


def swap_bits(parts, distances):
    parts = list(parts)
    lane = lane_iota(parts[0].shape[0])
    for level, distance in enumerate(distances):
        stride = len(parts) >> (level + 1)
        bit = (lane & distance) != 0
        for low in range(len(parts)):
            if low & stride == 0:
                parts[low], parts[low | stride] = swap_bit(
                    parts[low], parts[low | stride], distance, bit
                )
    return parts


def partner(x, sign):
    lanes = lax.broadcasted_iota(jnp.int32, x.shape, 1)
    columns = x.shape[1] // LANES
    swapped = jnp.concatenate(
        [pltpu.roll(x[:, i * LANES : (i + 1) * LANES], 64, 1) for i in range(columns)], axis=1
    )
    return jnp.where((lanes & 64) == 0, swapped, -swapped)


def charges_kernel(src_ref, w_ref, slot_ref, block_ref, msg_ref):
    channels, tris = src_ref.shape
    slots = block_ref.shape[1]
    pencils = msg_ref.shape[0]
    cap = slots // pencils
    hit = lax.broadcasted_iota(jnp.int32, (slots, tris), 0) == slot_ref[...]
    w_high, w_low = halves(w_ref[...])
    w_both = jnp.concatenate([w_high, w_low], axis=1)
    for c in range(channels):
        left = jnp.where(hit, src_ref[c : c + 1, :], 0.0)
        high, low = halves(left)
        both = dot(high, w_both)
        total = both[:, :LANES] + (both[:, LANES:] + dot(low, w_high))
        msg_ref[:, c * cap : (c + 1) * cap, :] = total.reshape(pencils, cap, LANES)
    place = jnp.broadcast_to(block_ref[...].astype(f32), (LANES, slots)).T
    msg_ref[:, channels * cap :, :] = place.reshape(pencils, cap, LANES)


def hits(place, x_blocks, y_blocks, z_blocks):
    place = place.astype(jnp.int32)
    z = place % z_blocks
    y = place // z_blocks % 64 % y_blocks
    x = place // (z_blocks * 64) % x_blocks
    group = z // 8
    lane = x * 64 + z % 8 * 8 + y
    lanes = lane_iota(place.shape[0])
    return [
        jnp.where((lanes == lane) & (group == g), 1.0, 0.0).astype(bf16)
        for g in range(z_blocks // 8)
    ]


def forward_kernel(got_ref, green_ref, table_ref, msg_ref, hit_ref, placed_ref, z_ref):
    pencils, rows, _ = got_ref.shape
    cells = hit_ref.shape[0]
    cap = cells // pencils
    channels = rows // cap - 1
    place = got_ref[:, channels * cap :, :].reshape(cells, LANES)
    hit = jnp.concatenate(hits(place, 2, 8, 32), axis=1)
    hit_ref[...] = hit
    hit2 = jnp.concatenate([hit, hit], axis=0)
    for c in range(channels):
        charge = got_ref[:, c * cap : (c + 1) * cap, :].reshape(cells, LANES).T
        high, low = halves(charge)
        placed_ref[c] = dot(jnp.concatenate([high, low], axis=1), hit2)
    for g in range(4):
        for sx in range(4):
            tiles = [
                placed_ref[c, (sx * 4 + sy) * 8 : (sx * 4 + sy + 1) * 8, g * LANES : (g + 1) * LANES]
                for c in range(4)
                for sy in range(4)
            ]
            tiles = swap_bits(tiles, (64, 32, 16, 8))
            for e in range(16):
                x, z_lo = e // 8, e % 8
                row, column = (g * 8 + z_lo) * 8, (x * 4 + sx) * LANES
                z_ref[row : row + 8, column : column + LANES] = tiles[e]
    field = z_ref[...]
    field = jnp.concatenate([field, partner(field, 1)], axis=0)
    high, low = halves(field)
    spec = dot3(halves(table_ref[...]), (high, low))
    n = msg_ref.shape[0] // 10
    for x in range(8):
        msg_ref[pl.ds(x, n, 10), :] = spec[:, x * LANES : (x + 1) * LANES]
    green = green_ref[...].T
    msg_ref[pl.ds(8, n, 10), :] = green[:, :LANES]
    msg_ref[pl.ds(9, n, 10), :] = green[:, LANES:]


def plane_kernel(got_ref, xf_ref, yf_ref, yi_ref, xi_ref, msg_ref):
    n = xf_ref.shape[0]
    xf, xi = halves(xf_ref[...]), halves(xi_ref[...])
    got = got_ref.reshape(32, 8, 10, LANES)
    green = []
    for r in range(2):
        columns = []
        for j_hi in range(2):
            parts = [got[:, j_hi * 4 + j_lo, 8 + r, :] for j_lo in range(4)]
            columns.append(jnp.concatenate(swap_bits(parts, (64, 32)), axis=0))
        green.append(jnp.concatenate(columns, axis=1))
    green = jnp.concatenate(green, axis=0)
    green = jnp.concatenate([green, green], axis=1)
    waves = ([], [])
    for j in range(0, 8, 2):
        pair = [got[:, j + o, :8, :].reshape(n, LANES) for o in range(2)]
        for w, part in enumerate(swap_bits(pair, (32,))):
            waves[w].append(part)
    spec = []
    for w in range(2):
        plane = jnp.concatenate(waves[w], axis=1)
        plane = jnp.concatenate([plane, partner(plane, 1)], axis=0)
        spec.append(dot3(xf, halves(plane)))
    spec = jnp.concatenate(spec, axis=0)
    spec = dot3(halves(spec), halves(yf_ref[...]))
    spec = spec * jnp.concatenate([green, green], axis=0)
    spec = dot3(halves(spec), halves(yi_ref[...]))
    out = []
    for w in range(2):
        plane = spec[w * n : (w + 1) * n]
        plane = jnp.concatenate([plane, partner(plane, 1)], axis=0)
        out.append(dot3(xi, halves(plane)))
    msg = msg_ref.reshape(32, 8, 8, LANES)
    for j in range(0, 8, 2):
        pair = [out[w][:, j // 2 * LANES : (j // 2 + 1) * LANES] for w in range(2)]
        for o, part in enumerate(swap_bits(pair, (32,))):
            msg[:, j + o, :, :] = part.reshape(32, 8, LANES)


def inverse_kernel(got_ref, hit_ref, table_ref, msg_ref, z_ref, a_ref):
    n = table_ref.shape[0]
    pencils = msg_ref.shape[0]
    cells = hit_ref.shape[0]
    cap = cells // pencils
    spec = jnp.concatenate([got_ref[pl.ds(x, n, 8), :] for x in range(8)], axis=1)
    spec = jnp.concatenate([spec, partner(spec, 1)], axis=0)
    z_ref[...] = dot3(halves(table_ref[...]), halves(spec))
    for g in range(4):
        for sx in range(4):
            tiles = []
            for e in range(16):
                x, z_lo = e // 8, e % 8
                row, column = (g * 8 + z_lo) * 8, (x * 4 + sx) * LANES
                tiles.append(z_ref[row : row + 8, column : column + LANES])
            tiles = swap_bits(tiles, (64, 32, 16, 8))
            for m in range(16):
                c, sy = m // 4, m % 4
                row = c * LANES + (sx * 4 + sy) * 8
                a_ref[row : row + 8, g * LANES : (g + 1) * LANES] = tiles[m]
    high, low = halves(a_ref[...])
    hit = hit_ref[...]
    picked = dot(hit, high, ((1,), (1,))) + dot(hit, low, ((1,), (1,)))
    for c in range(4):
        msg_ref[:, c * cap : (c + 1) * cap, :] = picked[:, c * LANES : (c + 1) * LANES].reshape(
            pencils, cap, LANES
        )


def near_kernel(src_ref, table_ref, index_ref, coef_ref, w_ref, near_ref, wt_ref):
    channels = src_ref.shape[0]
    near, tris = index_ref.shape
    for start in range(0, tris, LANES):
        cols = slice(start, start + LANES)
        total = [jnp.zeros((8, LANES), f32) for _ in range(channels)]
        for top in range(0, near, 8):
            index = index_ref[top : top + 8, cols]
            lane, row = index & (LANES - 1), index >> 7
            got = [jnp.zeros((8, LANES), f32) for _ in range(channels)]
            for r in range(8):
                hit = row == r
                for c in range(channels):
                    line = jnp.broadcast_to(table_ref[c, r : r + 1, :], (8, LANES))
                    got[c] = jnp.where(hit, jnp.take_along_axis(line, lane, axis=1), got[c])
            a = coef_ref[0, top : top + 8, cols]
            b = coef_ref[1, top : top + 8, cols]
            for w in range(channels // 2):
                re, im = got[w], got[w + channels // 2]
                total[w] += a * re - b * im
                total[w + channels // 2] += a * im + b * re
        for c in range(channels):
            near_ref[c : c + 1, cols] = jnp.sum(total[c], axis=0, keepdims=True)
    wt_ref[...] = w_ref[...].T


def far_kernel(got_ref, slot_ref, wt_ref, near_ref, out_ref):
    pencils, rows, _ = got_ref.shape
    channels, tris = near_ref.shape
    cap = rows // channels
    slots = pencils * cap
    hit = lax.broadcasted_iota(jnp.int32, (slots, tris), 0) == slot_ref[...]
    hit = jnp.where(hit, 1.0, 0.0).astype(bf16)
    hit = jnp.concatenate([hit, hit], axis=0)
    wt = wt_ref[...]
    for c in range(channels):
        values = got_ref[:, c * cap : (c + 1) * cap, :].reshape(slots, LANES).T
        high, low = halves(values)
        picked = dot(jnp.concatenate([high, low], axis=1), hit)
        far = jnp.sum(picked * wt, axis=0, keepdims=True)
        out_ref[c : c + 1, :] = far + near_ref[c : c + 1, :]


def exchange(x, axis):
    parts = lax.axis_size(axis)
    sent = x.reshape(parts, 1, x.size // parts)
    return lax.all_to_all(sent, axis, split_axis=0, concat_axis=0, tiled=True).reshape(x.shape)


def per_device(sources, proj_weight, tri_slot, cell_block, green, near_index, near_coef):
    slabs, pencils = lax.axis_size("slab"), lax.axis_size("pencil")
    channels, tris = sources.shape
    slots = cell_block.shape[0]
    cap = slots // pencils
    n = green.shape[2]
    devices = slabs * pencils
    struct = jax.ShapeDtypeStruct
    y_local = np.arange(32) % 8 * 4 + np.arange(32) // 8
    y_order = np.arange(8)[:, None] * 32 + y_local[None, :]
    r, lo, i = np.meshgrid(np.arange(2), np.arange(4), np.arange(32), indexing="ij")
    kx_order = (i * 8 + r * 4 + lo).reshape(-1)
    zf, xf, yf, yi, xi, zi = tables(n, y_order, kx_order)
    slot_row = tri_slot.reshape(1, tris)

    msg = call(charges_kernel, struct((pencils, (channels + 1) * cap, LANES), f32))(
        sources, proj_weight, slot_row, cell_block.reshape(1, slots)
    )
    got = exchange(msg, "pencil")
    near, wt = call(
        near_kernel,
        (struct((channels, tris), f32), struct((LANES, tris), f32)),
        cost=(1 << 30, 1 << 20),
    )(sources, sources.reshape(channels, 8, LANES), near_index, near_coef, proj_weight)
    msg, hit = call(
        forward_kernel,
        (struct((devices * 10, LANES), f32), struct((slots, 512), bf16)),
        scratch=[pltpu.VMEM((channels, LANES, 512), f32), pltpu.VMEM((n, 1024), f32)],
    )(got, green.reshape(n, n), zf)
    got = exchange(msg, BOTH)
    msg = call(plane_kernel, struct((devices * 8, LANES), f32), mib=56)(
        got, xf, yf, yi, xi
    )
    got = exchange(msg, BOTH)
    msg = call(
        inverse_kernel,
        struct((pencils, channels * cap, LANES), f32),
        scratch=[pltpu.VMEM((n, 1024), f32), pltpu.VMEM((channels * LANES, 512), f32)],
    )(got, hit, zi)
    got = exchange(msg, "pencil")
    return call(far_kernel, struct((channels, tris), f32))(got, slot_row, wt, near)


def solution(mesh):
    return jax.shard_map(
        per_device,
        mesh=mesh,
        in_specs=(
            P(None, BOTH),
            P(BOTH, None),
            P(BOTH),
            P(BOTH),
            P("slab", "pencil", None),
            P(None, BOTH),
            P(None, None, BOTH),
        ),
        out_specs=P(None, BOTH),
        check_vma=False,
    )
```

```python
import math

import jax
import jax.numpy as jnp
import numpy as np
from jax import lax
from jax.experimental import pallas as pl
from jax.experimental.pallas import tpu as pltpu
from jax.sharding import PartitionSpec as P

f32 = jnp.float32
bf16 = jnp.bfloat16
BOTH = ("slab", "pencil")
LANES = 128
struct = jax.ShapeDtypeStruct


def call(body, out_shape, scratch=(), mib=24, cost=(0, 0), in_specs=None):
    more = {} if in_specs is None else {"in_specs": in_specs}
    return pl.pallas_call(
        body,
        out_shape=out_shape,
        scratch_shapes=list(scratch),
        compiler_params=pltpu.CompilerParams(vmem_limit_bytes=mib << 20),
        cost_estimate=pl.CostEstimate(flops=cost[0], bytes_accessed=cost[1], transcendentals=0),
        **more,
    )


def halves(x):
    high = x.astype(bf16)
    return high, (x - high.astype(f32)).astype(bf16)


def dot(a, b, dims=((1,), (0,))):
    return lax.dot_general(a, b, (dims, ((), ())), preferred_element_type=f32)


def table_dot(table, x):
    t_high, t_low = table
    high, low = halves(x)
    m = t_high.shape[0]
    both = dot(jnp.concatenate([t_high, t_low], axis=0), high)
    return both[:m] + (both[m:] + dot(t_high, low))


def dot_table(x, table):
    m = x.shape[0]
    high, low = halves(x)
    both = dot(jnp.concatenate([high, low], axis=0), table[0])
    return both[:m] + (both[m:] + dot(high, table[1]))


def square(cosine, first, second):
    return jnp.concatenate(
        [jnp.concatenate([cosine, first], axis=1), jnp.concatenate([second, cosine], axis=1)], axis=0
    )


def complex_table(rows, row_part, columns, column_part, n, inverse):
    angle = (np.outer(rows, columns) % n) * (2.0 * math.pi / n)
    sine = np.sin(angle) * np.where(row_part == 0, 1.0, -1.0)[:, None]
    if inverse:
        sine = -sine
    same = row_part[:, None] == column_part[None, :]
    return np.where(same, np.cos(angle), sine) / (n if inverse else 1)


def tables(n):
    part, k = np.arange(2 * n) // n, np.arange(2 * n) % n
    b2, slab, x_part, b1, b0 = (a.reshape(-1) for a in np.indices((2, 32, 2, 2, 2)))
    x = slab * 8 + b2 * 4 + b1 * 2 + b0
    kx_part, kx_2, kx_01, kx_slab = (a.reshape(-1) for a in np.indices((2, 2, 4, 32)))
    kx = kx_slab * 8 + kx_2 * 4 + kx_01
    y = np.arange(n) // 32 * 32 + np.arange(n) % 8 * 4 + np.arange(n) // 8 % 4
    angle = (np.outer(y, np.arange(n)) % n) * (2.0 * math.pi / n)
    found = (
        complex_table(k, part, k, part, n, False),
        complex_table(kx, kx_part, x, x_part, n, False),
        np.stack([np.cos(angle), np.sin(angle)]),
        complex_table(x, x_part, kx, kx_part, n, True) / n,
        complex_table(k, part, k, part, n, True),
    )
    return [jnp.asarray(t.astype(np.float32)) for t in found]


def lane_iota(rows):
    return lax.broadcasted_iota(jnp.int32, (rows, LANES), 1)


def swap_bits(parts, distances):
    parts = list(parts)
    lane = lane_iota(parts[0].shape[0])
    for level, distance in enumerate(distances):
        stride = len(parts) >> (level + 1)
        bit = (lane & distance) != 0
        for low in range(len(parts)):
            if low & stride == 0:
                a, b = parts[low], parts[low | stride]
                parts[low] = jnp.where(bit, pltpu.roll(b, distance, 1), a)
                parts[low | stride] = jnp.where(bit, b, pltpu.roll(a, LANES - distance, 1))
    return parts


def charges_kernel(src_hbm, w_hbm, slot_hbm, block_hbm, msg_ref, src_ref, w_ref, slot_ref, block_ref, sems):
    pairs = ((src_hbm, src_ref), (slot_hbm, slot_ref), (block_hbm, block_ref), (w_hbm, w_ref))
    copies = [pltpu.make_async_copy(a, b, sems.at[i]) for i, (a, b) in enumerate(pairs)]
    for copy in copies:
        copy.start()
    for copy in copies:
        copy.wait()
    channels, tris = src_ref.shape
    slots = block_ref.shape[1]
    pencils = msg_ref.shape[0]
    cap = slots // pencils
    rows = channels * cap
    hit = lax.broadcasted_iota(jnp.int32, (slots, tris), 0) == slot_ref[...]
    w_high, w_low = halves(w_ref[...])
    w_both = jnp.concatenate([w_high, w_low], axis=1)
    for c in range(channels):
        high, low = halves(jnp.where(hit, src_ref[c : c + 1, :], 0.0))
        both = dot(high, w_both)
        total = both[:, :LANES] + (both[:, LANES:] + dot(low, w_high))
        msg_ref[:, c * cap : (c + 1) * cap, :] = total.reshape(pencils, cap, LANES)
    place = jnp.broadcast_to(block_ref[...].astype(f32), (LANES, slots)).T
    place = place.reshape(pencils, cap, LANES)
    lane = lax.broadcasted_iota(jnp.int32, (pencils, cap // 2, LANES), 2)
    msg_ref[:, rows:, :] = jnp.where(lane < 64, place[:, : cap // 2], place[:, cap // 2 :])


def hits(place, x_blocks, y_blocks, z_blocks):
    place = place.astype(jnp.int32)
    z = place % z_blocks
    y = place // z_blocks % 64 % y_blocks
    x = place // (z_blocks * 64) % x_blocks
    group = z // 8
    lane = x * 64 + z % 8 * 8 + y
    lanes = lane_iota(place.shape[0])
    return [
        jnp.where((lanes == lane) & (group == g), 1.0, 0.0).astype(bf16)
        for g in range(z_blocks // 8)
    ]


def tiles_of(part, g, x_1, x_0):
    blocks, grid = [], []
    for m in range(8):
        wave, y_low = m // 4, m % 4
        stencil = (x_1 * 2 + x_0) * 4 + y_low
        blocks.append(((part * 2 + wave) * LANES + stencil * 8, g * LANES))
        grid.append((part * 256 + (g * 8 + m) * 8, (x_1 * 2 + x_0) * LANES))
    return blocks, grid


GROUPS = [(part, g, x_1, x_0) for part in range(2) for g in range(4) for x_1 in range(2) for x_0 in range(2)]


def forward_kernel(got_ref, green_ref, table_ref, msg_ref, hit_ref, placed_ref, z_ref):
    pencils = got_ref.shape[0]
    cells = hit_ref.shape[1]
    cap = cells // pencils
    channels = 4
    place = got_ref[:, channels * cap :, :].reshape(cells // 2, LANES)
    lane = lane_iota(cells // 2)
    other = pltpu.roll(place, 64, 1)
    place = [jnp.where(lane < 64, a, b).reshape(pencils, cap // 2, LANES) for a, b in ((place, other), (other, place))]
    place = jnp.concatenate(place, axis=1).reshape(cells, LANES)
    hit = jnp.concatenate(hits(place, 2, 8, 32), axis=1)
    hit_ref[...] = hit.astype(f32).T.astype(bf16)
    charge = jnp.concatenate(
        [got_ref[:, c * cap : (c + 1) * cap, :].reshape(cells, LANES).T for c in range(channels)], axis=0
    )
    placed_ref[...] = dot(jnp.concatenate(halves(charge), axis=1), jnp.concatenate([hit, hit], axis=0))
    for group in GROUPS:
        blocks, grid = tiles_of(*group)
        found = swap_bits([placed_ref[r : r + 8, c : c + LANES] for r, c in blocks], (32, 16, 8))
        for (r, c), tile in zip(grid, found):
            z_ref[r : r + 8, c : c + LANES] = tile
    spec = table_dot(halves(table_ref[...]), z_ref[...])
    n = msg_ref.shape[0] // 10
    for row in range(8):
        part, x = row // 4, row % 4
        msg_ref[pl.ds(row, n, 10), :] = spec[part * n : (part + 1) * n, x * LANES : (x + 1) * LANES]
    green = green_ref[...].T
    msg_ref[pl.ds(8, n, 10), :] = green[:, :LANES]
    msg_ref[pl.ds(9, n, 10), :] = green[:, LANES:]


def plane_kernel(got_ref, xf_ref, y_ref, xi_ref, msg_ref):
    n = got_ref.shape[0] // 10
    got = got_ref.reshape(32, 8, 10, LANES)
    green = []
    for r in range(2):
        columns = []
        for j_2 in range(2):
            parts = [got[:, j_2 * 4 + j, 8 + r, :] for j in range(4)]
            columns.append(jnp.concatenate(swap_bits(parts, (64, 32)), axis=0))
        green.append(jnp.concatenate(columns, axis=1))
    green = jnp.concatenate(green, axis=0)
    green = jnp.concatenate([green, green], axis=1)
    found = []
    for j_2 in range(2):
        parts = [got[:, j_2 * 4 + j, :8, :].reshape(n, LANES) for j in range(4)]
        found.append(swap_bits(parts, (64, 32)))
    plane = jnp.concatenate(
        [
            jnp.concatenate([found[j_2][x_2 * 2 + w] for w in range(2) for j_2 in range(2)], axis=1)
            for x_2 in range(2)
        ],
        axis=0,
    )
    spec = table_dot(halves(xf_ref[...]), plane)
    spec = jnp.concatenate(
        [
            jnp.concatenate([spec[part * n : (part + 1) * n, w * n : (w + 1) * n] for part in range(2)], axis=1)
            for w in range(2)
        ],
        axis=0,
    )
    cosine, sine = halves(y_ref[0]), halves(y_ref[1])
    spec = dot_table(spec, [square(c, -s, s) for c, s in zip(cosine, sine)])
    spec = spec * jnp.concatenate([green, green], axis=0)
    cosine, sine = halves(y_ref[0].T), halves(y_ref[1].T)
    spec = dot_table(spec, [square(c, s, -s) for c, s in zip(cosine, sine)])
    spec = jnp.concatenate(
        [
            jnp.concatenate([spec[w * n : (w + 1) * n, part * n : (part + 1) * n] for w in range(2)], axis=1)
            for part in range(2)
        ],
        axis=0,
    )
    plane = table_dot(halves(xi_ref[...]), spec)
    msg = msg_ref.reshape(32, 8, 8, LANES)
    for j_2 in range(2):
        parts = [
            plane[x_2 * n : (x_2 + 1) * n, w * n + j_2 * LANES : w * n + (j_2 + 1) * LANES]
            for x_2 in range(2)
            for w in range(2)
        ]
        for j, part in enumerate(swap_bits(parts, (64, 32))):
            msg[:, j_2 * 4 + j, :, :] = part.reshape(32, 8, LANES)


def inverse_kernel(got_ref, hit_ref, table_ref, msg_ref, z_ref, a_ref):
    n = got_ref.shape[0] // 8
    pencils = msg_ref.shape[0]
    cells = hit_ref.shape[1]
    cap = cells // pencils
    spec = jnp.concatenate(
        [
            jnp.concatenate([got_ref[pl.ds(part * 4 + x, n, 8), :] for x in range(4)], axis=1)
            for part in range(2)
        ],
        axis=0,
    )
    z_ref[...] = table_dot(halves(table_ref[...]), spec)
    for group in GROUPS:
        blocks, grid = tiles_of(*group)
        found = swap_bits([z_ref[r : r + 8, c : c + LANES] for r, c in grid], (32, 16, 8))
        for (r, c), tile in zip(blocks, found):
            a_ref[r : r + 8, c : c + LANES] = tile
    picked = dot(jnp.concatenate(halves(a_ref[...]), axis=0), hit_ref[...])
    rows = 4 * LANES
    for c in range(4):
        cells_c = picked[c * LANES : (c + 1) * LANES] + picked[rows + c * LANES : rows + (c + 1) * LANES]
        msg_ref[:, c * cap : (c + 1) * cap, :] = cells_c.T.reshape(pencils, cap, LANES)


def near_kernel(src_ref, table_ref, index_ref, coef_ref, w_ref, near_ref, wt_ref):
    channels = src_ref.shape[0]
    near, tris = index_ref.shape
    for start in range(0, tris, LANES):
        cols = slice(start, start + LANES)
        total = [jnp.zeros((8, LANES), f32) for _ in range(channels)]
        for top in range(0, near, 8):
            index = index_ref[top : top + 8, cols]
            lane, row = index & (LANES - 1), index >> 7
            got = [jnp.zeros((8, LANES), f32) for _ in range(channels)]
            for r in range(8):
                hit = row == r
                for c in range(channels):
                    line = jnp.broadcast_to(table_ref[c, r : r + 1, :], (8, LANES))
                    got[c] = jnp.where(hit, jnp.take_along_axis(line, lane, axis=1), got[c])
            a = coef_ref[0, top : top + 8, cols]
            b = coef_ref[1, top : top + 8, cols]
            for w in range(channels // 2):
                re, im = got[w], got[w + channels // 2]
                total[w] += a * re - b * im
                total[w + channels // 2] += a * im + b * re
        for c in range(channels):
            near_ref[c : c + 1, cols] = jnp.sum(total[c], axis=0, keepdims=True)
    wt_ref[...] = w_ref[...].T


def far_kernel(got_ref, slot_ref, wt_ref, near_ref, out_ref):
    pencils, rows, _ = got_ref.shape
    channels, tris = near_ref.shape
    cap = rows // channels
    slots = pencils * cap
    hit = lax.broadcasted_iota(jnp.int32, (slots, tris), 0) == slot_ref[...]
    hit = jnp.where(hit, 1.0, 0.0).astype(bf16)
    values = jnp.concatenate(
        [got_ref[:, c * cap : (c + 1) * cap, :].reshape(slots, LANES).T for c in range(channels)], axis=0
    )
    picked = dot(jnp.concatenate(halves(values), axis=1), jnp.concatenate([hit, hit], axis=0))
    wt = wt_ref[...]
    for c in range(channels):
        far = jnp.sum(picked[c * LANES : (c + 1) * LANES] * wt, axis=0, keepdims=True)
        out_ref[c : c + 1, :] = far + near_ref[c : c + 1, :]


def exchange(x, axis):
    parts = lax.axis_size(axis)
    sent = x.reshape(parts, 1, x.size // parts)
    return lax.all_to_all(sent, axis, split_axis=0, concat_axis=0, tiled=True).reshape(x.shape)


def per_device(sources, proj_weight, tri_slot, cell_block, green, near_index, near_coef):
    slabs, pencils = lax.axis_size("slab"), lax.axis_size("pencil")
    channels, tris = sources.shape
    slots = cell_block.shape[0]
    cap = slots // pencils
    n = green.shape[2]
    devices = slabs * pencils
    zf, xf, y_both, xi, zi = tables(n)
    slot_row = tri_slot.reshape(1, tris)
    block_row = cell_block.reshape(1, slots)

    msg = call(
        charges_kernel,
        struct((pencils, channels * cap + cap // 2, LANES), f32),
        scratch=[
            pltpu.VMEM((channels, tris), f32),
            pltpu.VMEM((tris, LANES), f32),
            pltpu.VMEM((1, tris), jnp.int32),
            pltpu.VMEM((1, slots), jnp.int32),
            pltpu.SemaphoreType.DMA((4,)),
        ],
        in_specs=[pl.BlockSpec(memory_space=pltpu.HBM)] * 4,
        mib=60,
    )(sources, proj_weight, slot_row, block_row)
    got = exchange(msg, "pencil")
    msg, hit = call(
        forward_kernel,
        (struct((devices * 10, LANES), f32), struct((512, slots), bf16)),
        scratch=[pltpu.VMEM((channels * LANES, 512), f32), pltpu.VMEM((2 * n, 512), f32)],
    )(got, green.reshape(n, n), zf)
    got = exchange(msg, BOTH)
    msg = call(plane_kernel, struct((devices * 8, LANES), f32))(got, xf, y_both, xi)
    got = exchange(msg, BOTH)
    msg = call(
        inverse_kernel,
        struct((pencils, channels * cap, LANES), f32),
        scratch=[pltpu.VMEM((2 * n, 512), f32), pltpu.VMEM((channels * LANES, 512), f32)],
    )(got, hit, zi)
    near, wt = call(
        near_kernel,
        (struct((channels, tris), f32), struct((LANES, tris), f32)),
        cost=(1 << 30, 1 << 20),
    )(sources, sources.reshape(channels, 8, LANES), near_index, near_coef, proj_weight)
    got = exchange(msg, "pencil")
    return call(far_kernel, struct((channels, tris), f32))(got, slot_row, wt, near)


def solution(mesh):
    return jax.shard_map(
        per_device,
        mesh=mesh,
        in_specs=(
            P(None, BOTH),
            P(BOTH, None),
            P(BOTH),
            P(BOTH),
            P("slab", "pencil", None),
            P(None, BOTH),
            P(None, None, BOTH),
        ),
        out_specs=P(None, BOTH),
        check_vma=False,
    )
```

```python
import math

import jax
import jax.numpy as jnp
import numpy as np
from jax import lax
from jax.experimental import pallas as pl
from jax.experimental.pallas import tpu as pltpu
from jax.sharding import PartitionSpec as P

f32 = jnp.float32
bf16 = jnp.bfloat16
BOTH = ("slab", "pencil")
LANES = 128
struct = jax.ShapeDtypeStruct


def call(body, out_shape, scratch=(), mib=24, cost=(0, 0), in_specs=None):
    more = {} if in_specs is None else {"in_specs": in_specs}
    return pl.pallas_call(
        body,
        out_shape=out_shape,
        scratch_shapes=list(scratch),
        compiler_params=pltpu.CompilerParams(vmem_limit_bytes=mib << 20),
        cost_estimate=pl.CostEstimate(flops=cost[0], bytes_accessed=cost[1], transcendentals=0),
        **more,
    )


def halves(x):
    high = x.astype(bf16)
    return high, (x - high.astype(f32)).astype(bf16)


def dot(a, b, dims=((1,), (0,))):
    return lax.dot_general(a, b, (dims, ((), ())), preferred_element_type=f32)


def table_dot(table, x):
    t_high, t_low = table
    high, low = halves(x)
    m = t_high.shape[0]
    both = dot(jnp.concatenate([t_high, t_low], axis=0), high)
    return both[:m] + (both[m:] + dot(t_high, low))


def dot_table(x, table):
    m = x.shape[0]
    high, low = halves(x)
    both = dot(jnp.concatenate([high, low], axis=0), table[0])
    return both[:m] + (both[m:] + dot(high, table[1]))


def complex_table(rows, row_part, columns, column_part, n, inverse):
    angle = (np.outer(rows, columns) % n) * (2.0 * math.pi / n)
    sine = np.sin(angle) * np.where(row_part == 0, 1.0, -1.0)[:, None]
    if inverse:
        sine = -sine
    same = row_part[:, None] == column_part[None, :]
    return np.where(same, np.cos(angle), sine) / (n if inverse else 1)


def tables(n):
    half = n // 2
    part, z = np.arange(n) // half, np.arange(n) % half
    kz = [2 * z + p for p in range(2)]
    b2, slab, x_part, b1, b0 = (a.reshape(-1) for a in np.indices((2, 16, 2, 2, 2)))
    x = slab * 8 + b2 * 4 + b1 * 2 + b0
    kx_part, kx_high, kx_slab = (a.reshape(-1) for a in np.indices((2, 4, 32)))
    kx = [kx_slab * 8 + kx_high * 2 + p for p in range(2)]
    y = z // 32 * 32 + z % 8 * 4 + z // 8 % 4
    ky = [z // 16 * 32 + z % 16 * 2 + p for p in range(2)]

    def both(make):
        return jnp.asarray(np.stack([make(p) for p in range(2)]).astype(np.float32))

    return (
        both(lambda p: complex_table(kz[p], part, z, part, n, False)),
        both(lambda p: complex_table(kx[p], kx_part, x, x_part, n, False)),
        both(lambda p: complex_table(ky[p], part, y, part, n, False).T),
        both(lambda p: complex_table(y, part, ky[p], part, n, True).T),
        both(lambda p: complex_table(x, x_part, kx[p], kx_part, n, True)),
        both(lambda p: complex_table(z, part, kz[p], part, n, True)),
    )


def green_order(n):
    place = np.arange(n)
    kx = place // 64 % 2 + place // 16 % 4 * 2
    ky = place % 16 * 2 + place // 128
    return jnp.asarray((kx[:, None] * 32 + ky[:, None] == place[None, :]).astype(np.float32))


def lane_iota(rows):
    return lax.broadcasted_iota(jnp.int32, (rows, LANES), 1)


def swap_bits(parts, distances):
    parts = list(parts)
    lane = lane_iota(parts[0].shape[0])
    for level, distance in enumerate(distances):
        stride = len(parts) >> (level + 1)
        bit = (lane & distance) != 0
        for low in range(len(parts)):
            if low & stride == 0:
                a, b = parts[low], parts[low | stride]
                moved = jnp.where(bit, a, b)
                if distance == LANES // 2:
                    moved = pltpu.roll(moved, distance, 1)
                else:
                    moved = jnp.take_along_axis(moved, lane ^ distance, axis=1)
                parts[low], parts[low | stride] = jnp.where(bit, moved, a), jnp.where(bit, b, moved)
    return parts


def charges_kernel(src_hbm, w_hbm, slot_hbm, block_hbm, msg_ref, src_ref, w_ref, slot_ref, block_ref, sems):
    channels, tris = src_ref.shape
    quarter = tris // 4
    pairs = [(src_hbm, src_ref), (slot_hbm, slot_ref), (block_hbm, block_ref)]
    for i in range(4):
        rows = pl.ds(i * quarter, quarter)
        pairs.append((w_hbm.at[rows], w_ref.at[rows]))
    copies = [pltpu.make_async_copy(a, b, sems.at[i]) for i, (a, b) in enumerate(pairs)]
    for copy in copies:
        copy.start()
    for copy in copies[:3]:
        copy.wait()
    slots = block_ref.shape[1]
    pencils = msg_ref.shape[0]
    cap = slots // pencils
    rows = channels * cap
    place = jnp.broadcast_to(block_ref[...].astype(f32), (LANES, slots)).T
    place = place.reshape(pencils, cap, LANES)
    lane = lax.broadcasted_iota(jnp.int32, (pencils, cap // 2, LANES), 2)
    msg_ref[:, rows:, :] = jnp.where(lane < 64, place[:, : cap // 2], place[:, cap // 2 :])
    hit = lax.broadcasted_iota(jnp.int32, (slots, tris), 0) == slot_ref[...]
    left = [halves(jnp.where(hit, src_ref[c : c + 1, :], 0.0)) for c in range(channels)]
    left = [jnp.concatenate([pair[i] for pair in left], axis=0) for i in range(2)]
    for copy in copies[3:]:
        copy.wait()
    w_high, w_low = halves(w_ref[...])
    both = dot(left[0], jnp.concatenate([w_high, w_low], axis=1))
    total = both[:, :LANES] + (both[:, LANES:] + dot(left[1], w_high))
    for c in range(channels):
        msg_ref[:, c * cap : (c + 1) * cap, :] = total[c * slots : (c + 1) * slots].reshape(pencils, cap, LANES)


def hits(place, x_blocks, y_blocks, z_blocks):
    place = place.astype(jnp.int32)
    z = place % z_blocks
    y = place // z_blocks % 64 % y_blocks
    x = place // (z_blocks * 64) % x_blocks
    group = z // 8
    lane = x * 64 + z % 8 * 8 + y
    lanes = lane_iota(place.shape[0])
    return [
        jnp.where((lanes == lane) & (group == g), 1.0, 0.0).astype(bf16)
        for g in range(z_blocks // 8)
    ]


def tiles_of(part, g, x_1, x_0):
    blocks, grid = [], []
    for m in range(8):
        wave, y_low = m // 4, m % 4
        stencil = (x_1 * 2 + x_0) * 4 + y_low
        blocks.append(((part * 2 + wave) * LANES + stencil * 8, g * LANES))
        grid.append((part * 128 + (g * 8 + m) * 8, (x_1 * 2 + x_0) * LANES))
    return blocks, grid


GROUPS = [(part, g, x_1, x_0) for part in range(2) for g in range(2) for x_1 in range(2) for x_0 in range(2)]


def tile(ref, row, column):
    return ref[row : row + 8, column : column + LANES]


def forward_kernel(got_ref, green_ref, order_ref, table_ref, msg_ref, hit_ref, placed_ref, z_ref):
    pencils = got_ref.shape[0]
    cells = hit_ref.shape[1]
    cap = cells // pencils
    channels = 4
    place = got_ref[:, channels * cap :, :].reshape(cells // 2, LANES)
    lane = lane_iota(cells // 2)
    other = pltpu.roll(place, 64, 1)
    place = [jnp.where(lane < 64, a, b).reshape(pencils, cap // 2, LANES) for a, b in ((place, other), (other, place))]
    place = jnp.concatenate(place, axis=1).reshape(cells, LANES)
    hit = jnp.concatenate(hits(place, 2, 8, 32), axis=1)
    hit_ref[...] = hit.astype(f32).T.astype(bf16)
    charge = jnp.concatenate(
        [got_ref[:, c * cap : (c + 1) * cap, :].reshape(cells, LANES).T for c in range(channels)], axis=0
    )
    placed_ref[...] = dot(jnp.concatenate(halves(charge), axis=1), jnp.concatenate([hit, hit], axis=0))
    for group in GROUPS:
        blocks, grid = tiles_of(*group)
        low = swap_bits([tile(placed_ref, r, c) for r, c in blocks], (32, 16, 8))
        high = swap_bits([tile(placed_ref, r, c + 2 * LANES) for r, c in blocks], (32, 16, 8))
        for (r, c), first, second in zip(grid, low, high):
            z_ref[0, r : r + 8, c : c + LANES] = first + second
            z_ref[1, r : r + 8, c : c + LANES] = first - second
    half = msg_ref.shape[0] // 20
    for p in range(2):
        spec = table_dot(halves(table_ref[p]), z_ref[p])
        for row in range(8):
            part, x = row // 4, row % 4
            msg_ref[pl.ds(p * 10 + row, half, 20), :] = spec[
                part * half : (part + 1) * half, x * LANES : (x + 1) * LANES
            ]
    order = order_ref[...].astype(bf16)
    high, low = halves(green_ref[...])
    green = (dot(order, high) + dot(order, low)).T
    msg_ref[pl.ds(8, 2 * half, 10), :] = green[:, :LANES]
    msg_ref[pl.ds(9, 2 * half, 10), :] = green[:, LANES:]


def plane_kernel(got_ref, xf_ref, yf_ref, yi_ref, xi_ref, msg_ref):
    n = got_ref.shape[0] // 10
    half = n // 2
    got = got_ref.reshape(32, 8, 10, LANES)
    green = []
    for r in range(2):
        parts = [got[:, j, 8 + r, :] for j in range(8)]
        found = jnp.concatenate(swap_bits(parts, (64, 32, 16)), axis=0)
        green.append(jnp.concatenate([found, found], axis=1))
    found = []
    for j_2 in range(2):
        parts = [got[:, j_2 * 4 + j, :8, :].reshape(n, LANES) for j in range(4)]
        found.append(swap_bits(parts, (64, 32)))
    spec = [[], []]
    for p in range(2):
        rows = []
        for x_2 in range(2):
            columns = [found[j_2][x_2 * 2 + w] for w in range(2) for j_2 in range(2)]
            columns = [c[:half] - c[half:] if p else c[:half] + c[half:] for c in columns]
            rows.append(jnp.concatenate(columns, axis=1))
        result = table_dot(halves(xf_ref[p]), jnp.concatenate(rows, axis=0))
        for w in range(2):
            spec[w].append([result[part * half : (part + 1) * half, w * n : (w + 1) * n] for part in range(2)])
    spec = [
        jnp.concatenate([spec[w][p][part] for w in range(2) for p in range(2)], axis=0) for part in range(2)
    ]
    sums = []
    for p in range(2):
        points = [s[:, :half] - s[:, half:] if p else s[:, :half] + s[:, half:] for s in spec]
        result = dot_table(jnp.concatenate(points, axis=1), halves(yf_ref[p]))
        result = result * jnp.concatenate([green[p], green[p]], axis=0)
        sums.append(dot_table(result, halves(yi_ref[p])))
    even, odd = sums
    both = even + odd, even - odd
    spec = [
        jnp.concatenate([b[:, part * half : (part + 1) * half] for b in both], axis=1) for part in range(2)
    ]
    sums = []
    for p in range(2):
        rows = [
            jnp.concatenate([s[w * n + p * half : w * n + (p + 1) * half] for w in range(2)], axis=1)
            for s in spec
        ]
        sums.append(table_dot(halves(xi_ref[p]), jnp.concatenate(rows, axis=0)))
    even, odd = sums
    both = even + odd, even - odd
    msg = msg_ref.reshape(32, 8, 8, LANES)
    for j_2 in range(2):
        parts = [
            jnp.concatenate(
                [
                    b[x_2 * half : (x_2 + 1) * half, w * n + j_2 * LANES : w * n + (j_2 + 1) * LANES]
                    for b in both
                ],
                axis=0,
            )
            for x_2 in range(2)
            for w in range(2)
        ]
        for j, part in enumerate(swap_bits(parts, (64, 32))):
            msg[:, j_2 * 4 + j, :, :] = part.reshape(32, 8, LANES)


def inverse_kernel(got_ref, hit_ref, table_ref, msg_ref, z_ref, a_ref):
    n = got_ref.shape[0] // 8
    pencils = msg_ref.shape[0]
    cells = hit_ref.shape[1]
    cap = cells // pencils
    half = n // 2
    for p in range(2):
        rows = [
            jnp.concatenate([got_ref[pl.ds(p * 8 + part * 4 + x, half, 16), :] for x in range(4)], axis=1)
            for part in range(2)
        ]
        z_ref[p] = table_dot(halves(table_ref[p]), jnp.concatenate(rows, axis=0))
    for group in GROUPS:
        blocks, grid = tiles_of(*group)
        even = [tile(z_ref.at[0], r, c) for r, c in grid]
        odd = [tile(z_ref.at[1], r, c) for r, c in grid]
        low = swap_bits([a + b for a, b in zip(even, odd)], (32, 16, 8))
        high = swap_bits([a - b for a, b in zip(even, odd)], (32, 16, 8))
        for (r, c), first, second in zip(blocks, low, high):
            a_ref[r : r + 8, c : c + LANES] = first
            a_ref[r : r + 8, c + 2 * LANES : c + 3 * LANES] = second
    picked = dot(jnp.concatenate(halves(a_ref[...]), axis=0), hit_ref[...])
    rows = 4 * LANES
    for c in range(4):
        cells_c = picked[c * LANES : (c + 1) * LANES] + picked[rows + c * LANES : rows + (c + 1) * LANES]
        msg_ref[:, c * cap : (c + 1) * cap, :] = cells_c.T.reshape(pencils, cap, LANES)


def near_kernel(src_ref, table_ref, index_ref, coef_ref, w_ref, slot_ref, near_ref, wt_ref, hit_ref):
    channels = src_ref.shape[0]
    near, tris = index_ref.shape
    for start in range(0, tris, LANES):
        cols = slice(start, start + LANES)
        total = [jnp.zeros((8, LANES), f32) for _ in range(channels)]
        for top in range(0, near, 8):
            index = index_ref[top : top + 8, cols]
            lane, row = index & (LANES - 1), index >> 7
            got = [jnp.zeros((8, LANES), f32) for _ in range(channels)]
            for r in range(8):
                hit = row == r
                for c in range(channels):
                    line = jnp.broadcast_to(table_ref[c, r : r + 1, :], (8, LANES))
                    got[c] = jnp.where(hit, jnp.take_along_axis(line, lane, axis=1), got[c])
            a = coef_ref[0, top : top + 8, cols]
            b = coef_ref[1, top : top + 8, cols]
            for w in range(channels // 2):
                re, im = got[w], got[w + channels // 2]
                total[w] += a * re - b * im
                total[w + channels // 2] += a * im + b * re
        for c in range(channels):
            near_ref[c : c + 1, cols] = jnp.sum(total[c], axis=0, keepdims=True)
    wt_ref[...] = w_ref[...].T
    hit = lax.broadcasted_iota(jnp.int32, hit_ref.shape, 0) == slot_ref[...]
    hit_ref[...] = jnp.where(hit, 1.0, 0.0).astype(bf16)


def far_kernel(got_ref, hit_ref, wt_ref, near_ref, out_ref):
    pencils, rows, _ = got_ref.shape
    channels, tris = near_ref.shape
    cap = rows // channels
    slots = pencils * cap
    hit = hit_ref[...]
    values = jnp.concatenate(
        [got_ref[:, c * cap : (c + 1) * cap, :].reshape(slots, LANES).T for c in range(channels)], axis=0
    )
    picked = dot(jnp.concatenate(halves(values), axis=1), jnp.concatenate([hit, hit], axis=0))
    wt = wt_ref[...]
    for c in range(channels):
        far = jnp.sum(picked[c * LANES : (c + 1) * LANES] * wt, axis=0, keepdims=True)
        out_ref[c : c + 1, :] = far + near_ref[c : c + 1, :]


def exchange(x, axis):
    parts = lax.axis_size(axis)
    sent = x.reshape(parts, 1, x.size // parts)
    return lax.all_to_all(sent, axis, split_axis=0, concat_axis=0, tiled=True).reshape(x.shape)


def per_device(sources, proj_weight, tri_slot, cell_block, green, near_index, near_coef):
    slabs, pencils = lax.axis_size("slab"), lax.axis_size("pencil")
    channels, tris = sources.shape
    slots = cell_block.shape[0]
    cap = slots // pencils
    n = green.shape[2]
    devices = slabs * pencils
    zf, xf, yf, yi, xi, zi = tables(n)
    slot_row = tri_slot.reshape(1, tris)
    block_row = cell_block.reshape(1, slots)

    msg = call(
        charges_kernel,
        struct((pencils, channels * cap + cap // 2, LANES), f32),
        scratch=[
            pltpu.VMEM((channels, tris), f32),
            pltpu.VMEM((tris, LANES), f32),
            pltpu.VMEM((1, tris), jnp.int32),
            pltpu.VMEM((1, slots), jnp.int32),
            pltpu.SemaphoreType.DMA((7,)),
        ],
        in_specs=[pl.BlockSpec(memory_space=pltpu.HBM)] * 4,
        mib=60,
    )(sources, proj_weight, slot_row, block_row)
    near, wt, tri_hit = call(
        near_kernel,
        (struct((channels, tris), f32), struct((LANES, tris), f32), struct((slots, tris), bf16)),
        cost=(1 << 30, 1 << 20),
    )(sources, sources.reshape(channels, 8, LANES), near_index, near_coef, proj_weight, slot_row)
    got = exchange(msg, "pencil")
    got, near, wt, tri_hit = lax.optimization_barrier((got, near, wt, tri_hit))
    msg, hit = call(
        forward_kernel,
        (struct((devices * 10, LANES), f32), struct((512, slots), bf16)),
        scratch=[pltpu.VMEM((channels * LANES, 512), f32), pltpu.VMEM((2, n, 512), f32)],
    )(got, green.reshape(n, n), green_order(n), zf)
    got = exchange(msg, BOTH)
    msg = call(plane_kernel, struct((devices * 8, LANES), f32))(got, xf, yf, yi, xi)
    got = exchange(msg, BOTH)
    msg = call(
        inverse_kernel,
        struct((pencils, channels * cap, LANES), f32),
        scratch=[pltpu.VMEM((2, n, 512), f32), pltpu.VMEM((channels * LANES, 512), f32)],
    )(got, hit, zi)
    got = exchange(msg, "pencil")
    return call(far_kernel, struct((channels, tris), f32))(got, tri_hit, wt, near)


def solution(mesh):
    return jax.shard_map(
        per_device,
        mesh=mesh,
        in_specs=(
            P(None, BOTH),
            P(BOTH, None),
            P(BOTH),
            P(BOTH),
            P("slab", "pencil", None),
            P(None, BOTH),
            P(None, None, BOTH),
        ),
        out_specs=P(None, BOTH),
        check_vma=False,
    )
```

```python
import math

import jax
import jax.numpy as jnp
import numpy as np
from jax import lax
from jax.experimental import pallas as pl
from jax.experimental.pallas import tpu as pltpu
from jax.sharding import PartitionSpec as P

f32 = jnp.float32
bf16 = jnp.bfloat16
BOTH = ("slab", "pencil")
LANES = 128
struct = jax.ShapeDtypeStruct


def call(body, out_shape, scratch=(), mib=24, cost=(0, 0), in_specs=None):
    more = {} if in_specs is None else {"in_specs": in_specs}
    return pl.pallas_call(
        body,
        out_shape=out_shape,
        scratch_shapes=list(scratch),
        compiler_params=pltpu.CompilerParams(vmem_limit_bytes=mib << 20),
        cost_estimate=pl.CostEstimate(flops=cost[0], bytes_accessed=cost[1], transcendentals=0),
        **more,
    )


def halves(x):
    high = x.astype(bf16)
    return high, (x - high.astype(f32)).astype(bf16)


def dot(a, b, dims=((1,), (0,))):
    return lax.dot_general(a, b, (dims, ((), ())), preferred_element_type=f32)


def table_dot(table, x):
    t_high, t_low = table
    high, low = halves(x)
    m = t_high.shape[0]
    both = dot(jnp.concatenate([t_high, t_low], axis=0), high)
    return both[:m] + (both[m:] + dot(t_high, low))


def dot_table(x, table):
    m = x.shape[0]
    high, low = halves(x)
    both = dot(jnp.concatenate([high, low], axis=0), table[0])
    return both[:m] + (both[m:] + dot(high, table[1]))


def complex_table(rows, row_part, columns, column_part, n, inverse):
    angle = (np.outer(rows, columns) % n) * (2.0 * math.pi / n)
    sine = np.sin(angle) * np.where(row_part == 0, 1.0, -1.0)[:, None]
    if inverse:
        sine = -sine
    same = row_part[:, None] == column_part[None, :]
    return np.where(same, np.cos(angle), sine) / (n if inverse else 1)


def tables(n):
    half = n // 2
    part, z = np.arange(n) // half, np.arange(n) % half
    kz = [2 * z + p for p in range(2)]
    b2, slab, x_part, b1, b0 = (a.reshape(-1) for a in np.indices((2, 16, 2, 2, 2)))
    x = slab * 8 + b2 * 4 + b1 * 2 + b0
    kx_part, kx_high, kx_slab = (a.reshape(-1) for a in np.indices((2, 4, 32)))
    kx = [kx_slab * 8 + kx_high * 2 + p for p in range(2)]
    y = z // 32 * 32 + z % 8 * 4 + z // 8 % 4
    ky = [z // 16 * 32 + z % 16 * 2 + p for p in range(2)]

    def both(make):
        return jnp.asarray(np.stack([make(p) for p in range(2)]).astype(np.float32))

    return (
        both(lambda p: complex_table(kz[p], part, z, part, n, False)),
        both(lambda p: complex_table(kx[p], kx_part, x, x_part, n, False)),
        both(lambda p: complex_table(ky[p], part, y, part, n, False).T),
        both(lambda p: complex_table(y, part, ky[p], part, n, True).T),
        both(lambda p: complex_table(x, x_part, kx[p], kx_part, n, True)),
        both(lambda p: complex_table(z, part, kz[p], part, n, True)),
    )


def green_order(n):
    place = np.arange(n)
    kx = place // 64 % 2 + place // 16 % 4 * 2
    ky = place % 16 * 2 + place // 128
    return jnp.asarray((kx[:, None] * 32 + ky[:, None] == place[None, :]).astype(np.float32))


def lane_iota(rows):
    return lax.broadcasted_iota(jnp.int32, (rows, LANES), 1)


def swap_bits(parts, distances):
    parts = list(parts)
    lane = lane_iota(parts[0].shape[0])
    for level, distance in enumerate(distances):
        stride = len(parts) >> (level + 1)
        bit = (lane & distance) != 0
        for low in range(len(parts)):
            if low & stride == 0:
                a, b = parts[low], parts[low | stride]
                moved = jnp.where(bit, a, b)
                if distance == LANES // 2:
                    moved = pltpu.roll(moved, distance, 1)
                else:
                    moved = jnp.take_along_axis(moved, lane ^ distance, axis=1)
                parts[low], parts[low | stride] = jnp.where(bit, moved, a), jnp.where(bit, b, moved)
    return parts


def charges_kernel(src_hbm, w_hbm, slot_hbm, block_hbm, msg_ref, src_ref, w_ref, slot_ref, block_ref, sems):
    channels, tris = src_ref.shape
    pairs = [(src_hbm, src_ref), (slot_hbm, slot_ref), (block_hbm, block_ref), (w_hbm, w_ref)]
    copies = [pltpu.make_async_copy(a, b, sems.at[i]) for i, (a, b) in enumerate(pairs)]
    for copy in copies:
        copy.start()
    for copy in copies[:3]:
        copy.wait()
    slots = block_ref.shape[1]
    pencils = msg_ref.shape[0] - channels * slots
    cap = slots // pencils
    rows = channels * cap + 1
    place = block_ref[...].astype(f32)
    for q in range(pencils):
        row = place if q == 0 else pltpu.roll(place, slots - q * cap, 1)
        msg_ref[q * rows + rows - 1 : (q + 1) * rows, :] = row
    hit = lax.broadcasted_iota(jnp.int32, (slots, tris), 0) == slot_ref[...]
    hit = jnp.where(hit, 1.0, 0.0).astype(bf16)
    left = [jnp.concatenate([hit * half[c : c + 1, :] for c in range(channels)], axis=0) for half in halves(src_ref[...])]
    for copy in copies[3:]:
        copy.wait()
    w_high, w_low = halves(w_ref[...])
    both = dot(left[0], jnp.concatenate([w_high, w_low], axis=1))
    total = both[:, :LANES] + (both[:, LANES:] + dot(left[1], w_high))
    for c in range(channels):
        for q in range(pencils):
            msg_ref[q * rows + c * cap : q * rows + (c + 1) * cap, :] = total[
                c * slots + q * cap : c * slots + (q + 1) * cap
            ]


def hits(place, x_blocks, y_blocks, z_blocks):
    place = place.astype(jnp.int32)
    z = place % z_blocks
    y = place // z_blocks % 64 % y_blocks
    x = place // (z_blocks * 64) % x_blocks
    group = z // 8
    lane = x * 64 + z % 8 * 8 + y
    lanes = lane_iota(place.shape[0])
    return [
        jnp.where((lanes == lane) & (group == g), 1.0, 0.0).astype(bf16)
        for g in range(z_blocks // 8)
    ]


def tiles_of(part, g, x_1, x_0):
    blocks, grid = [], []
    for m in range(8):
        wave, y_low = m // 4, m % 4
        stencil = (x_1 * 2 + x_0) * 4 + y_low
        blocks.append(((part * 2 + wave) * LANES + stencil * 8, g * LANES))
        grid.append((part * 128 + (g * 8 + m) * 8, (x_1 * 2 + x_0) * LANES))
    return blocks, grid


GROUPS = [(part, g, x_1, x_0) for part in range(2) for g in range(2) for x_1 in range(2) for x_0 in range(2)]


def tile(ref, row, column):
    return ref[row : row + 8, column : column + LANES]


def forward_kernel(got_ref, green_ref, order_ref, table_ref, msg_ref, hit_ref, placed_ref, z_ref):
    cells = hit_ref.shape[1]
    channels = 4
    pencils = got_ref.shape[0] - channels * cells
    cap = cells // pencils
    rows = channels * cap + 1
    place = jnp.concatenate(
        [jnp.broadcast_to(got_ref[(q + 1) * rows - 1 : (q + 1) * rows, :], (cap, LANES)) for q in range(pencils)], axis=0
    )
    own = lane_iota(cells) == lax.broadcasted_iota(jnp.int32, (cells, LANES), 0) % cap
    place = jnp.sum(jnp.where(own, place, 0.0), axis=1, keepdims=True)
    place = jnp.broadcast_to(place, (cells, LANES))
    hit = jnp.concatenate(hits(place, 2, 8, 32), axis=1)
    hit_ref[...] = hit.astype(f32).T.astype(bf16)
    charge = jnp.concatenate(
        [
            jnp.concatenate(
                [got_ref[q * rows + c * cap : q * rows + (c + 1) * cap, :] for q in range(pencils)], axis=0
            ).T
            for c in range(channels)
        ],
        axis=0,
    )
    placed_ref[...] = dot(jnp.concatenate(halves(charge), axis=1), jnp.concatenate([hit, hit], axis=0))
    for group in GROUPS:
        blocks, grid = tiles_of(*group)
        low = swap_bits([tile(placed_ref, r, c) for r, c in blocks], (32, 16, 8))
        high = swap_bits([tile(placed_ref, r, c + 2 * LANES) for r, c in blocks], (32, 16, 8))
        for (r, c), first, second in zip(grid, low, high):
            z_ref[0, r : r + 8, c : c + LANES] = first + second
            z_ref[1, r : r + 8, c : c + LANES] = first - second
    half = msg_ref.shape[0] // 20
    for p in range(2):
        spec = table_dot(halves(table_ref[p]), z_ref[p])
        for row in range(8):
            part, x = row // 4, row % 4
            msg_ref[pl.ds(p * 10 + row, half, 20), :] = spec[
                part * half : (part + 1) * half, x * LANES : (x + 1) * LANES
            ]
    order = order_ref[...].astype(bf16)
    high, low = halves(green_ref[...])
    green = (dot(order, high) + dot(order, low)).T
    msg_ref[pl.ds(8, 2 * half, 10), :] = green[:, :LANES]
    msg_ref[pl.ds(9, 2 * half, 10), :] = green[:, LANES:]


def plane_kernel(got_ref, xf_ref, yf_ref, yi_ref, xi_ref, msg_ref):
    n = got_ref.shape[0] // 10
    half = n // 2
    got = got_ref.reshape(32, 8, 10, LANES)
    green = []
    for r in range(2):
        parts = [got[:, j, 8 + r, :] for j in range(8)]
        found = jnp.concatenate(swap_bits(parts, (64, 32, 16)), axis=0)
        green.append(jnp.concatenate([found, found], axis=1))
    found = []
    for j_2 in range(2):
        parts = [got[:, j_2 * 4 + j, :8, :].reshape(n, LANES) for j in range(4)]
        found.append(swap_bits(parts, (64, 32)))
    spec = [[], []]
    for p in range(2):
        rows = []
        for x_2 in range(2):
            columns = [found[j_2][x_2 * 2 + w] for w in range(2) for j_2 in range(2)]
            columns = [c[:half] - c[half:] if p else c[:half] + c[half:] for c in columns]
            rows.append(jnp.concatenate(columns, axis=1))
        result = table_dot(halves(xf_ref[p]), jnp.concatenate(rows, axis=0))
        for w in range(2):
            spec[w].append([result[part * half : (part + 1) * half, w * n : (w + 1) * n] for part in range(2)])
    spec = [
        jnp.concatenate([spec[w][p][part] for w in range(2) for p in range(2)], axis=0) for part in range(2)
    ]
    sums = []
    for p in range(2):
        points = [s[:, :half] - s[:, half:] if p else s[:, :half] + s[:, half:] for s in spec]
        result = dot_table(jnp.concatenate(points, axis=1), halves(yf_ref[p]))
        result = result * jnp.concatenate([green[p], green[p]], axis=0)
        sums.append(dot_table(result, halves(yi_ref[p])))
    even, odd = sums
    both = even + odd, even - odd
    spec = [
        jnp.concatenate([b[:, part * half : (part + 1) * half] for b in both], axis=1) for part in range(2)
    ]
    sums = []
    for p in range(2):
        rows = [
            jnp.concatenate([s[w * n + p * half : w * n + (p + 1) * half] for w in range(2)], axis=1)
            for s in spec
        ]
        sums.append(table_dot(halves(xi_ref[p]), jnp.concatenate(rows, axis=0)))
    even, odd = sums
    both = even + odd, even - odd
    msg = msg_ref.reshape(32, 8, 8, LANES)
    for j_2 in range(2):
        parts = [
            jnp.concatenate(
                [
                    b[x_2 * half : (x_2 + 1) * half, w * n + j_2 * LANES : w * n + (j_2 + 1) * LANES]
                    for b in both
                ],
                axis=0,
            )
            for x_2 in range(2)
            for w in range(2)
        ]
        for j, part in enumerate(swap_bits(parts, (64, 32))):
            msg[:, j_2 * 4 + j, :, :] = part.reshape(32, 8, LANES)


def inverse_kernel(got_ref, hit_ref, table_ref, msg_ref, z_ref, a_ref):
    n = got_ref.shape[0] // 8
    pencils = msg_ref.shape[0]
    cells = hit_ref.shape[1]
    cap = cells // pencils
    half = n // 2
    for p in range(2):
        rows = [
            jnp.concatenate([got_ref[pl.ds(p * 8 + part * 4 + x, half, 16), :] for x in range(4)], axis=1)
            for part in range(2)
        ]
        z_ref[p] = table_dot(halves(table_ref[p]), jnp.concatenate(rows, axis=0))
    for group in GROUPS:
        blocks, grid = tiles_of(*group)
        even = [tile(z_ref.at[0], r, c) for r, c in grid]
        odd = [tile(z_ref.at[1], r, c) for r, c in grid]
        low = swap_bits([a + b for a, b in zip(even, odd)], (32, 16, 8))
        high = swap_bits([a - b for a, b in zip(even, odd)], (32, 16, 8))
        for (r, c), first, second in zip(blocks, low, high):
            a_ref[r : r + 8, c : c + LANES] = first
            a_ref[r : r + 8, c + 2 * LANES : c + 3 * LANES] = second
    picked = dot(jnp.concatenate(halves(a_ref[...]), axis=0), hit_ref[...])
    rows = 4 * LANES
    for c in range(4):
        cells_c = picked[c * LANES : (c + 1) * LANES] + picked[rows + c * LANES : rows + (c + 1) * LANES]
        msg_ref[:, c * cap : (c + 1) * cap, :] = cells_c.T.reshape(pencils, cap, LANES)


def near_kernel(src_ref, table_ref, index_ref, coef_ref, w_ref, slot_ref, near_ref, wt_ref, hit_ref):
    channels = src_ref.shape[0]
    near, tris = index_ref.shape
    for start in range(0, tris, LANES):
        cols = slice(start, start + LANES)
        total = [jnp.zeros((8, LANES), f32) for _ in range(channels)]
        for top in range(0, near, 8):
            index = index_ref[top : top + 8, cols]
            lane, row = index & (LANES - 1), index >> 7
            got = [jnp.zeros((8, LANES), f32) for _ in range(channels)]
            for r in range(8):
                hit = row == r
                for c in range(channels):
                    line = jnp.broadcast_to(table_ref[c, r : r + 1, :], (8, LANES))
                    got[c] = jnp.where(hit, jnp.take_along_axis(line, lane, axis=1), got[c])
            a = coef_ref[0, top : top + 8, cols]
            b = coef_ref[1, top : top + 8, cols]
            for w in range(channels // 2):
                re, im = got[w], got[w + channels // 2]
                total[w] += a * re - b * im
                total[w + channels // 2] += a * im + b * re
        for c in range(channels):
            near_ref[c : c + 1, cols] = jnp.sum(total[c], axis=0, keepdims=True)
    wt_ref[...] = w_ref[...].T
    hit = lax.broadcasted_iota(jnp.int32, hit_ref.shape, 0) == slot_ref[...]
    hit_ref[...] = jnp.where(hit, 1.0, 0.0).astype(bf16)


def far_kernel(got_ref, hit_ref, wt_ref, near_ref, out_ref):
    pencils, rows, _ = got_ref.shape
    channels, tris = near_ref.shape
    cap = rows // channels
    slots = pencils * cap
    hit = hit_ref[...]
    values = jnp.concatenate(
        [got_ref[:, c * cap : (c + 1) * cap, :].reshape(slots, LANES).T for c in range(channels)], axis=0
    )
    picked = dot(jnp.concatenate(halves(values), axis=1), jnp.concatenate([hit, hit], axis=0))
    wt = wt_ref[...]
    for c in range(channels):
        far = jnp.sum(picked[c * LANES : (c + 1) * LANES] * wt, axis=0, keepdims=True)
        out_ref[c : c + 1, :] = far + near_ref[c : c + 1, :]


def exchange(x, axis):
    parts = lax.axis_size(axis)
    sent = x.reshape(parts, 1, x.size // parts)
    return lax.all_to_all(sent, axis, split_axis=0, concat_axis=0, tiled=True).reshape(x.shape)


def per_device(sources, proj_weight, tri_slot, cell_block, green, near_index, near_coef):
    slabs, pencils = lax.axis_size("slab"), lax.axis_size("pencil")
    channels, tris = sources.shape
    slots = cell_block.shape[0]
    cap = slots // pencils
    n = green.shape[2]
    devices = slabs * pencils
    zf, xf, yf, yi, xi, zi = tables(n)
    slot_row = tri_slot.reshape(1, tris)
    block_row = cell_block.reshape(1, slots)

    msg = call(
        charges_kernel,
        struct((pencils * (channels * cap + 1), LANES), f32),
        scratch=[
            pltpu.VMEM((channels, tris), f32),
            pltpu.VMEM((tris, LANES), f32),
            pltpu.VMEM((1, tris), jnp.int32),
            pltpu.VMEM((1, slots), jnp.int32),
            pltpu.SemaphoreType.DMA((4,)),
        ],
        in_specs=[pl.BlockSpec(memory_space=pltpu.HBM)] * 4,
        mib=60,
    )(sources, proj_weight, slot_row, block_row)
    near, wt, tri_hit = call(
        near_kernel,
        (struct((channels, tris), f32), struct((LANES, tris), f32), struct((slots, tris), bf16)),
        cost=(1 << 30, 1 << 20),
    )(sources, sources.reshape(channels, 8, LANES), near_index, near_coef, proj_weight, slot_row)
    got = exchange(msg, "pencil")
    got, near, wt, tri_hit = lax.optimization_barrier((got, near, wt, tri_hit))
    msg, hit = call(
        forward_kernel,
        (struct((devices * 10, LANES), f32), struct((512, slots), bf16)),
        scratch=[pltpu.VMEM((channels * LANES, 512), f32), pltpu.VMEM((2, n, 512), f32)],
    )(got, green.reshape(n, n), green_order(n), zf)
    got = exchange(msg, BOTH)
    msg = call(plane_kernel, struct((devices * 8, LANES), f32))(got, xf, yf, yi, xi)
    got = exchange(msg, BOTH)
    msg = call(
        inverse_kernel,
        struct((pencils, channels * cap, LANES), f32),
        scratch=[pltpu.VMEM((2, n, 512), f32), pltpu.VMEM((channels * LANES, 512), f32)],
    )(got, hit, zi)
    got = exchange(msg, "pencil")
    return call(far_kernel, struct((channels, tris), f32))(got, tri_hit, wt, near)


def solution(mesh):
    return jax.shard_map(
        per_device,
        mesh=mesh,
        in_specs=(
            P(None, BOTH),
            P(BOTH, None),
            P(BOTH),
            P(BOTH),
            P("slab", "pencil", None),
            P(None, BOTH),
            P(None, None, BOTH),
        ),
        out_specs=P(None, BOTH),
        check_vma=False,
    )
```

```python
import math

import jax
import jax.numpy as jnp
import numpy as np
from jax import lax
from jax.experimental import pallas as pl
from jax.experimental.pallas import tpu as pltpu
from jax.sharding import PartitionSpec as P

f32 = jnp.float32
bf16 = jnp.bfloat16
BOTH = ("slab", "pencil")
LANES = 128
struct = jax.ShapeDtypeStruct


def call(body, out_shape, scratch=(), mib=24, cost=(0, 0), in_specs=None):
    more = {} if in_specs is None else {"in_specs": in_specs}
    return pl.pallas_call(
        body,
        out_shape=out_shape,
        scratch_shapes=list(scratch),
        compiler_params=pltpu.CompilerParams(vmem_limit_bytes=mib << 20),
        cost_estimate=pl.CostEstimate(flops=cost[0], bytes_accessed=cost[1], transcendentals=0),
        **more,
    )


def halves(x):
    high = x.astype(bf16)
    return high, (x - high.astype(f32)).astype(bf16)


def dot(a, b, dims=((1,), (0,))):
    return lax.dot_general(a, b, (dims, ((), ())), preferred_element_type=f32)


def table_dot(table, x):
    t_high, t_low = table
    high, low = halves(x)
    m = t_high.shape[0]
    both = dot(jnp.concatenate([t_high, t_low], axis=0), high)
    return both[:m] + (both[m:] + dot(t_high, low))


def dot_table(x, table):
    m = x.shape[0]
    high, low = halves(x)
    both = dot(jnp.concatenate([high, low], axis=0), table[0])
    return both[:m] + (both[m:] + dot(high, table[1]))


def complex_table(rows, row_part, columns, column_part, n, inverse):
    angle = (np.outer(rows, columns) % n) * (2.0 * math.pi / n)
    sine = np.sin(angle) * np.where(row_part == 0, 1.0, -1.0)[:, None]
    if inverse:
        sine = -sine
    same = row_part[:, None] == column_part[None, :]
    return np.where(same, np.cos(angle), sine) / (n if inverse else 1)


def tables(n):
    half = n // 2
    part, z = np.arange(n) // half, np.arange(n) % half
    kz = [2 * z + p for p in range(2)]
    b2, slab, x_part, b1, b0 = (a.reshape(-1) for a in np.indices((2, 16, 2, 2, 2)))
    x = slab * 8 + b2 * 4 + b1 * 2 + b0
    kx_part, kx_high, kx_slab = (a.reshape(-1) for a in np.indices((2, 4, 32)))
    kx = [kx_slab * 8 + kx_high * 2 + p for p in range(2)]
    y = z // 32 * 32 + z % 8 * 4 + z // 8 % 4
    ky = [z // 16 * 32 + z % 16 * 2 + p for p in range(2)]

    def both(make):
        return jnp.asarray(np.stack([make(p) for p in range(2)]).astype(np.float32))

    return (
        both(lambda p: complex_table(kz[p], part, z, part, n, False)),
        both(lambda p: complex_table(kx[p], kx_part, x, x_part, n, False)),
        both(lambda p: complex_table(ky[p], part, y, part, n, False).T),
        both(lambda p: complex_table(y, part, ky[p], part, n, True).T),
        both(lambda p: complex_table(x, x_part, kx[p], kx_part, n, True)),
        both(lambda p: complex_table(z, part, kz[p], part, n, True)),
    )


def green_order(n):
    place = np.arange(n)
    kx = place // 64 % 2 + place // 16 % 4 * 2
    ky = place % 16 * 2 + place // 128
    return jnp.asarray((kx[:, None] * 32 + ky[:, None] == place[None, :]).astype(np.float32))


def lane_iota(rows):
    return lax.broadcasted_iota(jnp.int32, (rows, LANES), 1)


def swap_bits(parts, distances):
    parts = list(parts)
    lane = lane_iota(parts[0].shape[0])
    for level, distance in enumerate(distances):
        stride = len(parts) >> (level + 1)
        bit = (lane & distance) != 0
        for low in range(len(parts)):
            if low & stride == 0:
                a, b = parts[low], parts[low | stride]
                moved = jnp.where(bit, a, b)
                if distance == LANES // 2:
                    moved = pltpu.roll(moved, distance, 1)
                else:
                    moved = jnp.take_along_axis(moved, lane ^ distance, axis=1)
                parts[low], parts[low | stride] = jnp.where(bit, moved, a), jnp.where(bit, b, moved)
    return parts


def block_column(block, x_blocks, y_blocks, z_blocks):
    z = block % z_blocks
    y = block // z_blocks % 64 % y_blocks
    x = block // (z_blocks * 64) % x_blocks
    return z // 8 * LANES + x * 64 + z % 8 * 8 + y


def charges_kernel(src_hbm, w_hbm, slot_hbm, block_hbm, msg_ref, src_ref, w_ref, slot_ref, block_ref, sems):
    channels, tris = src_ref.shape
    pairs = [(src_hbm, src_ref), (slot_hbm, slot_ref), (block_hbm, block_ref), (w_hbm, w_ref)]
    copies = [pltpu.make_async_copy(a, b, sems.at[i]) for i, (a, b) in enumerate(pairs)]
    for copy in copies:
        copy.start()
    for copy in copies[:3]:
        copy.wait()
    slots = block_ref.shape[1]
    pencils = msg_ref.shape[0] - channels * slots
    cap = slots // pencils
    rows = channels * cap + 1
    place = block_column(block_ref[...], 2, 8, 32).astype(f32)
    for q in range(pencils):
        row = place if q == 0 else pltpu.roll(place, slots - q * cap, 1)
        msg_ref[q * rows + rows - 1 : (q + 1) * rows, :] = row
    hit = lax.broadcasted_iota(jnp.int32, (slots, tris), 0) == slot_ref[...]
    hit = jnp.where(hit, 1.0, 0.0).astype(bf16)
    left = [jnp.concatenate([hit * half[c : c + 1, :] for c in range(channels)], axis=0) for half in halves(src_ref[...])]
    for copy in copies[3:]:
        copy.wait()
    w_high, w_low = halves(w_ref[...])
    both = dot(left[0], jnp.concatenate([w_high, w_low], axis=1))
    total = both[:, :LANES] + (both[:, LANES:] + dot(left[1], w_high))
    for c in range(channels):
        for q in range(pencils):
            msg_ref[q * rows + c * cap : q * rows + (c + 1) * cap, :] = total[
                c * slots + q * cap : c * slots + (q + 1) * cap
            ]


def tiles_of(part, g, x_1, x_0):
    blocks, grid = [], []
    for m in range(8):
        wave, y_low = m // 4, m % 4
        stencil = (x_1 * 2 + x_0) * 4 + y_low
        blocks.append(((part * 2 + wave) * LANES + stencil * 8, g * LANES))
        grid.append((part * 128 + (g * 8 + m) * 8, (x_1 * 2 + x_0) * LANES))
    return blocks, grid


GROUPS = [(part, g, x_1, x_0) for part in range(2) for g in range(2) for x_1 in range(2) for x_0 in range(2)]


def tile(ref, row, column):
    return ref[row : row + 8, column : column + LANES]


def forward_kernel(got_ref, green_ref, table_ref, msg_ref, hit_ref, placed_ref, z_ref):
    cells = hit_ref.shape[1]
    channels = 4
    pencils = got_ref.shape[0] - channels * cells
    cap = cells // pencils
    rows = channels * cap + 1
    place = jnp.concatenate(
        [jnp.broadcast_to(got_ref[(q + 1) * rows - 1 : (q + 1) * rows, :], (cap, LANES)) for q in range(pencils)], axis=0
    )
    own = lane_iota(cells) == lax.broadcasted_iota(jnp.int32, (cells, LANES), 0) % cap
    place = jnp.sum(jnp.where(own, place, 0.0), axis=1, keepdims=True)
    place = jnp.broadcast_to(place, (cells, LANES))
    lane = lane_iota(cells).astype(f32)
    hit = jnp.concatenate([jnp.where(lane + g * LANES == place, 1.0, 0.0).astype(bf16) for g in range(4)], axis=1)
    hit_ref[...] = hit.astype(f32).T.astype(bf16)
    charge = jnp.concatenate(
        [
            jnp.concatenate(
                [got_ref[q * rows + c * cap : q * rows + (c + 1) * cap, :] for q in range(pencils)], axis=0
            ).T
            for c in range(channels)
        ],
        axis=0,
    )
    placed_ref[...] = dot(jnp.concatenate(halves(charge), axis=1), jnp.concatenate([hit, hit], axis=0))
    for group in GROUPS:
        blocks, grid = tiles_of(*group)
        low = swap_bits([tile(placed_ref, r, c) for r, c in blocks], (32, 16, 8))
        high = swap_bits([tile(placed_ref, r, c + 2 * LANES) for r, c in blocks], (32, 16, 8))
        for (r, c), first, second in zip(grid, low, high):
            z_ref[0, r : r + 8, c : c + LANES] = first + second
            z_ref[1, r : r + 8, c : c + LANES] = first - second
    half = msg_ref.shape[0] // 20
    for p in range(2):
        spec = table_dot((table_ref[p, 0], table_ref[p, 1]), z_ref[p])
        for row in range(8):
            part, x = row // 4, row % 4
            msg_ref[pl.ds(p * 10 + row, half, 20), :] = spec[
                part * half : (part + 1) * half, x * LANES : (x + 1) * LANES
            ]
    for row in range(2):
        msg_ref[pl.ds(8 + row, 2 * half, 10), :] = green_ref[:, row * LANES : (row + 1) * LANES]


def plane_kernel(got_ref, xf_ref, yf_ref, yi_ref, xi_ref, msg_ref):
    n = got_ref.shape[0] // 10
    half = n // 2
    got = got_ref.reshape(32, 8, 10, LANES)
    green = []
    for r in range(2):
        parts = [got[:, j, 8 + r, :] for j in range(8)]
        found = jnp.concatenate(swap_bits(parts, (64, 32, 16)), axis=0)
        green.append(jnp.concatenate([found, found], axis=1))
    found = []
    for j_2 in range(2):
        parts = [got[:, j_2 * 4 + j, :8, :].reshape(n, LANES) for j in range(4)]
        found.append(swap_bits(parts, (64, 32)))
    spec = [[], []]
    for p in range(2):
        rows = []
        for x_2 in range(2):
            columns = [found[j_2][x_2 * 2 + w] for w in range(2) for j_2 in range(2)]
            columns = [c[:half] - c[half:] if p else c[:half] + c[half:] for c in columns]
            rows.append(jnp.concatenate(columns, axis=1))
        result = table_dot(halves(xf_ref[p]), jnp.concatenate(rows, axis=0))
        for w in range(2):
            spec[w].append([result[part * half : (part + 1) * half, w * n : (w + 1) * n] for part in range(2)])
    spec = [
        jnp.concatenate([spec[w][p][part] for w in range(2) for p in range(2)], axis=0) for part in range(2)
    ]
    sums = []
    for p in range(2):
        points = [s[:, :half] - s[:, half:] if p else s[:, :half] + s[:, half:] for s in spec]
        result = dot_table(jnp.concatenate(points, axis=1), halves(yf_ref[p]))
        result = result * jnp.concatenate([green[p], green[p]], axis=0)
        sums.append(dot_table(result, halves(yi_ref[p])))
    even, odd = sums
    both = even + odd, even - odd
    spec = [
        jnp.concatenate([b[:, part * half : (part + 1) * half] for b in both], axis=1) for part in range(2)
    ]
    sums = []
    for p in range(2):
        rows = [
            jnp.concatenate([s[w * n + p * half : w * n + (p + 1) * half] for w in range(2)], axis=1)
            for s in spec
        ]
        sums.append(table_dot(halves(xi_ref[p]), jnp.concatenate(rows, axis=0)))
    even, odd = sums
    both = even + odd, even - odd
    msg = msg_ref.reshape(32, 8, 8, LANES)
    for j_2 in range(2):
        parts = [
            jnp.concatenate(
                [
                    b[x_2 * half : (x_2 + 1) * half, w * n + j_2 * LANES : w * n + (j_2 + 1) * LANES]
                    for b in both
                ],
                axis=0,
            )
            for x_2 in range(2)
            for w in range(2)
        ]
        for j, part in enumerate(swap_bits(parts, (64, 32))):
            msg[:, j_2 * 4 + j, :, :] = part.reshape(32, 8, LANES)


def inverse_kernel(got_ref, hit_ref, table_ref, msg_ref, z_ref, a_ref):
    n = got_ref.shape[0] // 8
    pencils = msg_ref.shape[0]
    cells = hit_ref.shape[1]
    cap = cells // pencils
    half = n // 2
    for p in range(2):
        rows = [
            jnp.concatenate([got_ref[pl.ds(p * 8 + part * 4 + x, half, 16), :] for x in range(4)], axis=1)
            for part in range(2)
        ]
        z_ref[p] = table_dot(halves(table_ref[p]), jnp.concatenate(rows, axis=0))
    for group in GROUPS:
        blocks, grid = tiles_of(*group)
        even = [tile(z_ref.at[0], r, c) for r, c in grid]
        odd = [tile(z_ref.at[1], r, c) for r, c in grid]
        low = swap_bits([a + b for a, b in zip(even, odd)], (32, 16, 8))
        high = swap_bits([a - b for a, b in zip(even, odd)], (32, 16, 8))
        for (r, c), first, second in zip(blocks, low, high):
            a_ref[r : r + 8, c : c + LANES] = first
            a_ref[r : r + 8, c + 2 * LANES : c + 3 * LANES] = second
    picked = dot(jnp.concatenate(halves(a_ref[...]), axis=0), hit_ref[...])
    rows = 4 * LANES
    for c in range(4):
        cells_c = picked[c * LANES : (c + 1) * LANES] + picked[rows + c * LANES : rows + (c + 1) * LANES]
        msg_ref[:, c * cap : (c + 1) * cap, :] = cells_c.T.reshape(pencils, cap, LANES)


def near_kernel(
    src_ref, table_ref, index_ref, coef_ref, w_ref, slot_ref, green_ref, order_ref, z_ref, near_ref, wt_ref, hit_ref, out_ref, split_ref
):
    channels = src_ref.shape[0]
    near, tris = index_ref.shape
    for start in range(0, tris, LANES):
        cols = slice(start, start + LANES)
        total = [jnp.zeros((8, LANES), f32) for _ in range(channels)]
        for top in range(0, near, 8):
            index = index_ref[top : top + 8, cols]
            lane, row = index & (LANES - 1), index >> 7
            got = [jnp.zeros((8, LANES), f32) for _ in range(channels)]
            for r in range(8):
                hit = row == r
                for c in range(channels):
                    line = jnp.broadcast_to(table_ref[c, r : r + 1, :], (8, LANES))
                    got[c] = jnp.where(hit, jnp.take_along_axis(line, lane, axis=1), got[c])
            a = coef_ref[0, top : top + 8, cols]
            b = coef_ref[1, top : top + 8, cols]
            for w in range(channels // 2):
                re, im = got[w], got[w + channels // 2]
                total[w] += a * re - b * im
                total[w + channels // 2] += a * im + b * re
        for c in range(channels):
            near_ref[c : c + 1, cols] = jnp.sum(total[c], axis=0, keepdims=True)
    wt_ref[...] = w_ref[...].T
    hit = lax.broadcasted_iota(jnp.int32, hit_ref.shape, 0) == slot_ref[...]
    hit_ref[...] = jnp.where(hit, 1.0, 0.0).astype(bf16)
    order = order_ref[...].astype(bf16)
    high, low = halves(green_ref[...])
    out_ref[...] = (dot(order, high) + dot(order, low)).T
    for p in range(2):
        split_ref[p, 0], split_ref[p, 1] = halves(z_ref[p])


def far_kernel(got_ref, hit_ref, wt_ref, near_ref, out_ref):
    pencils, rows, _ = got_ref.shape
    channels, tris = near_ref.shape
    cap = rows // channels
    slots = pencils * cap
    hit = hit_ref[...]
    values = jnp.concatenate(
        [got_ref[:, c * cap : (c + 1) * cap, :].reshape(slots, LANES).T for c in range(channels)], axis=0
    )
    picked = dot(jnp.concatenate(halves(values), axis=1), jnp.concatenate([hit, hit], axis=0))
    wt = wt_ref[...]
    for c in range(channels):
        far = jnp.sum(picked[c * LANES : (c + 1) * LANES] * wt, axis=0, keepdims=True)
        out_ref[c : c + 1, :] = far + near_ref[c : c + 1, :]


def exchange(x, axis):
    parts = lax.axis_size(axis)
    sent = x.reshape(parts, 1, x.size // parts)
    return lax.all_to_all(sent, axis, split_axis=0, concat_axis=0, tiled=True).reshape(x.shape)


def per_device(sources, proj_weight, tri_slot, cell_block, green, near_index, near_coef):
    slabs, pencils = lax.axis_size("slab"), lax.axis_size("pencil")
    channels, tris = sources.shape
    slots = cell_block.shape[0]
    cap = slots // pencils
    n = green.shape[2]
    devices = slabs * pencils
    zf, xf, yf, yi, xi, zi = tables(n)
    slot_row = tri_slot.reshape(1, tris)
    block_row = cell_block.reshape(1, slots)

    msg = call(
        charges_kernel,
        struct((pencils * (channels * cap + 1), LANES), f32),
        scratch=[
            pltpu.VMEM((channels, tris), f32),
            pltpu.VMEM((tris, LANES), f32),
            pltpu.VMEM((1, tris), jnp.int32),
            pltpu.VMEM((1, slots), jnp.int32),
            pltpu.SemaphoreType.DMA((4,)),
        ],
        in_specs=[pl.BlockSpec(memory_space=pltpu.HBM)] * 4,
        mib=60,
    )(sources, proj_weight, slot_row, block_row)
    near, wt, tri_hit, green_rows, zf = call(
        near_kernel,
        (
            struct((channels, tris), f32),
            struct((LANES, tris), f32),
            struct((slots, tris), bf16),
            struct((n, n), f32),
            struct((2, 2, n, n), bf16),
        ),
        cost=(1 << 30, 1 << 20),
    )(sources, sources.reshape(channels, 8, LANES), near_index, near_coef, proj_weight, slot_row, green.reshape(n, n), green_order(n), zf)
    got = exchange(msg, "pencil")
    got, near, wt, tri_hit, green_rows, zf = lax.optimization_barrier((got, near, wt, tri_hit, green_rows, zf))
    msg, hit = call(
        forward_kernel,
        (struct((devices * 10, LANES), f32), struct((512, slots), bf16)),
        scratch=[pltpu.VMEM((channels * LANES, 512), f32), pltpu.VMEM((2, n, 512), f32)],
    )(got, green_rows, zf)
    got = exchange(msg, BOTH)
    msg = call(plane_kernel, struct((devices * 8, LANES), f32))(got, xf, yf, yi, xi)
    got = exchange(msg, BOTH)
    msg = call(
        inverse_kernel,
        struct((pencils, channels * cap, LANES), f32),
        scratch=[pltpu.VMEM((2, n, 512), f32), pltpu.VMEM((channels * LANES, 512), f32)],
    )(got, hit, zi)
    got = exchange(msg, "pencil")
    return call(far_kernel, struct((channels, tris), f32))(got, tri_hit, wt, near)


def solution(mesh):
    return jax.shard_map(
        per_device,
        mesh=mesh,
        in_specs=(
            P(None, BOTH),
            P(BOTH, None),
            P(BOTH),
            P(BOTH),
            P("slab", "pencil", None),
            P(None, BOTH),
            P(None, None, BOTH),
        ),
        out_specs=P(None, BOTH),
        check_vma=False,
    )
```

```python
import math

import jax
import jax.numpy as jnp
import numpy as np
from jax import lax
from jax.experimental import pallas as pl
from jax.experimental.pallas import tpu as pltpu
from jax.sharding import PartitionSpec as P

f32 = jnp.float32
bf16 = jnp.bfloat16
BOTH = ("slab", "pencil")
LANES = 128
struct = jax.ShapeDtypeStruct


def call(body, out_shape, scratch=(), mib=24, cost=(0, 0), in_specs=None):
    more = {} if in_specs is None else {"in_specs": in_specs}
    return pl.pallas_call(
        body,
        out_shape=out_shape,
        scratch_shapes=list(scratch),
        compiler_params=pltpu.CompilerParams(vmem_limit_bytes=mib << 20),
        cost_estimate=pl.CostEstimate(flops=cost[0], bytes_accessed=cost[1], transcendentals=0),
        **more,
    )


def halves(x):
    high = x.astype(bf16)
    return high, (x - high.astype(f32)).astype(bf16)


def dot(a, b, dims=((1,), (0,))):
    return lax.dot_general(a, b, (dims, ((), ())), preferred_element_type=f32)


def table_dot(table, x):
    t_high, t_low = table
    high, low = halves(x)
    m = t_high.shape[0]
    both = dot(jnp.concatenate([t_high, t_low], axis=0), high)
    return both[:m] + (both[m:] + dot(t_high, low))


def dot_table(x, table):
    m = x.shape[0]
    high, low = halves(x)
    both = dot(jnp.concatenate([high, low], axis=0), table[0])
    return both[:m] + (both[m:] + dot(high, table[1]))


def complex_table(rows, row_part, columns, column_part, n, inverse):
    angle = (np.outer(rows, columns) % n) * (2.0 * math.pi / n)
    sine = np.sin(angle) * np.where(row_part == 0, 1.0, -1.0)[:, None]
    if inverse:
        sine = -sine
    same = row_part[:, None] == column_part[None, :]
    return np.where(same, np.cos(angle), sine) / (n if inverse else 1)


def tables(n):
    half = n // 2
    part, z = np.arange(n) // half, np.arange(n) % half
    kz = [2 * z + p for p in range(2)]
    b2, slab, x_part, b1, b0 = (a.reshape(-1) for a in np.indices((2, 16, 2, 2, 2)))
    x = slab * 8 + b2 * 4 + b1 * 2 + b0
    kx_part, kx_high, kx_slab = (a.reshape(-1) for a in np.indices((2, 4, 32)))
    kx = [kx_slab * 8 + kx_high * 2 + p for p in range(2)]
    y = z // 32 * 32 + z % 8 * 4 + z // 8 % 4
    ky = [z // 16 * 32 + z % 16 * 2 + p for p in range(2)]

    def both(make):
        return jnp.asarray(np.stack([make(p) for p in range(2)]).astype(np.float32))

    return (
        both(lambda p: complex_table(kz[p], part, z, part, n, False)),
        both(lambda p: complex_table(kx[p], kx_part, x, x_part, n, False)),
        both(lambda p: complex_table(ky[p], part, y, part, n, False).T),
        both(lambda p: complex_table(y, part, ky[p], part, n, True).T),
        both(lambda p: complex_table(x, x_part, kx[p], kx_part, n, True)),
        both(lambda p: complex_table(z, part, kz[p], part, n, True)),
    )


def green_order(n):
    place = np.arange(n)
    kx = place // 64 % 2 + place // 16 % 4 * 2
    ky = place % 16 * 2 + place // 128
    return jnp.asarray((kx[:, None] * 32 + ky[:, None] == place[None, :]).astype(np.float32))


def lane_iota(rows):
    return lax.broadcasted_iota(jnp.int32, (rows, LANES), 1)


def swap_bits(parts, distances):
    parts = list(parts)
    lane = lane_iota(parts[0].shape[0])
    for level, distance in enumerate(distances):
        stride = len(parts) >> (level + 1)
        bit = (lane & distance) != 0
        for low in range(len(parts)):
            if low & stride == 0:
                a, b = parts[low], parts[low | stride]
                moved = jnp.where(bit, a, b)
                if distance == LANES // 2:
                    moved = pltpu.roll(moved, distance, 1)
                else:
                    moved = jnp.take_along_axis(moved, lane ^ distance, axis=1)
                parts[low], parts[low | stride] = jnp.where(bit, moved, a), jnp.where(bit, b, moved)
    return parts


def block_column(block, x_blocks, y_blocks, z_blocks):
    z = block % z_blocks
    y = block // z_blocks % 64 % y_blocks
    x = block // (z_blocks * 64) % x_blocks
    return z // 8 * LANES + x * 64 + z % 8 * 8 + y


def charges_kernel(src_hbm, w_hbm, slot_hbm, block_hbm, msg_ref, src_ref, w_ref, slot_ref, block_ref, sems):
    channels, tris = src_ref.shape
    pairs = [(src_hbm, src_ref), (slot_hbm, slot_ref), (block_hbm, block_ref), (w_hbm, w_ref)]
    copies = [pltpu.make_async_copy(a, b, sems.at[i]) for i, (a, b) in enumerate(pairs)]
    for copy in copies:
        copy.start()
    for copy in copies[:3]:
        copy.wait()
    slots = block_ref.shape[1]
    pencils = msg_ref.shape[0] - channels * slots
    cap = slots // pencils
    rows = channels * cap + 1
    place = block_column(block_ref[...], 2, 8, 32).astype(f32)
    for q in range(pencils):
        row = place if q == 0 else pltpu.roll(place, slots - q * cap, 1)
        msg_ref[q * rows + rows - 1 : (q + 1) * rows, :] = row
    hit = lax.broadcasted_iota(jnp.int32, (slots, tris), 0) == slot_ref[...]
    hit = jnp.where(hit, 1.0, 0.0).astype(bf16)
    left = [jnp.concatenate([hit * half[c : c + 1, :] for c in range(channels)], axis=0) for half in halves(src_ref[...])]
    for copy in copies[3:]:
        copy.wait()
    w_high, w_low = halves(w_ref[...])
    both = dot(left[0], jnp.concatenate([w_high, w_low], axis=1))
    total = both[:, :LANES] + (both[:, LANES:] + dot(left[1], w_high))
    for c in range(channels):
        for q in range(pencils):
            msg_ref[q * rows + c * cap : q * rows + (c + 1) * cap, :] = total[
                c * slots + q * cap : c * slots + (q + 1) * cap
            ]


def tiles_of(part, g, x_1, x_0):
    blocks, grid = [], []
    for m in range(8):
        wave, y_low = m // 4, m % 4
        stencil = (x_1 * 2 + x_0) * 4 + y_low
        blocks.append(((part * 2 + wave) * LANES + stencil * 8, g * LANES))
        grid.append((part * 128 + (g * 8 + m) * 8, (x_1 * 2 + x_0) * LANES))
    return blocks, grid


GROUPS = [(part, g, x_1, x_0) for part in range(2) for g in range(2) for x_1 in range(2) for x_0 in range(2)]


def tile(ref, row, column):
    return ref[row : row + 8, column : column + LANES]


def forward_kernel(got_ref, green_ref, table_ref, msg_ref, hit_ref, placed_ref, z_ref):
    cells = hit_ref.shape[1]
    channels = 4
    pencils = got_ref.shape[0] - channels * cells
    cap = cells // pencils
    rows = channels * cap + 1
    place = jnp.concatenate(
        [jnp.broadcast_to(got_ref[(q + 1) * rows - 1 : (q + 1) * rows, :], (cap, LANES)) for q in range(pencils)], axis=0
    )
    own = lane_iota(cells) == lax.broadcasted_iota(jnp.int32, (cells, LANES), 0) % cap
    place = jnp.sum(jnp.where(own, place, 0.0), axis=1, keepdims=True)
    place = jnp.broadcast_to(place, (cells, LANES))
    upper = place >= 2 * LANES
    at = jnp.where(upper, place - 2 * LANES, place)
    lane = lane_iota(cells).astype(f32)
    marks = [jnp.where(lane + g * LANES == at, 1.0, 0.0) for g in range(2)]
    hit = jnp.concatenate(marks + [jnp.where(upper, -mark, mark) for mark in marks], axis=1)
    hit_ref[...] = hit.T.astype(bf16)
    hit = hit.astype(bf16)
    charge = jnp.concatenate(
        [
            jnp.concatenate(
                [got_ref[q * rows + c * cap : q * rows + (c + 1) * cap, :] for q in range(pencils)], axis=0
            ).T
            for c in range(channels)
        ],
        axis=0,
    )
    placed_ref[...] = dot(jnp.concatenate(halves(charge), axis=1), jnp.concatenate([hit, hit], axis=0))
    for group in GROUPS:
        blocks, grid = tiles_of(*group)
        for p in range(2):
            found = swap_bits([tile(placed_ref, r, c + p * 2 * LANES) for r, c in blocks], (32, 16, 8))
            for (r, c), moved in zip(grid, found):
                z_ref[p, r : r + 8, c : c + LANES] = moved
    half = msg_ref.shape[0] // 20
    for p in range(2):
        spec = table_dot((table_ref[p, 0], table_ref[p, 1]), z_ref[p])
        for row in range(8):
            part, x = row // 4, row % 4
            msg_ref[pl.ds(p * 10 + row, half, 20), :] = spec[
                part * half : (part + 1) * half, x * LANES : (x + 1) * LANES
            ]
    for row in range(2):
        msg_ref[pl.ds(8 + row, 2 * half, 10), :] = green_ref[:, row * LANES : (row + 1) * LANES]


def plane_kernel(got_ref, xf_ref, yf_ref, yi_ref, xi_ref, msg_ref):
    n = got_ref.shape[0] // 10
    half = n // 2
    got = got_ref.reshape(32, 8, 10, LANES)
    green = []
    for r in range(2):
        parts = [got[:, j, 8 + r, :] for j in range(8)]
        found = jnp.concatenate(swap_bits(parts, (64, 32, 16)), axis=0)
        green.append(jnp.concatenate([found, found], axis=1))
    found = []
    for j_2 in range(2):
        parts = [got[:, j_2 * 4 + j, :8, :].reshape(n, LANES) for j in range(4)]
        found.append(swap_bits(parts, (64, 32)))
    spec = [[], []]
    for p in range(2):
        rows = []
        for x_2 in range(2):
            columns = [found[j_2][x_2 * 2 + w] for w in range(2) for j_2 in range(2)]
            columns = [c[:half] - c[half:] if p else c[:half] + c[half:] for c in columns]
            rows.append(jnp.concatenate(columns, axis=1))
        result = table_dot(halves(xf_ref[p]), jnp.concatenate(rows, axis=0))
        for w in range(2):
            spec[w].append([result[part * half : (part + 1) * half, w * n : (w + 1) * n] for part in range(2)])
    spec = [
        jnp.concatenate([spec[w][p][part] for w in range(2) for p in range(2)], axis=0) for part in range(2)
    ]
    sums = []
    for p in range(2):
        points = [s[:, :half] - s[:, half:] if p else s[:, :half] + s[:, half:] for s in spec]
        result = dot_table(jnp.concatenate(points, axis=1), halves(yf_ref[p]))
        result = result * jnp.concatenate([green[p], green[p]], axis=0)
        sums.append(dot_table(result, halves(yi_ref[p])))
    even, odd = sums
    both = even + odd, even - odd
    spec = [
        jnp.concatenate([b[:, part * half : (part + 1) * half] for b in both], axis=1) for part in range(2)
    ]
    sums = []
    for p in range(2):
        rows = [
            jnp.concatenate([s[w * n + p * half : w * n + (p + 1) * half] for w in range(2)], axis=1)
            for s in spec
        ]
        sums.append(table_dot(halves(xi_ref[p]), jnp.concatenate(rows, axis=0)))
    even, odd = sums
    both = even + odd, even - odd
    msg = msg_ref.reshape(32, 8, 8, LANES)
    for j_2 in range(2):
        parts = [
            jnp.concatenate(
                [
                    b[x_2 * half : (x_2 + 1) * half, w * n + j_2 * LANES : w * n + (j_2 + 1) * LANES]
                    for b in both
                ],
                axis=0,
            )
            for x_2 in range(2)
            for w in range(2)
        ]
        for j, part in enumerate(swap_bits(parts, (64, 32))):
            msg[:, j_2 * 4 + j, :, :] = part.reshape(32, 8, LANES)


def inverse_kernel(got_ref, hit_ref, table_ref, msg_ref, z_ref, a_ref):
    n = got_ref.shape[0] // 8
    pencils = msg_ref.shape[0]
    cells = hit_ref.shape[1]
    cap = cells // pencils
    half = n // 2
    for p in range(2):
        rows = [
            jnp.concatenate([got_ref[pl.ds(p * 8 + part * 4 + x, half, 16), :] for x in range(4)], axis=1)
            for part in range(2)
        ]
        z_ref[p] = table_dot(halves(table_ref[p]), jnp.concatenate(rows, axis=0))
    for group in GROUPS:
        blocks, grid = tiles_of(*group)
        for p in range(2):
            found = swap_bits([tile(z_ref.at[p], r, c) for r, c in grid], (32, 16, 8))
            for (r, c), moved in zip(blocks, found):
                a_ref[r : r + 8, c + p * 2 * LANES : c + (p * 2 + 1) * LANES] = moved
    picked = dot(jnp.concatenate(halves(a_ref[...]), axis=0), hit_ref[...])
    rows = 4 * LANES
    for c in range(4):
        cells_c = picked[c * LANES : (c + 1) * LANES] + picked[rows + c * LANES : rows + (c + 1) * LANES]
        msg_ref[:, c * cap : (c + 1) * cap, :] = cells_c.T.reshape(pencils, cap, LANES)


def near_kernel(
    src_ref, table_ref, index_ref, coef_ref, w_ref, slot_ref, green_ref, order_ref, z_ref, near_ref, wt_ref, hit_ref, out_ref, split_ref
):
    channels = src_ref.shape[0]
    near, tris = index_ref.shape
    for start in range(0, tris, LANES):
        cols = slice(start, start + LANES)
        total = [jnp.zeros((8, LANES), f32) for _ in range(channels)]
        for top in range(0, near, 8):
            index = index_ref[top : top + 8, cols]
            lane, row = index & (LANES - 1), index >> 7
            got = [jnp.zeros((8, LANES), f32) for _ in range(channels)]
            for r in range(8):
                hit = row == r
                for c in range(channels):
                    line = jnp.broadcast_to(table_ref[c, r : r + 1, :], (8, LANES))
                    got[c] = jnp.where(hit, jnp.take_along_axis(line, lane, axis=1), got[c])
            a = coef_ref[0, top : top + 8, cols]
            b = coef_ref[1, top : top + 8, cols]
            for w in range(channels // 2):
                re, im = got[w], got[w + channels // 2]
                total[w] += a * re - b * im
                total[w + channels // 2] += a * im + b * re
        for c in range(channels):
            near_ref[c : c + 1, cols] = jnp.sum(total[c], axis=0, keepdims=True)
    wt_ref[...] = w_ref[...].T
    hit = lax.broadcasted_iota(jnp.int32, hit_ref.shape, 0) == slot_ref[...]
    hit_ref[...] = jnp.where(hit, 1.0, 0.0).astype(bf16)
    order = order_ref[...].astype(bf16)
    high, low = halves(green_ref[...])
    out_ref[...] = (dot(order, high) + dot(order, low)).T
    for p in range(2):
        split_ref[p, 0], split_ref[p, 1] = halves(z_ref[p])


def far_kernel(got_ref, hit_ref, wt_ref, near_ref, out_ref):
    pencils, rows, _ = got_ref.shape
    channels, tris = near_ref.shape
    cap = rows // channels
    slots = pencils * cap
    hit = hit_ref[...]
    values = jnp.concatenate(
        [got_ref[:, c * cap : (c + 1) * cap, :].reshape(slots, LANES).T for c in range(channels)], axis=0
    )
    picked = dot(jnp.concatenate(halves(values), axis=1), jnp.concatenate([hit, hit], axis=0))
    wt = wt_ref[...]
    for c in range(channels):
        far = jnp.sum(picked[c * LANES : (c + 1) * LANES] * wt, axis=0, keepdims=True)
        out_ref[c : c + 1, :] = far + near_ref[c : c + 1, :]


def exchange(x, axis):
    parts = lax.axis_size(axis)
    sent = x.reshape(parts, 1, x.size // parts)
    return lax.all_to_all(sent, axis, split_axis=0, concat_axis=0, tiled=True).reshape(x.shape)


def per_device(sources, proj_weight, tri_slot, cell_block, green, near_index, near_coef):
    slabs, pencils = lax.axis_size("slab"), lax.axis_size("pencil")
    channels, tris = sources.shape
    slots = cell_block.shape[0]
    cap = slots // pencils
    n = green.shape[2]
    devices = slabs * pencils
    zf, xf, yf, yi, xi, zi = tables(n)
    slot_row = tri_slot.reshape(1, tris)
    block_row = cell_block.reshape(1, slots)

    msg = call(
        charges_kernel,
        struct((pencils * (channels * cap + 1), LANES), f32),
        scratch=[
            pltpu.VMEM((channels, tris), f32),
            pltpu.VMEM((tris, LANES), f32),
            pltpu.VMEM((1, tris), jnp.int32),
            pltpu.VMEM((1, slots), jnp.int32),
            pltpu.SemaphoreType.DMA((4,)),
        ],
        in_specs=[pl.BlockSpec(memory_space=pltpu.HBM)] * 4,
        mib=60,
    )(sources, proj_weight, slot_row, block_row)
    near, wt, tri_hit, green_rows, zf = call(
        near_kernel,
        (
            struct((channels, tris), f32),
            struct((LANES, tris), f32),
            struct((slots, tris), bf16),
            struct((n, n), f32),
            struct((2, 2, n, n), bf16),
        ),
        cost=(1 << 30, 1 << 20),
    )(sources, sources.reshape(channels, 8, LANES), near_index, near_coef, proj_weight, slot_row, green.reshape(n, n), green_order(n), zf)
    got = exchange(msg, "pencil")
    got, near, wt, tri_hit, green_rows, zf = lax.optimization_barrier((got, near, wt, tri_hit, green_rows, zf))
    msg, hit = call(
        forward_kernel,
        (struct((devices * 10, LANES), f32), struct((512, slots), bf16)),
        scratch=[pltpu.VMEM((channels * LANES, 512), f32), pltpu.VMEM((2, n, 512), f32)],
    )(got, green_rows, zf)
    got = exchange(msg, BOTH)
    msg = call(plane_kernel, struct((devices * 8, LANES), f32))(got, xf, yf, yi, xi)
    got = exchange(msg, BOTH)
    msg = call(
        inverse_kernel,
        struct((pencils, channels * cap, LANES), f32),
        scratch=[pltpu.VMEM((2, n, 512), f32), pltpu.VMEM((channels * LANES, 512), f32)],
    )(got, hit, zi)
    got = exchange(msg, "pencil")
    return call(far_kernel, struct((channels, tris), f32))(got, tri_hit, wt, near)


def solution(mesh):
    return jax.shard_map(
        per_device,
        mesh=mesh,
        in_specs=(
            P(None, BOTH),
            P(BOTH, None),
            P(BOTH),
            P(BOTH),
            P("slab", "pencil", None),
            P(None, BOTH),
            P(None, None, BOTH),
        ),
        out_specs=P(None, BOTH),
        check_vma=False,
    )
```

```python
import math

import jax
import jax.numpy as jnp
import numpy as np
from jax import lax
from jax.experimental import pallas as pl
from jax.experimental.pallas import tpu as pltpu
from jax.sharding import PartitionSpec as P

f32 = jnp.float32
bf16 = jnp.bfloat16
BOTH = ("slab", "pencil")
LANES = 128
struct = jax.ShapeDtypeStruct


def call(body, out_shape, scratch=(), mib=24, cost=(0, 0), in_specs=None):
    more = {} if in_specs is None else {"in_specs": in_specs}
    return pl.pallas_call(
        body,
        out_shape=out_shape,
        scratch_shapes=list(scratch),
        compiler_params=pltpu.CompilerParams(vmem_limit_bytes=mib << 20),
        cost_estimate=pl.CostEstimate(flops=cost[0], bytes_accessed=cost[1], transcendentals=0),
        **more,
    )


def halves(x):
    high = x.astype(bf16)
    return high, (x - high.astype(f32)).astype(bf16)


def dot(a, b, dims=((1,), (0,))):
    return lax.dot_general(a, b, (dims, ((), ())), preferred_element_type=f32)


def table_dot(table, x):
    t_high, t_low = table
    high, low = halves(x)
    m = t_high.shape[0]
    both = dot(jnp.concatenate([t_high, t_low], axis=0), high)
    return both[:m] + (both[m:] + dot(t_high, low))


def dot_table(x, table):
    m = x.shape[0]
    high, low = halves(x)
    both = dot(jnp.concatenate([high, low], axis=0), table[0])
    return both[:m] + (both[m:] + dot(high, table[1]))


def complex_table(rows, row_part, columns, column_part, n, inverse):
    angle = (np.outer(rows, columns) % n) * (2.0 * math.pi / n)
    sine = np.sin(angle) * np.where(row_part == 0, 1.0, -1.0)[:, None]
    if inverse:
        sine = -sine
    same = row_part[:, None] == column_part[None, :]
    return np.where(same, np.cos(angle), sine) / (n if inverse else 1)


def tables(n):
    half = n // 2
    part, z = np.arange(n) // half, np.arange(n) % half
    kz = [2 * z + p for p in range(2)]
    b2, slab, x_part, b1, b0 = (a.reshape(-1) for a in np.indices((2, 16, 2, 2, 2)))
    x = slab * 8 + b2 * 4 + b1 * 2 + b0
    kx_part, kx_high, kx_slab = (a.reshape(-1) for a in np.indices((2, 4, 32)))
    kx = [kx_slab * 8 + kx_high * 2 + p for p in range(2)]
    y = z // 32 * 32 + z % 8 * 4 + z // 8 % 4
    ky = [z // 16 * 32 + z % 16 * 2 + p for p in range(2)]

    def both(make):
        return jnp.asarray(np.stack([make(p) for p in range(2)]).astype(np.float32))

    return (
        both(lambda p: complex_table(kz[p], part, z, part, n, False)),
        both(lambda p: complex_table(kx[p], kx_part, x, x_part, n, False)),
        both(lambda p: complex_table(ky[p], part, y, part, n, False).T),
        both(lambda p: complex_table(y, part, ky[p], part, n, True).T),
        both(lambda p: complex_table(x, x_part, kx[p], kx_part, n, True)),
        both(lambda p: complex_table(z, part, kz[p], part, n, True)),
    )


def green_order(n):
    place = np.arange(n)
    kx = place // 64 % 2 + place // 16 % 4 * 2
    ky = place % 16 * 2 + place // 128
    return jnp.asarray((kx[:, None] * 32 + ky[:, None] == place[None, :]).astype(np.float32))


def lane_iota(rows):
    return lax.broadcasted_iota(jnp.int32, (rows, LANES), 1)


def swap_bits(parts, distances):
    parts = list(parts)
    lane = lane_iota(parts[0].shape[0])
    for level, distance in enumerate(distances):
        stride = len(parts) >> (level + 1)
        bit = (lane & distance) != 0
        for low in range(len(parts)):
            if low & stride == 0:
                a, b = parts[low], parts[low | stride]
                moved = jnp.where(bit, a, b)
                if distance == LANES // 2:
                    moved = pltpu.roll(moved, distance, 1)
                else:
                    moved = jnp.take_along_axis(moved, lane ^ distance, axis=1)
                parts[low], parts[low | stride] = jnp.where(bit, moved, a), jnp.where(bit, b, moved)
    return parts


def block_column(block, x_blocks, y_blocks, z_blocks):
    z = block % z_blocks
    y = block // z_blocks % 64 % y_blocks
    x = block // (z_blocks * 64) % x_blocks
    return z // 8 * LANES + x * 64 + z % 8 * 8 + y


def charges_kernel(src_hbm, w_hbm, slot_hbm, block_hbm, msg_ref, src_ref, w_ref, slot_ref, block_ref, sems):
    channels, tris = src_ref.shape
    pairs = [(src_hbm, src_ref), (slot_hbm, slot_ref), (block_hbm, block_ref), (w_hbm, w_ref)]
    copies = [pltpu.make_async_copy(a, b, sems.at[i]) for i, (a, b) in enumerate(pairs)]
    for copy in copies:
        copy.start()
    for copy in copies[:3]:
        copy.wait()
    slots = block_ref.shape[1]
    pencils = msg_ref.shape[0] - channels * slots
    cap = slots // pencils
    rows = channels * cap + 1
    place = block_column(block_ref[...], 2, 8, 32).astype(f32)
    for q in range(pencils):
        row = place if q == 0 else pltpu.roll(place, slots - q * cap, 1)
        msg_ref[q * rows + rows - 1 : (q + 1) * rows, :] = row
    hit = lax.broadcasted_iota(jnp.int32, (slots, tris), 0) == slot_ref[...]
    hit = jnp.where(hit, 1.0, 0.0).astype(bf16)
    left = [jnp.concatenate([hit * half[c : c + 1, :] for c in range(channels)], axis=0) for half in halves(src_ref[...])]
    for copy in copies[3:]:
        copy.wait()
    w_high, w_low = halves(w_ref[...])
    both = dot(left[0], jnp.concatenate([w_high, w_low], axis=1))
    total = both[:, :LANES] + (both[:, LANES:] + dot(left[1], w_high))
    for c in range(channels):
        for q in range(pencils):
            msg_ref[q * rows + c * cap : q * rows + (c + 1) * cap, :] = total[
                c * slots + q * cap : c * slots + (q + 1) * cap
            ]


def tiles_of(part, g, x_1, x_0):
    blocks, grid = [], []
    for m in range(8):
        wave, y_low = m // 4, m % 4
        stencil = (x_1 * 2 + x_0) * 4 + y_low
        blocks.append(((part * 2 + wave) * LANES + stencil * 8, g * LANES))
        grid.append((part * 128 + (g * 8 + m) * 8, (x_1 * 2 + x_0) * LANES))
    return blocks, grid


GROUPS = [(part, g, x_1, x_0) for part in range(2) for g in range(2) for x_1 in range(2) for x_0 in range(2)]


def tile(ref, row, column):
    return ref[row : row + 8, column : column + LANES]


def forward_kernel(got_ref, green_ref, table_ref, msg_ref, hit_ref, placed_ref, z_ref):
    cells = hit_ref.shape[1]
    channels = 4
    pencils = got_ref.shape[0] - channels * cells
    cap = cells // pencils
    rows = channels * cap + 1
    place = jnp.concatenate(
        [jnp.broadcast_to(got_ref[(q + 1) * rows - 1 : (q + 1) * rows, :], (cap, LANES)) for q in range(pencils)], axis=0
    )
    own = lane_iota(cells) == lax.broadcasted_iota(jnp.int32, (cells, LANES), 0) % cap
    place = jnp.sum(jnp.where(own, place, 0.0), axis=1, keepdims=True)
    place = jnp.broadcast_to(place, (cells, LANES))
    upper = place >= 2 * LANES
    at = jnp.where(upper, place - 2 * LANES, place)
    lane = lane_iota(cells).astype(f32)
    marks = [jnp.where(lane + g * LANES == at, 1.0, 0.0) for g in range(2)]
    hit = jnp.concatenate(marks + [jnp.where(upper, -mark, mark) for mark in marks], axis=1)
    hit_ref[...] = hit.T.astype(bf16)
    hit = hit.astype(bf16)
    charge = jnp.concatenate(
        [
            jnp.concatenate(
                [got_ref[q * rows + c * cap : q * rows + (c + 1) * cap, :] for q in range(pencils)], axis=0
            ).T
            for c in range(channels)
        ],
        axis=0,
    )
    placed_ref[...] = dot(jnp.concatenate(halves(charge), axis=1), jnp.concatenate([hit, hit], axis=0))
    for group in GROUPS:
        blocks, grid = tiles_of(*group)
        for p in range(2):
            found = swap_bits([tile(placed_ref, r, c + p * 2 * LANES) for r, c in blocks], (32, 16, 8))
            for (r, c), moved in zip(grid, found):
                z_ref[p, r : r + 8, c : c + LANES] = moved
    half = msg_ref.shape[0] // 20
    for p in range(2):
        spec = table_dot((table_ref[p, 0], table_ref[p, 1]), z_ref[p])
        for row in range(8):
            part, x = row // 4, row % 4
            msg_ref[pl.ds(p * 10 + row, half, 20), :] = spec[
                part * half : (part + 1) * half, x * LANES : (x + 1) * LANES
            ]
    for row in range(2):
        msg_ref[pl.ds(8 + row, 2 * half, 10), :] = green_ref[:, row * LANES : (row + 1) * LANES]


def plane_kernel(got_ref, xf_ref, yf_ref, yi_ref, xi_ref, msg_ref):
    n = got_ref.shape[0] // 10
    half = n // 2
    got = got_ref.reshape(32, 8, 10, LANES)
    green = []
    for r in range(2):
        parts = [got[:, j, 8 + r, :] for j in range(8)]
        found = jnp.concatenate(swap_bits(parts, (64, 32, 16)), axis=0)
        green.append(jnp.concatenate([found, found], axis=1))
    tiles = [got[:, j, :8, :].reshape(n, LANES) for j in range(8)]
    by_x = [[t[:half] + t[half:] for t in tiles], [t[:half] - t[half:] for t in tiles]]
    spec = []
    for p in range(2):
        low, high = by_x[p][:4], by_x[p][4:]
        found = [
            swap_bits([u + v for u, v in zip(low, high)], (64, 32)),
            swap_bits([u - v for u, v in zip(low, high)], (64, 32)),
        ]
        rows = [
            jnp.concatenate([found[q][x_2 * 2 + w] for w in range(2) for q in range(2)], axis=1) for x_2 in range(2)
        ]
        spec.append(table_dot(halves(xf_ref[p]), jnp.concatenate(rows, axis=0)))
    sums = []
    for q in range(2):
        rows = [
            jnp.concatenate(
                [spec[p][part * half : (part + 1) * half, (w * 2 + q) * LANES : (w * 2 + q + 1) * LANES] for part in range(2)],
                axis=1,
            )
            for w in range(2)
            for p in range(2)
        ]
        result = dot_table(jnp.concatenate(rows, axis=0), halves(yf_ref[q]))
        result = result * jnp.concatenate([green[q], green[q]], axis=0)
        sums.append(dot_table(result, halves(yi_ref[q])))
    plane = []
    for p in range(2):
        rows = [
            jnp.concatenate(
                [
                    sums[q][(w * 2 + p) * half : (w * 2 + p + 1) * half, part * half : (part + 1) * half]
                    for w in range(2)
                    for q in range(2)
                ],
                axis=1,
            )
            for part in range(2)
        ]
        plane.append(table_dot(halves(xi_ref[p]), jnp.concatenate(rows, axis=0)))
    msg = msg_ref.reshape(32, 8, 8, LANES)
    for upper in range(2):
        moved = []
        for q in range(2):
            parts = []
            for x_2 in range(2):
                for w in range(2):
                    even, odd = [
                        o[x_2 * half : (x_2 + 1) * half, (w * 2 + q) * LANES : (w * 2 + q + 1) * LANES] for o in plane
                    ]
                    parts.append(even - odd if upper else even + odd)
            moved.append(swap_bits(parts, (64, 32)))
        for j in range(4):
            for j_2 in range(2):
                part = moved[0][j] - moved[1][j] if j_2 else moved[0][j] + moved[1][j]
                msg[upper * 16 : (upper + 1) * 16, j_2 * 4 + j, :, :] = part.reshape(16, 8, LANES)


def inverse_kernel(got_ref, hit_ref, table_ref, msg_ref, z_ref, a_ref):
    n = got_ref.shape[0] // 8
    pencils = msg_ref.shape[0]
    cells = hit_ref.shape[1]
    cap = cells // pencils
    half = n // 2
    for p in range(2):
        rows = [
            jnp.concatenate([got_ref[pl.ds(p * 8 + part * 4 + x, half, 16), :] for x in range(4)], axis=1)
            for part in range(2)
        ]
        z_ref[p] = table_dot(halves(table_ref[p]), jnp.concatenate(rows, axis=0))
    for group in GROUPS:
        blocks, grid = tiles_of(*group)
        for p in range(2):
            found = swap_bits([tile(z_ref.at[p], r, c) for r, c in grid], (32, 16, 8))
            for (r, c), moved in zip(blocks, found):
                a_ref[r : r + 8, c + p * 2 * LANES : c + (p * 2 + 1) * LANES] = moved
    picked = dot(jnp.concatenate(halves(a_ref[...]), axis=0), hit_ref[...])
    rows = 4 * LANES
    for c in range(4):
        cells_c = picked[c * LANES : (c + 1) * LANES] + picked[rows + c * LANES : rows + (c + 1) * LANES]
        msg_ref[:, c * cap : (c + 1) * cap, :] = cells_c.T.reshape(pencils, cap, LANES)


def near_kernel(
    src_ref, table_ref, index_ref, coef_ref, w_ref, slot_ref, green_ref, order_ref, z_ref, near_ref, wt_ref, hit_ref, out_ref, split_ref
):
    channels = src_ref.shape[0]
    near, tris = index_ref.shape
    for start in range(0, tris, LANES):
        cols = slice(start, start + LANES)
        total = [jnp.zeros((8, LANES), f32) for _ in range(channels)]
        for top in range(0, near, 8):
            index = index_ref[top : top + 8, cols]
            lane, row = index & (LANES - 1), index >> 7
            got = [jnp.zeros((8, LANES), f32) for _ in range(channels)]
            for r in range(8):
                hit = row == r
                for c in range(channels):
                    line = jnp.broadcast_to(table_ref[c, r : r + 1, :], (8, LANES))
                    got[c] = jnp.where(hit, jnp.take_along_axis(line, lane, axis=1), got[c])
            a = coef_ref[0, top : top + 8, cols]
            b = coef_ref[1, top : top + 8, cols]
            for w in range(channels // 2):
                re, im = got[w], got[w + channels // 2]
                total[w] += a * re - b * im
                total[w + channels // 2] += a * im + b * re
        for c in range(channels):
            near_ref[c : c + 1, cols] = jnp.sum(total[c], axis=0, keepdims=True)
    wt_ref[...] = w_ref[...].T
    hit = lax.broadcasted_iota(jnp.int32, hit_ref.shape, 0) == slot_ref[...]
    hit_ref[...] = jnp.where(hit, 1.0, 0.0).astype(bf16)
    order = order_ref[...].astype(bf16)
    high, low = halves(green_ref[...])
    out_ref[...] = (dot(order, high) + dot(order, low)).T
    for p in range(2):
        split_ref[p, 0], split_ref[p, 1] = halves(z_ref[p])


def far_kernel(got_ref, hit_ref, wt_ref, near_ref, out_ref):
    pencils, rows, _ = got_ref.shape
    channels, tris = near_ref.shape
    cap = rows // channels
    slots = pencils * cap
    hit = hit_ref[...]
    values = jnp.concatenate(
        [got_ref[:, c * cap : (c + 1) * cap, :].reshape(slots, LANES).T for c in range(channels)], axis=0
    )
    picked = dot(jnp.concatenate(halves(values), axis=1), jnp.concatenate([hit, hit], axis=0))
    wt = wt_ref[...]
    for c in range(channels):
        far = jnp.sum(picked[c * LANES : (c + 1) * LANES] * wt, axis=0, keepdims=True)
        out_ref[c : c + 1, :] = far + near_ref[c : c + 1, :]


def exchange(x, axis):
    parts = lax.axis_size(axis)
    sent = x.reshape(parts, 1, x.size // parts)
    return lax.all_to_all(sent, axis, split_axis=0, concat_axis=0, tiled=True).reshape(x.shape)


def per_device(sources, proj_weight, tri_slot, cell_block, green, near_index, near_coef):
    slabs, pencils = lax.axis_size("slab"), lax.axis_size("pencil")
    channels, tris = sources.shape
    slots = cell_block.shape[0]
    cap = slots // pencils
    n = green.shape[2]
    devices = slabs * pencils
    zf, xf, yf, yi, xi, zi = tables(n)
    slot_row = tri_slot.reshape(1, tris)
    block_row = cell_block.reshape(1, slots)

    msg = call(
        charges_kernel,
        struct((pencils * (channels * cap + 1), LANES), f32),
        scratch=[
            pltpu.VMEM((channels, tris), f32),
            pltpu.VMEM((tris, LANES), f32),
            pltpu.VMEM((1, tris), jnp.int32),
            pltpu.VMEM((1, slots), jnp.int32),
            pltpu.SemaphoreType.DMA((4,)),
        ],
        in_specs=[pl.BlockSpec(memory_space=pltpu.HBM)] * 4,
        mib=60,
    )(sources, proj_weight, slot_row, block_row)
    near, wt, tri_hit, green_rows, zf = call(
        near_kernel,
        (
            struct((channels, tris), f32),
            struct((LANES, tris), f32),
            struct((slots, tris), bf16),
            struct((n, n), f32),
            struct((2, 2, n, n), bf16),
        ),
        cost=(1 << 30, 1 << 20),
    )(sources, sources.reshape(channels, 8, LANES), near_index, near_coef, proj_weight, slot_row, green.reshape(n, n), green_order(n), zf)
    got = exchange(msg, "pencil")
    got, near, wt, tri_hit, green_rows, zf = lax.optimization_barrier((got, near, wt, tri_hit, green_rows, zf))
    msg, hit = call(
        forward_kernel,
        (struct((devices * 10, LANES), f32), struct((512, slots), bf16)),
        scratch=[pltpu.VMEM((channels * LANES, 512), f32), pltpu.VMEM((2, n, 512), f32)],
    )(got, green_rows, zf)
    got = exchange(msg, BOTH)
    msg = call(plane_kernel, struct((devices * 8, LANES), f32))(got, xf, yf, yi, xi)
    got = exchange(msg, BOTH)
    msg = call(
        inverse_kernel,
        struct((pencils, channels * cap, LANES), f32),
        scratch=[pltpu.VMEM((2, n, 512), f32), pltpu.VMEM((channels * LANES, 512), f32)],
    )(got, hit, zi)
    got = exchange(msg, "pencil")
    return call(far_kernel, struct((channels, tris), f32))(got, tri_hit, wt, near)


def solution(mesh):
    return jax.shard_map(
        per_device,
        mesh=mesh,
        in_specs=(
            P(None, BOTH),
            P(BOTH, None),
            P(BOTH),
            P(BOTH),
            P("slab", "pencil", None),
            P(None, BOTH),
            P(None, None, BOTH),
        ),
        out_specs=P(None, BOTH),
        check_vma=False,
    )
```

```python
import math

import jax
import jax.numpy as jnp
import numpy as np
from jax import lax
from jax.experimental import pallas as pl
from jax.experimental.pallas import tpu as pltpu
from jax.sharding import PartitionSpec as P

f32 = jnp.float32
bf16 = jnp.bfloat16
BOTH = ("slab", "pencil")
LANES = 128
struct = jax.ShapeDtypeStruct


def call(body, out_shape, scratch=(), mib=24, cost=(0, 0), in_specs=None):
    more = {} if in_specs is None else {"in_specs": in_specs}
    return pl.pallas_call(
        body,
        out_shape=out_shape,
        scratch_shapes=list(scratch),
        compiler_params=pltpu.CompilerParams(vmem_limit_bytes=mib << 20),
        cost_estimate=pl.CostEstimate(flops=cost[0], bytes_accessed=cost[1], transcendentals=0),
        **more,
    )


def halves(x):
    high = x.astype(bf16)
    return high, (x - high.astype(f32)).astype(bf16)


def dot(a, b, dims=((1,), (0,))):
    return lax.dot_general(a, b, (dims, ((), ())), preferred_element_type=f32)


def table_dot(table, x):
    t_high, t_low = table
    high, low = halves(x)
    m = t_high.shape[0]
    both = dot(jnp.concatenate([t_high, t_low], axis=0), high)
    return both[:m] + (both[m:] + dot(t_high, low))


def dot_table(x, table):
    m = x.shape[0]
    high, low = halves(x)
    both = dot(jnp.concatenate([high, low], axis=0), table[0])
    return both[:m] + (both[m:] + dot(high, table[1]))


def complex_table(rows, row_part, columns, column_part, n, inverse):
    angle = (np.outer(rows, columns) % n) * (2.0 * math.pi / n)
    sine = np.sin(angle) * np.where(row_part == 0, 1.0, -1.0)[:, None]
    if inverse:
        sine = -sine
    same = row_part[:, None] == column_part[None, :]
    return np.where(same, np.cos(angle), sine) / (n if inverse else 1)


def tables(n):
    half = n // 2
    part, z = np.arange(n) // half, np.arange(n) % half
    kz = [2 * z + p for p in range(2)]
    b2, slab, x_part, b1, b0 = (a.reshape(-1) for a in np.indices((2, 16, 2, 2, 2)))
    x = slab * 8 + b2 * 4 + b1 * 2 + b0
    kx_part, kx_high, kx_slab = (a.reshape(-1) for a in np.indices((2, 4, 32)))
    kx = [kx_slab * 8 + kx_high * 2 + p for p in range(2)]
    y = z // 32 * 32 + z % 8 * 4 + z // 8 % 4
    ky = [z // 16 * 32 + z % 16 * 2 + p for p in range(2)]

    def both(make):
        return jnp.asarray(np.stack([make(p) for p in range(2)]).astype(np.float32))

    return (
        both(lambda p: complex_table(kz[p], part, z, part, n, False)),
        both(lambda p: complex_table(kx[p], kx_part, x, x_part, n, False)),
        both(lambda p: complex_table(ky[p], part, y, part, n, False).T),
        both(lambda p: complex_table(y, part, ky[p], part, n, True).T),
        both(lambda p: complex_table(x, x_part, kx[p], kx_part, n, True)),
        both(lambda p: complex_table(z, part, kz[p], part, n, True)),
    )


def green_order(n):
    place = np.arange(n)
    kx = place // 64 % 2 + place // 16 % 4 * 2
    ky = place % 16 * 2 + place // 128
    return jnp.asarray((kx[:, None] * 32 + ky[:, None] == place[None, :]).astype(np.float32))


def lane_iota(rows):
    return lax.broadcasted_iota(jnp.int32, (rows, LANES), 1)


def swap_bits(parts, distances):
    parts = list(parts)
    lane = lane_iota(parts[0].shape[0])
    for level, distance in enumerate(distances):
        stride = len(parts) >> (level + 1)
        bit = (lane & distance) != 0
        for low in range(len(parts)):
            if low & stride == 0:
                a, b = parts[low], parts[low | stride]
                moved = jnp.where(bit, a, b)
                if distance == LANES // 2:
                    moved = pltpu.roll(moved, distance, 1)
                else:
                    moved = jnp.take_along_axis(moved, lane ^ distance, axis=1)
                parts[low], parts[low | stride] = jnp.where(bit, moved, a), jnp.where(bit, b, moved)
    return parts


def block_column(block, x_blocks, y_blocks, z_blocks):
    z = block % z_blocks
    y = block // z_blocks % 64 % y_blocks
    x = block // (z_blocks * 64) % x_blocks
    return z // 8 * LANES + x * 64 + z % 8 * 8 + y


def charges_kernel(src_hbm, w_hbm, slot_hbm, block_hbm, msg_ref, src_ref, w_ref, slot_ref, block_ref, sems):
    channels, tris = src_ref.shape
    pairs = [(src_hbm, src_ref), (slot_hbm, slot_ref), (block_hbm, block_ref), (w_hbm, w_ref)]
    copies = [pltpu.make_async_copy(a, b, sems.at[i]) for i, (a, b) in enumerate(pairs)]
    for i in (1, 3, 0, 2):
        copies[i].start()
    copies[1].wait()
    hit = lax.broadcasted_iota(jnp.int32, (block_ref.shape[1], tris), 0) == slot_ref[...]
    hit = jnp.where(hit, 1.0, 0.0).astype(bf16)
    copies[0].wait()
    copies[2].wait()
    slots = block_ref.shape[1]
    pencils = msg_ref.shape[0] - channels * slots
    cap = slots // pencils
    rows = channels * cap + 1
    place = block_column(block_ref[...], 2, 8, 32).astype(f32)
    for q in range(pencils):
        row = place if q == 0 else pltpu.roll(place, slots - q * cap, 1)
        msg_ref[q * rows + rows - 1 : (q + 1) * rows, :] = row
    left = [jnp.concatenate([hit * half[c : c + 1, :] for c in range(channels)], axis=0) for half in halves(src_ref[...])]
    for copy in copies[3:]:
        copy.wait()
    w_high, w_low = halves(w_ref[...])
    both = dot(left[0], jnp.concatenate([w_high, w_low], axis=1))
    total = both[:, :LANES] + (both[:, LANES:] + dot(left[1], w_high))
    for c in range(channels):
        for q in range(pencils):
            msg_ref[q * rows + c * cap : q * rows + (c + 1) * cap, :] = total[
                c * slots + q * cap : c * slots + (q + 1) * cap
            ]


def tiles_of(part, g, x_1, x_0):
    blocks, grid = [], []
    for m in range(8):
        wave, y_low = m // 4, m % 4
        stencil = (x_1 * 2 + x_0) * 4 + y_low
        blocks.append(((part * 2 + wave) * LANES + stencil * 8, g * LANES))
        grid.append((part * 128 + (g * 8 + m) * 8, (x_1 * 2 + x_0) * LANES))
    return blocks, grid


GROUPS = [(part, g, x_1, x_0) for part in range(2) for g in range(2) for x_1 in range(2) for x_0 in range(2)]


def tile(ref, row, column):
    return ref[row : row + 8, column : column + LANES]


def forward_kernel(got_ref, green_ref, table_ref, msg_ref, hit_ref, placed_ref, z_ref):
    cells = hit_ref.shape[1]
    channels = 4
    pencils = got_ref.shape[0] - channels * cells
    cap = cells // pencils
    rows = channels * cap + 1
    place = jnp.concatenate(
        [jnp.broadcast_to(got_ref[(q + 1) * rows - 1 : (q + 1) * rows, :], (cap, LANES)) for q in range(pencils)], axis=0
    )
    own = lane_iota(cells) == lax.broadcasted_iota(jnp.int32, (cells, LANES), 0) % cap
    place = jnp.sum(jnp.where(own, place, 0.0), axis=1, keepdims=True)
    place = jnp.broadcast_to(place, (cells, LANES))
    upper = place >= 2 * LANES
    at = jnp.where(upper, place - 2 * LANES, place)
    lane = lane_iota(cells).astype(f32)
    marks = [jnp.where(lane + g * LANES == at, 1.0, 0.0) for g in range(2)]
    hit = jnp.concatenate(marks + [jnp.where(upper, -mark, mark) for mark in marks], axis=1)
    hit_ref[...] = hit.T.astype(bf16)
    hit = hit.astype(bf16)
    charge = jnp.concatenate(
        [
            jnp.concatenate(
                [got_ref[q * rows + c * cap : q * rows + (c + 1) * cap, :] for q in range(pencils)], axis=0
            ).T
            for c in range(channels)
        ],
        axis=0,
    )
    placed_ref[...] = dot(jnp.concatenate(halves(charge), axis=1), jnp.concatenate([hit, hit], axis=0))
    for group in GROUPS:
        blocks, grid = tiles_of(*group)
        for p in range(2):
            found = swap_bits([tile(placed_ref, r, c + p * 2 * LANES) for r, c in blocks], (32, 16, 8))
            for (r, c), moved in zip(grid, found):
                z_ref[p, r : r + 8, c : c + LANES] = moved
    half = msg_ref.shape[0] // 20
    for p in range(2):
        spec = table_dot((table_ref[p, 0], table_ref[p, 1]), z_ref[p])
        for row in range(8):
            part, x = row // 4, row % 4
            msg_ref[pl.ds(p * 10 + row, half, 20), :] = spec[
                part * half : (part + 1) * half, x * LANES : (x + 1) * LANES
            ]
    for row in range(2):
        msg_ref[pl.ds(8 + row, 2 * half, 10), :] = green_ref[:, row * LANES : (row + 1) * LANES]


def plane_kernel(got_ref, xf_ref, yf_ref, yi_ref, xi_ref, msg_ref):
    n = got_ref.shape[0] // 10
    half = n // 2
    got = got_ref.reshape(32, 8, 10, LANES)
    green = []
    for r in range(2):
        parts = [got[:, j, 8 + r, :] for j in range(8)]
        found = jnp.concatenate(swap_bits(parts, (64, 32, 16)), axis=0)
        green.append(jnp.concatenate([found, found], axis=1))
    tiles = [got[:, j, :8, :].reshape(n, LANES) for j in range(8)]
    by_x = [[t[:half] + t[half:] for t in tiles], [t[:half] - t[half:] for t in tiles]]
    spec = []
    for p in range(2):
        low, high = by_x[p][:4], by_x[p][4:]
        found = [
            swap_bits([u + v for u, v in zip(low, high)], (64, 32)),
            swap_bits([u - v for u, v in zip(low, high)], (64, 32)),
        ]
        rows = [
            jnp.concatenate([found[q][x_2 * 2 + w] for w in range(2) for q in range(2)], axis=1) for x_2 in range(2)
        ]
        spec.append(table_dot(halves(xf_ref[p]), jnp.concatenate(rows, axis=0)))
    sums = []
    for q in range(2):
        rows = [
            jnp.concatenate(
                [spec[p][part * half : (part + 1) * half, (w * 2 + q) * LANES : (w * 2 + q + 1) * LANES] for part in range(2)],
                axis=1,
            )
            for w in range(2)
            for p in range(2)
        ]
        result = dot_table(jnp.concatenate(rows, axis=0), halves(yf_ref[q]))
        result = result * jnp.concatenate([green[q], green[q]], axis=0)
        sums.append(dot_table(result, halves(yi_ref[q])))
    plane = []
    for p in range(2):
        rows = [
            jnp.concatenate(
                [
                    sums[q][(w * 2 + p) * half : (w * 2 + p + 1) * half, part * half : (part + 1) * half]
                    for w in range(2)
                    for q in range(2)
                ],
                axis=1,
            )
            for part in range(2)
        ]
        plane.append(table_dot(halves(xi_ref[p]), jnp.concatenate(rows, axis=0)))
    msg = msg_ref.reshape(32, 8, 8, LANES)
    for upper in range(2):
        moved = []
        for q in range(2):
            parts = []
            for x_2 in range(2):
                for w in range(2):
                    even, odd = [
                        o[x_2 * half : (x_2 + 1) * half, (w * 2 + q) * LANES : (w * 2 + q + 1) * LANES] for o in plane
                    ]
                    parts.append(even - odd if upper else even + odd)
            moved.append(swap_bits(parts, (64, 32)))
        for j in range(4):
            for j_2 in range(2):
                part = moved[0][j] - moved[1][j] if j_2 else moved[0][j] + moved[1][j]
                msg[upper * 16 : (upper + 1) * 16, j_2 * 4 + j, :, :] = part.reshape(16, 8, LANES)


def inverse_kernel(got_ref, hit_ref, table_ref, msg_ref, z_ref, a_ref):
    n = got_ref.shape[0] // 8
    pencils = msg_ref.shape[0]
    cells = hit_ref.shape[1]
    cap = cells // pencils
    half = n // 2
    for p in range(2):
        rows = [
            jnp.concatenate([got_ref[pl.ds(p * 8 + part * 4 + x, half, 16), :] for x in range(4)], axis=1)
            for part in range(2)
        ]
        z_ref[p] = table_dot(halves(table_ref[p]), jnp.concatenate(rows, axis=0))
    for group in GROUPS:
        blocks, grid = tiles_of(*group)
        for p in range(2):
            found = swap_bits([tile(z_ref.at[p], r, c) for r, c in grid], (32, 16, 8))
            for (r, c), moved in zip(blocks, found):
                a_ref[r : r + 8, c + p * 2 * LANES : c + (p * 2 + 1) * LANES] = moved
    picked = dot(jnp.concatenate(halves(a_ref[...]), axis=0), hit_ref[...])
    rows = 4 * LANES
    for c in range(4):
        cells_c = picked[c * LANES : (c + 1) * LANES] + picked[rows + c * LANES : rows + (c + 1) * LANES]
        msg_ref[:, c * cap : (c + 1) * cap, :] = cells_c.T.reshape(pencils, cap, LANES)


def near_kernel(
    src_ref, table_ref, index_ref, coef_ref, w_ref, slot_ref, green_ref, order_ref, z_ref, near_ref, wt_ref, hit_ref, out_ref, split_ref
):
    channels = src_ref.shape[0]
    near, tris = index_ref.shape
    for start in range(0, tris, LANES):
        cols = slice(start, start + LANES)
        total = [jnp.zeros((8, LANES), f32) for _ in range(channels)]
        for top in range(0, near, 8):
            index = index_ref[top : top + 8, cols]
            lane, row = index & (LANES - 1), index >> 7
            got = [jnp.zeros((8, LANES), f32) for _ in range(channels)]
            for r in range(8):
                hit = row == r
                for c in range(channels):
                    line = jnp.broadcast_to(table_ref[c, r : r + 1, :], (8, LANES))
                    got[c] = jnp.where(hit, jnp.take_along_axis(line, lane, axis=1), got[c])
            a = coef_ref[0, top : top + 8, cols]
            b = coef_ref[1, top : top + 8, cols]
            for w in range(channels // 2):
                re, im = got[w], got[w + channels // 2]
                total[w] += a * re - b * im
                total[w + channels // 2] += a * im + b * re
        for c in range(channels):
            near_ref[c : c + 1, cols] = jnp.sum(total[c], axis=0, keepdims=True)
    wt_ref[...] = w_ref[...].T
    hit = lax.broadcasted_iota(jnp.int32, hit_ref.shape, 0) == slot_ref[...]
    hit_ref[...] = jnp.where(hit, 1.0, 0.0).astype(bf16)
    order = order_ref[...].astype(bf16)
    high, low = halves(green_ref[...])
    out_ref[...] = (dot(order, high) + dot(order, low)).T
    for p in range(2):
        split_ref[p, 0], split_ref[p, 1] = halves(z_ref[p])


def far_kernel(got_ref, hit_ref, wt_ref, near_ref, out_ref):
    pencils, rows, _ = got_ref.shape
    channels, tris = near_ref.shape
    cap = rows // channels
    slots = pencils * cap
    hit = hit_ref[...]
    values = jnp.concatenate(
        [got_ref[:, c * cap : (c + 1) * cap, :].reshape(slots, LANES).T for c in range(channels)], axis=0
    )
    picked = dot(jnp.concatenate(halves(values), axis=1), jnp.concatenate([hit, hit], axis=0))
    wt = wt_ref[...]
    for c in range(channels):
        far = jnp.sum(picked[c * LANES : (c + 1) * LANES] * wt, axis=0, keepdims=True)
        out_ref[c : c + 1, :] = far + near_ref[c : c + 1, :]


def exchange(x, axis):
    parts = lax.axis_size(axis)
    sent = x.reshape(parts, 1, x.size // parts)
    return lax.all_to_all(sent, axis, split_axis=0, concat_axis=0, tiled=True).reshape(x.shape)


def per_device(sources, proj_weight, tri_slot, cell_block, green, near_index, near_coef):
    slabs, pencils = lax.axis_size("slab"), lax.axis_size("pencil")
    channels, tris = sources.shape
    slots = cell_block.shape[0]
    cap = slots // pencils
    n = green.shape[2]
    devices = slabs * pencils
    zf, xf, yf, yi, xi, zi = tables(n)
    slot_row = tri_slot.reshape(1, tris)
    block_row = cell_block.reshape(1, slots)

    msg = call(
        charges_kernel,
        struct((pencils * (channels * cap + 1), LANES), f32),
        scratch=[
            pltpu.VMEM((channels, tris), f32),
            pltpu.VMEM((tris, LANES), f32),
            pltpu.VMEM((1, tris), jnp.int32),
            pltpu.VMEM((1, slots), jnp.int32),
            pltpu.SemaphoreType.DMA((4,)),
        ],
        in_specs=[pl.BlockSpec(memory_space=pltpu.HBM)] * 4,
        mib=60,
    )(sources, proj_weight, slot_row, block_row)
    near, wt, tri_hit, green_rows, zf = call(
        near_kernel,
        (
            struct((channels, tris), f32),
            struct((LANES, tris), f32),
            struct((slots, tris), bf16),
            struct((n, n), f32),
            struct((2, 2, n, n), bf16),
        ),
        cost=(1 << 30, 1 << 20),
    )(sources, sources.reshape(channels, 8, LANES), near_index, near_coef, proj_weight, slot_row, green.reshape(n, n), green_order(n), zf)
    got = exchange(msg, "pencil")
    got, near, wt, tri_hit, green_rows, zf = lax.optimization_barrier((got, near, wt, tri_hit, green_rows, zf))
    msg, hit = call(
        forward_kernel,
        (struct((devices * 10, LANES), f32), struct((512, slots), bf16)),
        scratch=[pltpu.VMEM((channels * LANES, 512), f32), pltpu.VMEM((2, n, 512), f32)],
    )(got, green_rows, zf)
    got = exchange(msg, BOTH)
    msg = call(plane_kernel, struct((devices * 8, LANES), f32))(got, xf, yf, yi, xi)
    got = exchange(msg, BOTH)
    msg = call(
        inverse_kernel,
        struct((pencils, channels * cap, LANES), f32),
        scratch=[pltpu.VMEM((2, n, 512), f32), pltpu.VMEM((channels * LANES, 512), f32)],
    )(got, hit, zi)
    got = exchange(msg, "pencil")
    return call(far_kernel, struct((channels, tris), f32))(got, tri_hit, wt, near)


def solution(mesh):
    return jax.shard_map(
        per_device,
        mesh=mesh,
        in_specs=(
            P(None, BOTH),
            P(BOTH, None),
            P(BOTH),
            P(BOTH),
            P("slab", "pencil", None),
            P(None, BOTH),
            P(None, None, BOTH),
        ),
        out_specs=P(None, BOTH),
        check_vma=False,
    )
```

```python
import math

import jax
import jax.numpy as jnp
import numpy as np
from jax import lax
from jax.experimental import pallas as pl
from jax.experimental.pallas import tpu as pltpu
from jax.sharding import PartitionSpec as P

f32 = jnp.float32
bf16 = jnp.bfloat16
BOTH = ("slab", "pencil")
LANES = 128
struct = jax.ShapeDtypeStruct


def call(body, out_shape, scratch=(), mib=24, cost=(0, 0), in_specs=None):
    more = {} if in_specs is None else {"in_specs": in_specs}
    return pl.pallas_call(
        body,
        out_shape=out_shape,
        scratch_shapes=list(scratch),
        compiler_params=pltpu.CompilerParams(vmem_limit_bytes=mib << 20),
        cost_estimate=pl.CostEstimate(flops=cost[0], bytes_accessed=cost[1], transcendentals=0),
        **more,
    )


def halves(x):
    high = x.astype(bf16)
    return high, (x - high.astype(f32)).astype(bf16)


def dot(a, b, dims=((1,), (0,))):
    return lax.dot_general(a, b, (dims, ((), ())), preferred_element_type=f32)


def table_dot(table, x):
    t_high, t_low = table
    high, low = halves(x)
    m = t_high.shape[0]
    both = dot(jnp.concatenate([t_high, t_low], axis=0), high)
    return both[:m] + (both[m:] + dot(t_high, low))


def dot_table(x, table):
    m = x.shape[0]
    high, low = halves(x)
    both = dot(jnp.concatenate([high, low], axis=0), table[0])
    return both[:m] + (both[m:] + dot(high, table[1]))


def complex_table(rows, row_part, columns, column_part, n, inverse):
    angle = (np.outer(rows, columns) % n) * (2.0 * math.pi / n)
    sine = np.sin(angle) * np.where(row_part == 0, 1.0, -1.0)[:, None]
    if inverse:
        sine = -sine
    same = row_part[:, None] == column_part[None, :]
    return np.where(same, np.cos(angle), sine) / (n if inverse else 1)


def tables(n):
    half = n // 2
    part, z = np.arange(n) // half, np.arange(n) % half
    kz = [2 * z + p for p in range(2)]
    b2, slab, x_part, b1, b0 = (a.reshape(-1) for a in np.indices((2, 16, 2, 2, 2)))
    x = slab * 8 + b2 * 4 + b1 * 2 + b0
    kx_part, kx_high, kx_slab = (a.reshape(-1) for a in np.indices((2, 4, 32)))
    kx = [kx_slab * 8 + kx_high * 2 + p for p in range(2)]
    y = z // 32 * 32 + z % 8 * 4 + z // 8 % 4
    ky = [z // 16 * 32 + z % 16 * 2 + p for p in range(2)]

    def both(make):
        return jnp.asarray(np.stack([make(p) for p in range(2)]).astype(np.float32))

    return (
        both(lambda p: complex_table(kz[p], part, z, part, n, False)),
        both(lambda p: complex_table(kx[p], kx_part, x, x_part, n, False)),
        both(lambda p: complex_table(ky[p], part, y, part, n, False).T),
        both(lambda p: complex_table(y, part, ky[p], part, n, True).T),
        both(lambda p: complex_table(x, x_part, kx[p], kx_part, n, True)),
        both(lambda p: complex_table(z, part, kz[p], part, n, True)),
    )


def green_order(n):
    place = np.arange(n)
    kx = place // 64 % 2 + place // 16 % 4 * 2
    ky = place % 16 * 2 + place // 128
    return jnp.asarray((kx[:, None] * 32 + ky[:, None] == place[None, :]).astype(np.float32))


def lane_iota(rows):
    return lax.broadcasted_iota(jnp.int32, (rows, LANES), 1)


def swap_bits(parts, distances):
    parts = list(parts)
    lane = lane_iota(parts[0].shape[0])
    for level, distance in enumerate(distances):
        stride = len(parts) >> (level + 1)
        bit = (lane & distance) != 0
        for low in range(len(parts)):
            if low & stride == 0:
                a, b = parts[low], parts[low | stride]
                moved = jnp.where(bit, a, b)
                if distance == LANES // 2:
                    moved = pltpu.roll(moved, distance, 1)
                else:
                    moved = jnp.take_along_axis(moved, lane ^ distance, axis=1)
                parts[low], parts[low | stride] = jnp.where(bit, moved, a), jnp.where(bit, b, moved)
    return parts


def block_column(block, x_blocks, y_blocks, z_blocks):
    z = block % z_blocks
    y = block // z_blocks % 64 % y_blocks
    x = block // (z_blocks * 64) % x_blocks
    return z // 8 * LANES + x * 64 + z % 8 * 8 + y


def charges_kernel(src_hbm, w_hbm, slot_hbm, block_hbm, msg_ref, src_ref, w_ref, slot_ref, block_ref, sems):
    channels, tris = src_ref.shape
    pairs = [(src_hbm, src_ref), (slot_hbm, slot_ref), (block_hbm, block_ref), (w_hbm, w_ref)]
    copies = [pltpu.make_async_copy(a, b, sems.at[i]) for i, (a, b) in enumerate(pairs)]
    for copy in copies:
        copy.start()
    for copy in copies[:3]:
        copy.wait()
    slots = block_ref.shape[1]
    pencils = msg_ref.shape[0] - channels * slots
    cap = slots // pencils
    rows = channels * cap + 1
    place = block_column(block_ref[...], 2, 8, 32).astype(f32)
    for q in range(pencils):
        row = place if q == 0 else pltpu.roll(place, slots - q * cap, 1)
        msg_ref[q * rows + rows - 1 : (q + 1) * rows, :] = row
    hit = lax.broadcasted_iota(jnp.int32, (slots, tris), 0) == slot_ref[...]
    hit = jnp.where(hit, 1.0, 0.0).astype(bf16)
    left = [jnp.concatenate([hit * half[c : c + 1, :] for c in range(channels)], axis=0) for half in halves(src_ref[...])]
    for copy in copies[3:]:
        copy.wait()
    w_high, w_low = halves(w_ref[...])
    both = dot(left[0], jnp.concatenate([w_high, w_low], axis=1))
    total = both[:, :LANES] + (both[:, LANES:] + dot(left[1], w_high))
    for c in range(channels):
        for q in range(pencils):
            msg_ref[q * rows + c * cap : q * rows + (c + 1) * cap, :] = total[
                c * slots + q * cap : c * slots + (q + 1) * cap
            ]


def tiles_of(part, g, x_1, x_0):
    blocks, grid = [], []
    for m in range(8):
        wave, y_low = m // 4, m % 4
        stencil = (x_1 * 2 + x_0) * 4 + y_low
        blocks.append(((part * 2 + wave) * LANES + stencil * 8, g * LANES))
        grid.append((part * 128 + (g * 8 + m) * 8, (x_1 * 2 + x_0) * LANES))
    return blocks, grid


GROUPS = [(part, g, x_1, x_0) for part in range(2) for g in range(2) for x_1 in range(2) for x_0 in range(2)]


def tile(ref, row, column):
    return ref[row : row + 8, column : column + LANES]


def forward_kernel(got_ref, green_ref, table_ref, msg_ref, hit_ref, placed_ref, z_ref):
    cells = hit_ref.shape[1]
    channels = 4
    pencils = got_ref.shape[0] - channels * cells
    cap = cells // pencils
    rows = channels * cap + 1
    place = jnp.concatenate(
        [jnp.broadcast_to(got_ref[(q + 1) * rows - 1 : (q + 1) * rows, :], (cap, LANES)) for q in range(pencils)], axis=0
    )
    own = lane_iota(cells) == lax.broadcasted_iota(jnp.int32, (cells, LANES), 0) % cap
    place = jnp.sum(jnp.where(own, place, 0.0), axis=1, keepdims=True)
    place = jnp.broadcast_to(place, (cells, LANES))
    upper = place >= 2 * LANES
    at = jnp.where(upper, place - 2 * LANES, place)
    lane = lane_iota(cells).astype(f32)
    marks = [jnp.where(lane + g * LANES == at, 1.0, 0.0) for g in range(2)]
    hit = jnp.concatenate(marks + [jnp.where(upper, -mark, mark) for mark in marks], axis=1)
    hit_ref[...] = hit.T.astype(bf16)
    hit = hit.astype(bf16)
    charge = jnp.concatenate(
        [
            jnp.concatenate(
                [got_ref[q * rows + c * cap : q * rows + (c + 1) * cap, :] for q in range(pencils)], axis=0
            ).T
            for c in range(channels)
        ],
        axis=0,
    )
    placed_ref[...] = dot(jnp.concatenate(halves(charge), axis=1), jnp.concatenate([hit, hit], axis=0))
    for group in GROUPS:
        blocks, grid = tiles_of(*group)
        for p in range(2):
            found = swap_bits([tile(placed_ref, r, c + p * 2 * LANES) for r, c in blocks], (32, 16, 8))
            for (r, c), moved in zip(grid, found):
                z_ref[p, r : r + 8, c : c + LANES] = moved
    half = msg_ref.shape[0] // 20
    for p in range(2):
        spec = table_dot((table_ref[p, 0], table_ref[p, 1]), z_ref[p])
        for row in range(8):
            part, x = row // 4, row % 4
            msg_ref[pl.ds(p * 10 + row, half, 20), :] = spec[
                part * half : (part + 1) * half, x * LANES : (x + 1) * LANES
            ]
    for row in range(2):
        msg_ref[pl.ds(8 + row, 2 * half, 10), :] = green_ref[:, row * LANES : (row + 1) * LANES]


def plane_kernel(got_ref, xf_ref, yf_ref, yi_ref, xi_ref, msg_ref):
    n = got_ref.shape[0] // 10
    half = n // 2
    got = got_ref.reshape(32, 8, 10, LANES)
    green = []
    for r in range(2):
        parts = [got[:, j, 8 + r, :] for j in range(8)]
        found = jnp.concatenate(swap_bits(parts, (64, 32, 16)), axis=0)
        green.append(jnp.concatenate([found, found], axis=1))
    tiles = [got[:, j, :8, :].reshape(n, LANES) for j in range(8)]
    by_x = [[t[:half] + t[half:] for t in tiles], [t[:half] - t[half:] for t in tiles]]
    spec = []
    for p in range(2):
        low, high = by_x[p][:4], by_x[p][4:]
        found = [
            swap_bits([u + v for u, v in zip(low, high)], (64, 32)),
            swap_bits([u - v for u, v in zip(low, high)], (64, 32)),
        ]
        rows = [
            jnp.concatenate([found[q][x_2 * 2 + w] for w in range(2) for q in range(2)], axis=1) for x_2 in range(2)
        ]
        spec.append(table_dot(halves(xf_ref[p]), jnp.concatenate(rows, axis=0)))
    sums = []
    for q in range(2):
        rows = [
            jnp.concatenate(
                [spec[p][part * half : (part + 1) * half, (w * 2 + q) * LANES : (w * 2 + q + 1) * LANES] for part in range(2)],
                axis=1,
            )
            for w in range(2)
            for p in range(2)
        ]
        result = dot_table(jnp.concatenate(rows, axis=0), halves(yf_ref[q]))
        result = result * jnp.concatenate([green[q], green[q]], axis=0)
        sums.append(dot_table(result, halves(yi_ref[q])))
    plane = []
    for p in range(2):
        rows = [
            jnp.concatenate(
                [
                    sums[q][(w * 2 + p) * half : (w * 2 + p + 1) * half, part * half : (part + 1) * half]
                    for w in range(2)
                    for q in range(2)
                ],
                axis=1,
            )
            for part in range(2)
        ]
        plane.append(table_dot(halves(xi_ref[p]), jnp.concatenate(rows, axis=0)))
    msg = msg_ref.reshape(32, 8, 8, LANES)
    for upper in range(2):
        moved = []
        for q in range(2):
            parts = []
            for x_2 in range(2):
                for w in range(2):
                    even, odd = [
                        o[x_2 * half : (x_2 + 1) * half, (w * 2 + q) * LANES : (w * 2 + q + 1) * LANES] for o in plane
                    ]
                    parts.append(even - odd if upper else even + odd)
            moved.append(swap_bits(parts, (64, 32)))
        for j in range(4):
            for j_2 in range(2):
                part = moved[0][j] - moved[1][j] if j_2 else moved[0][j] + moved[1][j]
                msg[upper * 16 : (upper + 1) * 16, j_2 * 4 + j, :, :] = part.reshape(16, 8, LANES)


def inverse_kernel(got_ref, hit_ref, table_ref, msg_ref, z_ref, a_ref):
    n = got_ref.shape[0] // 8
    pencils = msg_ref.shape[0]
    cells = hit_ref.shape[1]
    cap = cells // pencils
    half = n // 2
    for p in range(2):
        rows = [
            jnp.concatenate([got_ref[pl.ds(p * 8 + part * 4 + x, half, 16), :] for x in range(4)], axis=1)
            for part in range(2)
        ]
        z_ref[p] = table_dot((table_ref[p, 0], table_ref[p, 1]), jnp.concatenate(rows, axis=0))
    for group in GROUPS:
        blocks, grid = tiles_of(*group)
        for p in range(2):
            found = swap_bits([tile(z_ref.at[p], r, c) for r, c in grid], (32, 16, 8))
            for (r, c), moved in zip(blocks, found):
                a_ref[r : r + 8, c + p * 2 * LANES : c + (p * 2 + 1) * LANES] = moved
    picked = dot(jnp.concatenate(halves(a_ref[...]), axis=0), hit_ref[...])
    rows = 4 * LANES
    for c in range(4):
        cells_c = picked[c * LANES : (c + 1) * LANES] + picked[rows + c * LANES : rows + (c + 1) * LANES]
        msg_ref[:, c * cap : (c + 1) * cap, :] = cells_c.T.reshape(pencils, cap, LANES)


def near_kernel(
    src_ref, table_ref, index_ref, coef_ref, w_ref, slot_ref, green_ref, order_ref, zf_ref, zi_ref,
    near_ref, wt_ref, hit_ref, out_ref, zf_out_ref, zi_out_ref,
):
    channels = src_ref.shape[0]
    near, tris = index_ref.shape
    for start in range(0, tris, LANES):
        cols = slice(start, start + LANES)
        total = [jnp.zeros((8, LANES), f32) for _ in range(channels)]
        for top in range(0, near, 8):
            index = index_ref[top : top + 8, cols]
            lane, row = index & (LANES - 1), index >> 7
            got = [jnp.zeros((8, LANES), f32) for _ in range(channels)]
            for r in range(8):
                hit = row == r
                for c in range(channels):
                    line = jnp.broadcast_to(table_ref[c, r : r + 1, :], (8, LANES))
                    got[c] = jnp.where(hit, jnp.take_along_axis(line, lane, axis=1), got[c])
            a = coef_ref[0, top : top + 8, cols]
            b = coef_ref[1, top : top + 8, cols]
            for w in range(channels // 2):
                re, im = got[w], got[w + channels // 2]
                total[w] += a * re - b * im
                total[w + channels // 2] += a * im + b * re
        for c in range(channels):
            near_ref[c : c + 1, cols] = jnp.sum(total[c], axis=0, keepdims=True)
    wt_ref[...] = w_ref[...].T
    hit = lax.broadcasted_iota(jnp.int32, hit_ref.shape, 0) == slot_ref[...]
    hit_ref[...] = jnp.where(hit, 1.0, 0.0).astype(bf16)
    order = order_ref[...].astype(bf16)
    high, low = halves(green_ref[...])
    out_ref[...] = (dot(order, high) + dot(order, low)).T
    for p in range(2):
        zf_out_ref[p, 0], zf_out_ref[p, 1] = halves(zf_ref[p])
        zi_out_ref[p, 0], zi_out_ref[p, 1] = halves(zi_ref[p])


def far_kernel(got_ref, hit_ref, wt_ref, near_ref, out_ref):
    pencils, rows, _ = got_ref.shape
    channels, tris = near_ref.shape
    cap = rows // channels
    slots = pencils * cap
    hit = hit_ref[...]
    values = jnp.concatenate(
        [got_ref[:, c * cap : (c + 1) * cap, :].reshape(slots, LANES).T for c in range(channels)], axis=0
    )
    picked = dot(jnp.concatenate(halves(values), axis=1), jnp.concatenate([hit, hit], axis=0))
    wt = wt_ref[...]
    for c in range(channels):
        far = jnp.sum(picked[c * LANES : (c + 1) * LANES] * wt, axis=0, keepdims=True)
        out_ref[c : c + 1, :] = far + near_ref[c : c + 1, :]


def exchange(x, axis):
    parts = lax.axis_size(axis)
    sent = x.reshape(parts, 1, x.size // parts)
    return lax.all_to_all(sent, axis, split_axis=0, concat_axis=0, tiled=True).reshape(x.shape)


def per_device(sources, proj_weight, tri_slot, cell_block, green, near_index, near_coef):
    slabs, pencils = lax.axis_size("slab"), lax.axis_size("pencil")
    channels, tris = sources.shape
    slots = cell_block.shape[0]
    cap = slots // pencils
    n = green.shape[2]
    devices = slabs * pencils
    zf, xf, yf, yi, xi, zi = tables(n)
    slot_row = tri_slot.reshape(1, tris)
    block_row = cell_block.reshape(1, slots)

    msg = call(
        charges_kernel,
        struct((pencils * (channels * cap + 1), LANES), f32),
        scratch=[
            pltpu.VMEM((channels, tris), f32),
            pltpu.VMEM((tris, LANES), f32),
            pltpu.VMEM((1, tris), jnp.int32),
            pltpu.VMEM((1, slots), jnp.int32),
            pltpu.SemaphoreType.DMA((4,)),
        ],
        in_specs=[pl.BlockSpec(memory_space=pltpu.HBM)] * 4,
        mib=60,
    )(sources, proj_weight, slot_row, block_row)
    near, wt, tri_hit, green_rows, zf, zi = call(
        near_kernel,
        (
            struct((channels, tris), f32),
            struct((LANES, tris), f32),
            struct((slots, tris), bf16),
            struct((n, n), f32),
            struct((2, 2, n, n), bf16),
            struct((2, 2, n, n), bf16),
        ),
        cost=(1 << 30, 1 << 20),
    )(sources, sources.reshape(channels, 8, LANES), near_index, near_coef, proj_weight, slot_row, green.reshape(n, n), green_order(n), zf, zi)
    got = exchange(msg, "pencil")
    got, near, wt, tri_hit, green_rows, zf, zi = lax.optimization_barrier(
        (got, near, wt, tri_hit, green_rows, zf, zi)
    )
    msg, hit = call(
        forward_kernel,
        (struct((devices * 10, LANES), f32), struct((512, slots), bf16)),
        scratch=[pltpu.VMEM((channels * LANES, 512), f32), pltpu.VMEM((2, n, 512), f32)],
    )(got, green_rows, zf)
    got = exchange(msg, BOTH)
    msg = call(plane_kernel, struct((devices * 8, LANES), f32))(got, xf, yf, yi, xi)
    got = exchange(msg, BOTH)
    msg = call(
        inverse_kernel,
        struct((pencils, channels * cap, LANES), f32),
        scratch=[pltpu.VMEM((2, n, 512), f32), pltpu.VMEM((channels * LANES, 512), f32)],
    )(got, hit, zi)
    got = exchange(msg, "pencil")
    return call(far_kernel, struct((channels, tris), f32))(got, tri_hit, wt, near)


def solution(mesh):
    return jax.shard_map(
        per_device,
        mesh=mesh,
        in_specs=(
            P(None, BOTH),
            P(BOTH, None),
            P(BOTH),
            P(BOTH),
            P("slab", "pencil", None),
            P(None, BOTH),
            P(None, None, BOTH),
        ),
        out_specs=P(None, BOTH),
        check_vma=False,
    )
```

```python
import math

import jax
import jax.numpy as jnp
import numpy as np
from jax import lax
from jax.experimental import pallas as pl
from jax.experimental.pallas import tpu as pltpu
from jax.sharding import PartitionSpec as P

f32 = jnp.float32
bf16 = jnp.bfloat16
BOTH = ("slab", "pencil")
LANES = 128
struct = jax.ShapeDtypeStruct


def call(body, out_shape, scratch=(), mib=24, cost=(0, 0), in_specs=None):
    more = {} if in_specs is None else {"in_specs": in_specs}
    return pl.pallas_call(
        body,
        out_shape=out_shape,
        scratch_shapes=list(scratch),
        compiler_params=pltpu.CompilerParams(vmem_limit_bytes=mib << 20),
        cost_estimate=pl.CostEstimate(flops=cost[0], bytes_accessed=cost[1], transcendentals=0),
        **more,
    )


def halves(x):
    high = x.astype(bf16)
    return high, (x - high.astype(f32)).astype(bf16)


def dot(a, b, dims=((1,), (0,))):
    return lax.dot_general(a, b, (dims, ((), ())), preferred_element_type=f32)


def table_dot(table, x):
    t_high, t_low = table
    high, low = halves(x)
    m = t_high.shape[0]
    both = dot(jnp.concatenate([t_high, t_low], axis=0), high)
    return both[:m] + (both[m:] + dot(t_high, low))


def dot_table(x, table):
    m = x.shape[0]
    high, low = halves(x)
    both = dot(jnp.concatenate([high, low], axis=0), table[0])
    return both[:m] + (both[m:] + dot(high, table[1]))


def complex_table(rows, row_part, columns, column_part, n, inverse):
    angle = (np.outer(rows, columns) % n) * (2.0 * math.pi / n)
    sine = np.sin(angle) * np.where(row_part == 0, 1.0, -1.0)[:, None]
    if inverse:
        sine = -sine
    same = row_part[:, None] == column_part[None, :]
    return np.where(same, np.cos(angle), sine) / (n if inverse else 1)


def tables(n):
    half = n // 2
    part, z = np.arange(n) // half, np.arange(n) % half
    kz = [2 * z + p for p in range(2)]
    b2, slab, x_part, b1, b0 = (a.reshape(-1) for a in np.indices((2, 16, 2, 2, 2)))
    x = slab * 8 + b2 * 4 + b1 * 2 + b0
    kx_part, kx_high, kx_slab = (a.reshape(-1) for a in np.indices((2, 4, 32)))
    kx = [kx_slab * 8 + kx_high * 2 + p for p in range(2)]
    y = z // 32 * 32 + z % 8 * 4 + z // 8 % 4
    ky = [z // 16 * 32 + z % 16 * 2 + p for p in range(2)]

    def both(make):
        return jnp.asarray(np.stack([make(p) for p in range(2)]).astype(np.float32))

    return (
        both(lambda p: complex_table(kz[p], part, z, part, n, False)),
        both(lambda p: complex_table(kx[p], kx_part, x, x_part, n, False)),
        both(lambda p: complex_table(ky[p], part, y, part, n, False).T),
        both(lambda p: complex_table(y, part, ky[p], part, n, True).T),
        both(lambda p: complex_table(x, x_part, kx[p], kx_part, n, True)),
        both(lambda p: complex_table(z, part, kz[p], part, n, True)),
    )


def green_order(n):
    place = np.arange(n)
    kx = place // 64 % 2 + place // 16 % 4 * 2
    ky = place % 16 * 2 + place // 128
    return jnp.asarray((kx[:, None] * 32 + ky[:, None] == place[None, :]).astype(np.float32))


def lane_iota(rows):
    return lax.broadcasted_iota(jnp.int32, (rows, LANES), 1)


def swap_bits(parts, distances):
    parts = list(parts)
    lane = lane_iota(parts[0].shape[0])
    for level, distance in enumerate(distances):
        stride = len(parts) >> (level + 1)
        bit = (lane & distance) != 0
        for low in range(len(parts)):
            if low & stride == 0:
                a, b = parts[low], parts[low | stride]
                moved = jnp.where(bit, a, b)
                if distance == LANES // 2:
                    moved = pltpu.roll(moved, distance, 1)
                else:
                    moved = jnp.take_along_axis(moved, lane ^ distance, axis=1)
                parts[low], parts[low | stride] = jnp.where(bit, moved, a), jnp.where(bit, b, moved)
    return parts


def block_column(block, x_blocks, y_blocks, z_blocks):
    z = block % z_blocks
    y = block // z_blocks % 64 % y_blocks
    x = block // (z_blocks * 64) % x_blocks
    return z // 8 * LANES + x * 64 + z % 8 * 8 + y


def charges_kernel(src_hbm, w_hbm, slot_hbm, block_hbm, msg_ref, src_ref, w_ref, slot_ref, block_ref, sems):
    channels, tris = src_ref.shape
    pairs = [(src_hbm, src_ref), (slot_hbm, slot_ref), (block_hbm, block_ref), (w_hbm, w_ref)]
    copies = [pltpu.make_async_copy(a, b, sems.at[i]) for i, (a, b) in enumerate(pairs)]
    for copy in copies:
        copy.start()
    for copy in copies[:3]:
        copy.wait()
    slots = block_ref.shape[1]
    pencils = msg_ref.shape[0] - channels * slots
    cap = slots // pencils
    rows = channels * cap + 1
    place = block_column(block_ref[...], 2, 8, 32).astype(f32)
    for q in range(pencils):
        row = place if q == 0 else pltpu.roll(place, slots - q * cap, 1)
        msg_ref[q * rows + rows - 1 : (q + 1) * rows, :] = row
    hit = lax.broadcasted_iota(jnp.int32, (slots, tris), 0) == slot_ref[...]
    hit = jnp.where(hit, 1.0, 0.0).astype(bf16)
    left = [jnp.concatenate([hit * half[c : c + 1, :] for c in range(channels)], axis=0) for half in halves(src_ref[...])]
    for copy in copies[3:]:
        copy.wait()
    w_high, w_low = halves(w_ref[...])
    both = dot(left[0], jnp.concatenate([w_high, w_low], axis=1))
    total = both[:, :LANES] + (both[:, LANES:] + dot(left[1], w_high))
    for c in range(channels):
        for q in range(pencils):
            msg_ref[q * rows + c * cap : q * rows + (c + 1) * cap, :] = total[
                c * slots + q * cap : c * slots + (q + 1) * cap
            ]


def tiles_of(part, g, x_1, x_0):
    blocks, grid = [], []
    for m in range(8):
        wave, y_low = m // 4, m % 4
        stencil = (x_1 * 2 + x_0) * 4 + y_low
        blocks.append(((part * 2 + wave) * LANES + stencil * 8, g * LANES))
        grid.append((part * 128 + (g * 8 + m) * 8, (x_1 * 2 + x_0) * LANES))
    return blocks, grid


GROUPS = [(part, g, x_1, x_0) for part in range(2) for g in range(2) for x_1 in range(2) for x_0 in range(2)]


def tile(ref, row, column):
    return ref[row : row + 8, column : column + LANES]


def forward_kernel(got_ref, green_ref, table_ref, msg_ref, hit_ref, placed_ref, z_ref):
    half = msg_ref.shape[0] // 20
    for row in range(2):
        msg_ref[pl.ds(8 + row, 2 * half, 10), :] = green_ref[:, row * LANES : (row + 1) * LANES]
    cells = hit_ref.shape[1]
    channels = 4
    pencils = got_ref.shape[0] - channels * cells
    cap = cells // pencils
    rows = channels * cap + 1
    place = jnp.concatenate(
        [jnp.broadcast_to(got_ref[(q + 1) * rows - 1 : (q + 1) * rows, :], (cap, LANES)) for q in range(pencils)], axis=0
    )
    own = lane_iota(cells) == lax.broadcasted_iota(jnp.int32, (cells, LANES), 0) % cap
    place = jnp.sum(jnp.where(own, place, 0.0), axis=1, keepdims=True)
    place = jnp.broadcast_to(place, (cells, LANES))
    upper = place >= 2 * LANES
    at = jnp.where(upper, place - 2 * LANES, place)
    lane = lane_iota(cells).astype(f32)
    marks = [jnp.where(lane + g * LANES == at, 1.0, 0.0) for g in range(2)]
    hit = jnp.concatenate(marks + [jnp.where(upper, -mark, mark) for mark in marks], axis=1)
    hit_ref[...] = hit.T.astype(bf16)
    hit = hit.astype(bf16)
    charge = jnp.concatenate(
        [
            jnp.concatenate(
                [got_ref[q * rows + c * cap : q * rows + (c + 1) * cap, :] for q in range(pencils)], axis=0
            ).T
            for c in range(channels)
        ],
        axis=0,
    )
    placed_ref[...] = dot(jnp.concatenate(halves(charge), axis=1), jnp.concatenate([hit, hit], axis=0))
    for group in GROUPS:
        blocks, grid = tiles_of(*group)
        for p in range(2):
            found = swap_bits([tile(placed_ref, r, c + p * 2 * LANES) for r, c in blocks], (32, 16, 8))
            for (r, c), moved in zip(grid, found):
                z_ref[p, r : r + 8, c : c + LANES] = moved
    for p in range(2):
        spec = table_dot((table_ref[p, 0], table_ref[p, 1]), z_ref[p])
        for row in range(8):
            part, x = row // 4, row % 4
            msg_ref[pl.ds(p * 10 + row, half, 20), :] = spec[
                part * half : (part + 1) * half, x * LANES : (x + 1) * LANES
            ]


def plane_kernel(got_ref, xf_ref, yf_ref, yi_ref, xi_ref, msg_ref):
    n = got_ref.shape[0] // 10
    half = n // 2
    got = got_ref.reshape(32, 8, 10, LANES)
    green = []
    for r in range(2):
        parts = [got[:, j, 8 + r, :] for j in range(8)]
        found = jnp.concatenate(swap_bits(parts, (64, 32, 16)), axis=0)
        green.append(jnp.concatenate([found, found], axis=1))
    tiles = [got[:, j, :8, :].reshape(n, LANES) for j in range(8)]
    by_x = [[t[:half] + t[half:] for t in tiles], [t[:half] - t[half:] for t in tiles]]
    spec = []
    for p in range(2):
        low, high = by_x[p][:4], by_x[p][4:]
        found = [
            swap_bits([u + v for u, v in zip(low, high)], (64, 32)),
            swap_bits([u - v for u, v in zip(low, high)], (64, 32)),
        ]
        rows = [
            jnp.concatenate([found[q][x_2 * 2 + w] for w in range(2) for q in range(2)], axis=1) for x_2 in range(2)
        ]
        spec.append(table_dot(halves(xf_ref[p]), jnp.concatenate(rows, axis=0)))
    sums = []
    for q in range(2):
        rows = [
            jnp.concatenate(
                [spec[p][part * half : (part + 1) * half, (w * 2 + q) * LANES : (w * 2 + q + 1) * LANES] for part in range(2)],
                axis=1,
            )
            for w in range(2)
            for p in range(2)
        ]
        result = dot_table(jnp.concatenate(rows, axis=0), halves(yf_ref[q]))
        result = result * jnp.concatenate([green[q], green[q]], axis=0)
        sums.append(dot_table(result, halves(yi_ref[q])))
    plane = []
    for p in range(2):
        rows = [
            jnp.concatenate(
                [
                    sums[q][(w * 2 + p) * half : (w * 2 + p + 1) * half, part * half : (part + 1) * half]
                    for w in range(2)
                    for q in range(2)
                ],
                axis=1,
            )
            for part in range(2)
        ]
        plane.append(table_dot(halves(xi_ref[p]), jnp.concatenate(rows, axis=0)))
    msg = msg_ref.reshape(32, 8, 8, LANES)
    for upper in range(2):
        moved = []
        for q in range(2):
            parts = []
            for x_2 in range(2):
                for w in range(2):
                    even, odd = [
                        o[x_2 * half : (x_2 + 1) * half, (w * 2 + q) * LANES : (w * 2 + q + 1) * LANES] for o in plane
                    ]
                    parts.append(even - odd if upper else even + odd)
            moved.append(swap_bits(parts, (64, 32)))
        for j in range(4):
            for j_2 in range(2):
                part = moved[0][j] - moved[1][j] if j_2 else moved[0][j] + moved[1][j]
                msg[upper * 16 : (upper + 1) * 16, j_2 * 4 + j, :, :] = part.reshape(16, 8, LANES)


def inverse_kernel(got_ref, hit_ref, table_ref, msg_ref, z_ref, a_ref):
    n = got_ref.shape[0] // 8
    pencils = msg_ref.shape[0]
    cells = hit_ref.shape[1]
    cap = cells // pencils
    half = n // 2
    for p in range(2):
        rows = [
            jnp.concatenate([got_ref[pl.ds(p * 8 + part * 4 + x, half, 16), :] for x in range(4)], axis=1)
            for part in range(2)
        ]
        z_ref[p] = table_dot(halves(table_ref[p]), jnp.concatenate(rows, axis=0))
    for group in GROUPS:
        blocks, grid = tiles_of(*group)
        for p in range(2):
            found = swap_bits([tile(z_ref.at[p], r, c) for r, c in grid], (32, 16, 8))
            for (r, c), moved in zip(blocks, found):
                a_ref[r : r + 8, c + p * 2 * LANES : c + (p * 2 + 1) * LANES] = moved
    picked = dot(jnp.concatenate(halves(a_ref[...]), axis=0), hit_ref[...])
    rows = 4 * LANES
    for c in range(4):
        cells_c = picked[c * LANES : (c + 1) * LANES] + picked[rows + c * LANES : rows + (c + 1) * LANES]
        msg_ref[:, c * cap : (c + 1) * cap, :] = cells_c.T.reshape(pencils, cap, LANES)


def near_kernel(
    src_ref, table_ref, index_ref, coef_ref, w_ref, slot_ref, green_ref, order_ref, z_ref, near_ref, wt_ref, hit_ref, out_ref, split_ref
):
    channels = src_ref.shape[0]
    near, tris = index_ref.shape
    for start in range(0, tris, LANES):
        cols = slice(start, start + LANES)
        total = [jnp.zeros((8, LANES), f32) for _ in range(channels)]
        for top in range(0, near, 8):
            index = index_ref[top : top + 8, cols]
            lane, row = index & (LANES - 1), index >> 7
            got = [jnp.zeros((8, LANES), f32) for _ in range(channels)]
            for r in range(8):
                hit = row == r
                for c in range(channels):
                    line = jnp.broadcast_to(table_ref[c, r : r + 1, :], (8, LANES))
                    got[c] = jnp.where(hit, jnp.take_along_axis(line, lane, axis=1), got[c])
            a = coef_ref[0, top : top + 8, cols]
            b = coef_ref[1, top : top + 8, cols]
            for w in range(channels // 2):
                re, im = got[w], got[w + channels // 2]
                total[w] += a * re - b * im
                total[w + channels // 2] += a * im + b * re
        for c in range(channels):
            near_ref[c : c + 1, cols] = jnp.sum(total[c], axis=0, keepdims=True)
    wt_ref[...] = w_ref[...].T
    hit = lax.broadcasted_iota(jnp.int32, hit_ref.shape, 0) == slot_ref[...]
    hit_ref[...] = jnp.where(hit, 1.0, 0.0).astype(bf16)
    order = order_ref[...].astype(bf16)
    high, low = halves(green_ref[...])
    out_ref[...] = (dot(order, high) + dot(order, low)).T
    for p in range(2):
        split_ref[p, 0], split_ref[p, 1] = halves(z_ref[p])


def far_kernel(got_ref, hit_ref, wt_ref, near_ref, out_ref):
    pencils, rows, _ = got_ref.shape
    channels, tris = near_ref.shape
    cap = rows // channels
    slots = pencils * cap
    hit = hit_ref[...]
    values = jnp.concatenate(
        [got_ref[:, c * cap : (c + 1) * cap, :].reshape(slots, LANES).T for c in range(channels)], axis=0
    )
    picked = dot(jnp.concatenate(halves(values), axis=1), jnp.concatenate([hit, hit], axis=0))
    wt = wt_ref[...]
    for c in range(channels):
        far = jnp.sum(picked[c * LANES : (c + 1) * LANES] * wt, axis=0, keepdims=True)
        out_ref[c : c + 1, :] = far + near_ref[c : c + 1, :]


def exchange(x, axis):
    parts = lax.axis_size(axis)
    sent = x.reshape(parts, 1, x.size // parts)
    return lax.all_to_all(sent, axis, split_axis=0, concat_axis=0, tiled=True).reshape(x.shape)


def per_device(sources, proj_weight, tri_slot, cell_block, green, near_index, near_coef):
    slabs, pencils = lax.axis_size("slab"), lax.axis_size("pencil")
    channels, tris = sources.shape
    slots = cell_block.shape[0]
    cap = slots // pencils
    n = green.shape[2]
    devices = slabs * pencils
    zf, xf, yf, yi, xi, zi = tables(n)
    slot_row = tri_slot.reshape(1, tris)
    block_row = cell_block.reshape(1, slots)

    msg = call(
        charges_kernel,
        struct((pencils * (channels * cap + 1), LANES), f32),
        scratch=[
            pltpu.VMEM((channels, tris), f32),
            pltpu.VMEM((tris, LANES), f32),
            pltpu.VMEM((1, tris), jnp.int32),
            pltpu.VMEM((1, slots), jnp.int32),
            pltpu.SemaphoreType.DMA((4,)),
        ],
        in_specs=[pl.BlockSpec(memory_space=pltpu.HBM)] * 4,
        mib=60,
    )(sources, proj_weight, slot_row, block_row)
    near, wt, tri_hit, green_rows, zf = call(
        near_kernel,
        (
            struct((channels, tris), f32),
            struct((LANES, tris), f32),
            struct((slots, tris), bf16),
            struct((n, n), f32),
            struct((2, 2, n, n), bf16),
        ),
        cost=(1 << 30, 1 << 20),
    )(sources, sources.reshape(channels, 8, LANES), near_index, near_coef, proj_weight, slot_row, green.reshape(n, n), green_order(n), zf)
    got = exchange(msg, "pencil")
    got, near, wt, tri_hit, green_rows, zf = lax.optimization_barrier((got, near, wt, tri_hit, green_rows, zf))
    msg, hit = call(
        forward_kernel,
        (struct((devices * 10, LANES), f32), struct((512, slots), bf16)),
        scratch=[pltpu.VMEM((channels * LANES, 512), f32), pltpu.VMEM((2, n, 512), f32)],
    )(got, green_rows, zf)
    got = exchange(msg, BOTH)
    msg = call(plane_kernel, struct((devices * 8, LANES), f32))(got, xf, yf, yi, xi)
    got = exchange(msg, BOTH)
    msg = call(
        inverse_kernel,
        struct((pencils, channels * cap, LANES), f32),
        scratch=[pltpu.VMEM((2, n, 512), f32), pltpu.VMEM((channels * LANES, 512), f32)],
    )(got, hit, zi)
    got = exchange(msg, "pencil")
    return call(far_kernel, struct((channels, tris), f32))(got, tri_hit, wt, near)


def solution(mesh):
    return jax.shard_map(
        per_device,
        mesh=mesh,
        in_specs=(
            P(None, BOTH),
            P(BOTH, None),
            P(BOTH),
            P(BOTH),
            P("slab", "pencil", None),
            P(None, BOTH),
            P(None, None, BOTH),
        ),
        out_specs=P(None, BOTH),
        check_vma=False,
    )
```

```python
import math

import jax
import jax.numpy as jnp
import numpy as np
from jax import lax
from jax.experimental import pallas as pl
from jax.experimental.pallas import tpu as pltpu
from jax.sharding import PartitionSpec as P

f32 = jnp.float32
bf16 = jnp.bfloat16
BOTH = ("slab", "pencil")
LANES = 128
struct = jax.ShapeDtypeStruct


def call(body, out_shape, scratch=(), mib=24, cost=(0, 0), in_specs=None):
    more = {} if in_specs is None else {"in_specs": in_specs}
    return pl.pallas_call(
        body,
        out_shape=out_shape,
        scratch_shapes=list(scratch),
        compiler_params=pltpu.CompilerParams(vmem_limit_bytes=mib << 20),
        cost_estimate=pl.CostEstimate(flops=cost[0], bytes_accessed=cost[1], transcendentals=0),
        **more,
    )


def halves(x):
    high = x.astype(bf16)
    return high, (x - high.astype(f32)).astype(bf16)


def dot(a, b, dims=((1,), (0,))):
    return lax.dot_general(a, b, (dims, ((), ())), preferred_element_type=f32)


def table_dot(table, x):
    t_high, t_low = table
    high, low = halves(x)
    m = t_high.shape[0]
    both = dot(jnp.concatenate([t_high, t_low], axis=0), high)
    return both[:m] + (both[m:] + dot(t_high, low))


def dot_table(x, table):
    m = x.shape[0]
    high, low = halves(x)
    both = dot(jnp.concatenate([high, low], axis=0), table[0])
    return both[:m] + (both[m:] + dot(high, table[1]))


def complex_table(rows, row_part, columns, column_part, n, inverse):
    angle = (np.outer(rows, columns) % n) * (2.0 * math.pi / n)
    sine = np.sin(angle) * np.where(row_part == 0, 1.0, -1.0)[:, None]
    if inverse:
        sine = -sine
    same = row_part[:, None] == column_part[None, :]
    return np.where(same, np.cos(angle), sine) / (n if inverse else 1)


def tables(n):
    half = n // 2
    part, z = np.arange(n) // half, np.arange(n) % half
    kz = [2 * z + p for p in range(2)]
    b2, slab, x_part, b1, b0 = (a.reshape(-1) for a in np.indices((2, 16, 2, 2, 2)))
    x = slab * 8 + b2 * 4 + b1 * 2 + b0
    kx_part, kx_high, kx_slab = (a.reshape(-1) for a in np.indices((2, 4, 32)))
    kx = [kx_slab * 8 + kx_high * 2 + p for p in range(2)]
    y = z // 32 * 32 + z % 8 * 4 + z // 8 % 4
    ky = [z // 16 * 32 + z % 16 * 2 + p for p in range(2)]

    def both(make):
        return jnp.asarray(np.stack([make(p) for p in range(2)]).astype(np.float32))

    return (
        both(lambda p: complex_table(kz[p], part, z, part, n, False)),
        both(lambda p: complex_table(kx[p], kx_part, x, x_part, n, False)),
        both(lambda p: complex_table(ky[p], part, y, part, n, False).T),
        both(lambda p: complex_table(y, part, ky[p], part, n, True).T),
        both(lambda p: complex_table(x, x_part, kx[p], kx_part, n, True)),
        both(lambda p: complex_table(z, part, kz[p], part, n, True)),
    )


def green_order(n):
    place = np.arange(n)
    kx = place // 64 % 2 + place // 16 % 4 * 2
    ky = place % 16 * 2 + place // 128
    return jnp.asarray((kx[:, None] * 32 + ky[:, None] == place[None, :]).astype(np.float32))


def lane_iota(rows):
    return lax.broadcasted_iota(jnp.int32, (rows, LANES), 1)


def swap_bits(parts, distances):
    parts = list(parts)
    lane = lane_iota(parts[0].shape[0])
    for level, distance in enumerate(distances):
        stride = len(parts) >> (level + 1)
        bit = (lane & distance) != 0
        for low in range(len(parts)):
            if low & stride == 0:
                a, b = parts[low], parts[low | stride]
                moved = jnp.where(bit, a, b)
                if distance == LANES // 2:
                    moved = pltpu.roll(moved, distance, 1)
                else:
                    moved = jnp.take_along_axis(moved, lane ^ distance, axis=1)
                parts[low], parts[low | stride] = jnp.where(bit, moved, a), jnp.where(bit, b, moved)
    return parts


def block_column(block, x_blocks, y_blocks, z_blocks):
    z = block % z_blocks
    y = block // z_blocks % 64 % y_blocks
    x = block // (z_blocks * 64) % x_blocks
    return z // 8 * LANES + x * 64 + z % 8 * 8 + y


def charges_kernel(src_hbm, w_hbm, slot_hbm, block_hbm, msg_ref, src_ref, w_ref, slot_ref, block_ref, sems):
    channels, tris = src_ref.shape
    pairs = [(src_hbm, src_ref), (slot_hbm, slot_ref), (block_hbm, block_ref), (w_hbm, w_ref)]
    copies = [pltpu.make_async_copy(a, b, sems.at[i]) for i, (a, b) in enumerate(pairs)]
    for copy in copies:
        copy.start()
    for copy in copies[:3]:
        copy.wait()
    slots = block_ref.shape[1]
    pencils = msg_ref.shape[0] - channels * slots
    cap = slots // pencils
    rows = channels * cap + 1
    place = block_column(block_ref[...], 2, 8, 32).astype(f32)
    for q in range(pencils):
        row = place if q == 0 else pltpu.roll(place, slots - q * cap, 1)
        msg_ref[q * rows + rows - 1 : (q + 1) * rows, :] = row
    hit = lax.broadcasted_iota(jnp.int32, (slots, tris), 0) == slot_ref[...]
    hit = jnp.where(hit, 1.0, 0.0).astype(bf16)
    left = [jnp.concatenate([hit * half[c : c + 1, :] for c in range(channels)], axis=0) for half in halves(src_ref[...])]
    for copy in copies[3:]:
        copy.wait()
    w_high, w_low = halves(w_ref[...])
    both = dot(left[0], jnp.concatenate([w_high, w_low], axis=1))
    total = both[:, :LANES] + (both[:, LANES:] + dot(left[1], w_high))
    for c in range(channels):
        for q in range(pencils):
            msg_ref[q * rows + c * cap : q * rows + (c + 1) * cap, :] = total[
                c * slots + q * cap : c * slots + (q + 1) * cap
            ]


def tiles_of(part, g, x_1, x_0):
    blocks, grid = [], []
    for m in range(8):
        wave, y_low = m // 4, m % 4
        stencil = (x_1 * 2 + x_0) * 4 + y_low
        blocks.append(((part * 2 + wave) * LANES + stencil * 8, g * LANES))
        grid.append((part * 128 + (g * 8 + m) * 8, (x_1 * 2 + x_0) * LANES))
    return blocks, grid


GROUPS = [(part, g, x_1, x_0) for part in range(2) for g in range(2) for x_1 in range(2) for x_0 in range(2)]


def tile(ref, row, column):
    return ref[row : row + 8, column : column + LANES]


def forward_kernel(got_ref, green_ref, table_ref, msg_ref, hit_ref, placed_ref, z_ref):
    cells = hit_ref.shape[1]
    channels = 4
    pencils = got_ref.shape[0] - channels * cells
    cap = cells // pencils
    rows = channels * cap + 1
    place = jnp.concatenate(
        [jnp.broadcast_to(got_ref[(q + 1) * rows - 1 : (q + 1) * rows, :], (cap, LANES)) for q in range(pencils)], axis=0
    )
    own = lane_iota(cells) == lax.broadcasted_iota(jnp.int32, (cells, LANES), 0) % cap
    place = jnp.sum(jnp.where(own, place, 0.0), axis=1, keepdims=True)
    place = jnp.broadcast_to(place, (cells, LANES))
    upper = place >= 2 * LANES
    at = jnp.where(upper, place - 2 * LANES, place)
    lane = lane_iota(cells).astype(f32)
    marks = [jnp.where(lane + g * LANES == at, 1.0, 0.0) for g in range(2)]
    hit = jnp.concatenate(marks + [jnp.where(upper, -mark, mark) for mark in marks], axis=1)
    hit_ref[...] = hit.T.astype(bf16)
    hit = hit.astype(bf16)
    charge = jnp.concatenate(
        [
            jnp.concatenate(
                [got_ref[q * rows + c * cap : q * rows + (c + 1) * cap, :] for q in range(pencils)], axis=0
            ).T
            for c in range(channels)
        ],
        axis=0,
    )
    placed_ref[...] = dot(jnp.concatenate(halves(charge), axis=1), jnp.concatenate([hit, hit], axis=0))
    for group in GROUPS:
        blocks, grid = tiles_of(*group)
        for p in range(2):
            found = swap_bits([tile(placed_ref, r, c + p * 2 * LANES) for r, c in blocks], (32, 16, 8))
            for (r, c), moved in zip(grid, found):
                z_ref[p, r : r + 8, c : c + LANES] = moved
    half = msg_ref.shape[0] // 20
    for p in range(2):
        spec = table_dot((table_ref[p, 0], table_ref[p, 1]), z_ref[p])
        for row in range(8):
            part, x = row // 4, row % 4
            msg_ref[pl.ds(p * 10 + row, half, 20), :] = spec[
                part * half : (part + 1) * half, x * LANES : (x + 1) * LANES
            ]
    for row in range(2):
        msg_ref[pl.ds(8 + row, 2 * half, 10), :] = green_ref[:, row * LANES : (row + 1) * LANES]


def plane_kernel(got_ref, xf_ref, yf_ref, yi_ref, xi_ref, msg_ref):
    n = got_ref.shape[0] // 10
    half = n // 2
    got = got_ref.reshape(32, 8, 10, LANES)
    green = []
    for r in range(2):
        parts = [got[:, j, 8 + r, :] for j in range(8)]
        found = jnp.concatenate(swap_bits(parts, (64, 32, 16)), axis=0)
        green.append(jnp.concatenate([found, found], axis=1))
    tiles = [got[:, j, :8, :].reshape(n, LANES) for j in range(8)]
    by_x = [[t[:half] + t[half:] for t in tiles], [t[:half] - t[half:] for t in tiles]]
    spec = []
    for p in range(2):
        low, high = by_x[p][:4], by_x[p][4:]
        found = [
            swap_bits([u + v for u, v in zip(low, high)], (64, 32)),
            swap_bits([u - v for u, v in zip(low, high)], (64, 32)),
        ]
        rows = [
            jnp.concatenate([found[q][x_2 * 2 + w] for w in range(2) for q in range(2)], axis=1) for x_2 in range(2)
        ]
        spec.append(table_dot(halves(xf_ref[p]), jnp.concatenate(rows, axis=0)))
    sums = []
    for q in range(2):
        rows = [
            jnp.concatenate(
                [spec[p][part * half : (part + 1) * half, (w * 2 + q) * LANES : (w * 2 + q + 1) * LANES] for part in range(2)],
                axis=1,
            )
            for w in range(2)
            for p in range(2)
        ]
        result = dot_table(jnp.concatenate(rows, axis=0), halves(yf_ref[q]))
        result = result * jnp.concatenate([green[q], green[q]], axis=0)
        sums.append(dot_table(result, halves(yi_ref[q])))
    plane = []
    for p in range(2):
        rows = [
            jnp.concatenate(
                [
                    sums[q][(w * 2 + p) * half : (w * 2 + p + 1) * half, part * half : (part + 1) * half]
                    for w in range(2)
                    for q in range(2)
                ],
                axis=1,
            )
            for part in range(2)
        ]
        plane.append(table_dot(halves(xi_ref[p]), jnp.concatenate(rows, axis=0)))
    msg = msg_ref.reshape(32, 8, 8, LANES)
    for upper in range(2):
        moved = []
        for q in range(2):
            parts = []
            for x_2 in range(2):
                for w in range(2):
                    even, odd = [
                        o[x_2 * half : (x_2 + 1) * half, (w * 2 + q) * LANES : (w * 2 + q + 1) * LANES] for o in plane
                    ]
                    parts.append(even - odd if upper else even + odd)
            moved.append(swap_bits(parts, (64, 32)))
        for j in range(4):
            for j_2 in range(2):
                part = moved[0][j] - moved[1][j] if j_2 else moved[0][j] + moved[1][j]
                msg[upper * 16 : (upper + 1) * 16, j_2 * 4 + j, :, :] = part.reshape(16, 8, LANES)


def inverse_kernel(got_ref, hit_ref, table_ref, msg_ref, z_ref, a_ref):
    n = got_ref.shape[0] // 8
    pencils = msg_ref.shape[0]
    cells = hit_ref.shape[1]
    cap = cells // pencils
    half = n // 2
    rows = 4 * LANES
    picked = None
    for p in range(2):
        spec = [
            jnp.concatenate([got_ref[pl.ds(p * 8 + part * 4 + x, half, 16), :] for x in range(4)], axis=1)
            for part in range(2)
        ]
        z_ref[p] = table_dot(halves(table_ref[p]), jnp.concatenate(spec, axis=0))
    for p in range(2):
        for group in GROUPS:
            blocks, grid = tiles_of(*group)
            found = swap_bits([tile(z_ref.at[p], r, c) for r, c in grid], (32, 16, 8))
            for (r, c), moved in zip(blocks, found):
                a_ref[p, r : r + 8, c : c + LANES] = moved
        both = dot(jnp.concatenate(halves(a_ref[p]), axis=0), hit_ref[p * 2 * LANES : (p + 1) * 2 * LANES, :])
        both = both[:rows] + both[rows:]
        picked = both if picked is None else picked + both
    for c in range(4):
        msg_ref[:, c * cap : (c + 1) * cap, :] = picked[c * LANES : (c + 1) * LANES].T.reshape(pencils, cap, LANES)


def near_kernel(
    src_ref, table_ref, index_ref, coef_ref, w_ref, slot_ref, green_ref, order_ref, z_ref, near_ref, wt_ref, hit_ref, out_ref, split_ref
):
    channels = src_ref.shape[0]
    near, tris = index_ref.shape
    for start in range(0, tris, LANES):
        cols = slice(start, start + LANES)
        total = [jnp.zeros((8, LANES), f32) for _ in range(channels)]
        for top in range(0, near, 8):
            index = index_ref[top : top + 8, cols]
            lane, row = index & (LANES - 1), index >> 7
            got = [jnp.zeros((8, LANES), f32) for _ in range(channels)]
            for r in range(8):
                hit = row == r
                for c in range(channels):
                    line = jnp.broadcast_to(table_ref[c, r : r + 1, :], (8, LANES))
                    got[c] = jnp.where(hit, jnp.take_along_axis(line, lane, axis=1), got[c])
            a = coef_ref[0, top : top + 8, cols]
            b = coef_ref[1, top : top + 8, cols]
            for w in range(channels // 2):
                re, im = got[w], got[w + channels // 2]
                total[w] += a * re - b * im
                total[w + channels // 2] += a * im + b * re
        for c in range(channels):
            near_ref[c : c + 1, cols] = jnp.sum(total[c], axis=0, keepdims=True)
    wt_ref[...] = w_ref[...].T
    hit = lax.broadcasted_iota(jnp.int32, hit_ref.shape, 0) == slot_ref[...]
    hit_ref[...] = jnp.where(hit, 1.0, 0.0).astype(bf16)
    order = order_ref[...].astype(bf16)
    high, low = halves(green_ref[...])
    out_ref[...] = (dot(order, high) + dot(order, low)).T
    for p in range(2):
        split_ref[p, 0], split_ref[p, 1] = halves(z_ref[p])


def far_kernel(got_ref, hit_ref, wt_ref, near_ref, out_ref):
    pencils, rows, _ = got_ref.shape
    channels, tris = near_ref.shape
    cap = rows // channels
    slots = pencils * cap
    hit = hit_ref[...]
    values = jnp.concatenate(
        [got_ref[:, c * cap : (c + 1) * cap, :].reshape(slots, LANES).T for c in range(channels)], axis=0
    )
    picked = dot(jnp.concatenate(halves(values), axis=1), jnp.concatenate([hit, hit], axis=0))
    wt = wt_ref[...]
    for c in range(channels):
        far = jnp.sum(picked[c * LANES : (c + 1) * LANES] * wt, axis=0, keepdims=True)
        out_ref[c : c + 1, :] = far + near_ref[c : c + 1, :]


def exchange(x, axis):
    parts = lax.axis_size(axis)
    sent = x.reshape(parts, 1, x.size // parts)
    return lax.all_to_all(sent, axis, split_axis=0, concat_axis=0, tiled=True).reshape(x.shape)


def per_device(sources, proj_weight, tri_slot, cell_block, green, near_index, near_coef):
    slabs, pencils = lax.axis_size("slab"), lax.axis_size("pencil")
    channels, tris = sources.shape
    slots = cell_block.shape[0]
    cap = slots // pencils
    n = green.shape[2]
    devices = slabs * pencils
    zf, xf, yf, yi, xi, zi = tables(n)
    slot_row = tri_slot.reshape(1, tris)
    block_row = cell_block.reshape(1, slots)

    msg = call(
        charges_kernel,
        struct((pencils * (channels * cap + 1), LANES), f32),
        scratch=[
            pltpu.VMEM((channels, tris), f32),
            pltpu.VMEM((tris, LANES), f32),
            pltpu.VMEM((1, tris), jnp.int32),
            pltpu.VMEM((1, slots), jnp.int32),
            pltpu.SemaphoreType.DMA((4,)),
        ],
        in_specs=[pl.BlockSpec(memory_space=pltpu.HBM)] * 4,
        mib=60,
    )(sources, proj_weight, slot_row, block_row)
    near, wt, tri_hit, green_rows, zf = call(
        near_kernel,
        (
            struct((channels, tris), f32),
            struct((LANES, tris), f32),
            struct((slots, tris), bf16),
            struct((n, n), f32),
            struct((2, 2, n, n), bf16),
        ),
        cost=(1 << 30, 1 << 20),
    )(sources, sources.reshape(channels, 8, LANES), near_index, near_coef, proj_weight, slot_row, green.reshape(n, n), green_order(n), zf)
    got = exchange(msg, "pencil")
    got, near, wt, tri_hit, green_rows, zf = lax.optimization_barrier((got, near, wt, tri_hit, green_rows, zf))
    msg, hit = call(
        forward_kernel,
        (struct((devices * 10, LANES), f32), struct((512, slots), bf16)),
        scratch=[pltpu.VMEM((channels * LANES, 512), f32), pltpu.VMEM((2, n, 512), f32)],
    )(got, green_rows, zf)
    got = exchange(msg, BOTH)
    msg = call(plane_kernel, struct((devices * 8, LANES), f32))(got, xf, yf, yi, xi)
    got = exchange(msg, BOTH)
    msg = call(
        inverse_kernel,
        struct((pencils, channels * cap, LANES), f32),
        scratch=[pltpu.VMEM((2, n, 512), f32), pltpu.VMEM((2, channels * LANES, 256), f32)],
    )(got, hit, zi)
    got = exchange(msg, "pencil")
    return call(far_kernel, struct((channels, tris), f32))(got, tri_hit, wt, near)


def solution(mesh):
    return jax.shard_map(
        per_device,
        mesh=mesh,
        in_specs=(
            P(None, BOTH),
            P(BOTH, None),
            P(BOTH),
            P(BOTH),
            P("slab", "pencil", None),
            P(None, BOTH),
            P(None, None, BOTH),
        ),
        out_specs=P(None, BOTH),
        check_vma=False,
    )
```
